32 devices in a mesh: rep: 2 (over y), fsdp: 16 (over z, x, core).
Axes of the slice: x: 2, y: 2, z: 4, core: 2. Of those that a mesh axis runs over, the one named last changes fastest.
Arguments:
- inputs: bfloat16 [32768, 768], P(('rep', 'fsdp')), may hold values from -6 to 6
- block_kind: int32 [64], P(('rep', 'fsdp')), may hold values from 0 to 1
- query_weight: bfloat16 [768, 768], P('fsdp'), may hold values from -0.21875 to 0.21875
- query_bias: bfloat16 [768], P('fsdp'), may hold values from -3 to 3
- key_weight: bfloat16 [768, 768], P('fsdp'), may hold values from -0.21875 to 0.21875
- value_weight: bfloat16 [768, 768], P('fsdp'), may hold values from -0.21875 to 0.21875
- value_bias: bfloat16 [768], P('fsdp'), may hold values from -0.59765625 to 0.59765625
- out_weight: bfloat16 [768, 768], P('fsdp'), may hold values from -0.875 to 0.875
- out_bias: bfloat16 [768], P('fsdp'), may hold values from -3 to 3
- attn_gain: bfloat16 [768], P('fsdp'), may hold values from 0.5 to 1.5
- attn_shift: bfloat16 [768], P('fsdp'), may hold values from -3 to 3
- up_weight: bfloat16 [768, 3072], P('fsdp'), may hold values from -0.21875 to 0.21875
- up_bias: bfloat16 [3072], P('fsdp'), may hold values from -3 to 3
- down_weight: bfloat16 [3072, 768], P('fsdp'), may hold values from -0.15625 to 0.15625
- down_bias: bfloat16 [768], P('fsdp'), may hold values from -3 to 3
- ffn_gain: bfloat16 [768], P('fsdp'), may hold values from 0.5 to 1.5
- ffn_shift: bfloat16 [768], P('fsdp'), may hold values from -3 to 3
- cotangent: bfloat16 [32768, 768], P(('rep', 'fsdp')), may hold values from -6 to 6
Outputs:
- layer_out: bfloat16 [32768, 768], P(('rep', 'fsdp'))
- input_grad: float32 [32768, 768], P(('rep', 'fsdp'))
- query_weight_grad: float32 [768, 768], P('fsdp')
- query_bias_grad: float32 [768], P('fsdp')
- key_weight_grad: float32 [768, 768], P('fsdp')
- value_weight_grad: float32 [768, 768], P('fsdp')
- value_bias_grad: float32 [768], P('fsdp')
- out_weight_grad: float32 [768, 768], P('fsdp')
- out_bias_grad: float32 [768], P('fsdp')
- attn_gain_grad: float32 [768], P('fsdp')
- attn_shift_grad: float32 [768], P('fsdp')
- up_weight_grad: float32 [768, 3072], P('fsdp')
- up_bias_grad: float32 [3072], P('fsdp')
- down_weight_grad: float32 [3072, 768], P('fsdp')
- down_bias_grad: float32 [768], P('fsdp')
- ffn_gain_grad: float32 [768], P('fsdp')
- ffn_shift_grad: float32 [768], P('fsdp')
The draws below stay inside these ranges and needn't reach their ends.
Inputs may be any that keep to these rules, and one draw needn't show every extreme that they name: `block_kind`: 1 marks a block that holds one sequence of 512 tokens; 0 marks a block that holds 4 sequences of 128 tokens each.
All inputs are finite; a program needn't handle non-finite values.
Results may differ from the reference program's by a relative error of at most 0.017.
Values may be sent and summed in bfloat16 or wider, within the bound.
No kernel may reach another device: no remote copies, remote signals or barrier semaphores. Data moves between devices by JAX's collectives and lax.ppermute only.
A program may use at most 192 MiB of HBM per device.

```python
import jax
import jax.numpy as jnp
from jax import lax

D = 768
H = 12
HD = 64
FF = 3072
LONG = 512
SHORT = 128
TOKENS = 32768
BLOCKS = 64


def plant(values, rng, low, high):
    spot = [jax.random.randint(jax.random.fold_in(rng, axis), (), 0, length) for axis, length in enumerate(values.shape)]
    longest = values.shape.index(max(values.shape))
    beside = spot[:longest] + [(spot[longest] + 1) % values.shape[longest]] + spot[longest + 1:]
    return values.at[tuple(spot)].set(low).at[tuple(beside)].set(high)


def strengthened(values, own_key, source, target, shards_of, factor):
    def block_of(axis_at):
        return (jnp.arange(values.shape[axis_at]) // (values.shape[axis_at] // shards_of)).reshape((-1,) + (1,) * (values.ndim - 1 - axis_at))

    near = jax.random.permutation(own_key, shards_of)[block_of(target)]
    second = (block_of(target) + shards_of // 2) % shards_of
    return jnp.where((block_of(source) == near) | (block_of(source) == second), factor * values, values)


def levels(own_key, dims, split, least, high):
    level, own = 1.0, jax.random.fold_in(own_key, 6)
    for dim, blocks in split:
        draws = jnp.exp(jax.random.uniform(jax.random.fold_in(own, dim), (blocks,), jnp.float32, least / len(split), high / len(split)))
        level = level * jnp.repeat(draws, dims[dim] // blocks).reshape([-1 if axis == dim else 1 for axis in range(len(dims))])
    return level


def gaussian(key, extent, spread, most, shards=(), held_as=jnp.bfloat16):
    gain = levels(key, extent, shards, -0.22, 0.18) if shards else 1.0
    result = jax.random.normal(key, extent, jnp.float32) * spread * gain
    return jnp.minimum(jnp.maximum(result, -most), most).astype(held_as)


def heavy_noise(stream_key, extent, scale, most, cuts, heavy, dtype=jnp.bfloat16):
    values = scale * jax.random.normal(stream_key, extent, jnp.float32)
    if cuts:
        values = values * levels(stream_key, extent, cuts, -0.22, 0.18)
    return jnp.clip(strengthened(values, jax.random.fold_in(stream_key, 3), *heavy), -most, most).astype(dtype)


def setup_inputs(seed: int = 0) -> dict:
    seeds = jax.random.split(jax.random.key(seed), 19)
    inputs = gaussian(seeds[0], (TOKENS, D), 1.0, 6.0, ((0, 32),))
    block_kind = plant(jax.random.randint(seeds[1], (BLOCKS,), 0, 2), jax.random.fold_in(seeds[1], 1), 0, 1).astype(jnp.int32)
    query_weight = gaussian(seeds[2], (D, D), D ** -0.5, 0.21875, ((0, 16),))
    query_bias = gaussian(seeds[3], (D,), 0.5, 3.0, ((0, 16),))
    key_weight = gaussian(seeds[4], (D, D), D ** -0.5, 0.21875, ((0, 16),))
    value_weight = gaussian(seeds[5], (D, D), D ** -0.5, 0.21875, ((0, 16),))
    value_bias = gaussian(seeds[6], (D,), 0.1, 0.59765625, ((0, 16),))
    out_weight = gaussian(seeds[7], (D, D), (D // 16) ** -0.5, 0.875, ((0, 16),))
    out_bias = gaussian(seeds[8], (D,), 0.5, 3.0, ((0, 16),))
    attn_gain = jnp.clip(1.0 + 0.1 * jax.random.normal(seeds[9], (D,), jnp.float32), 0.5, 1.5).astype(jnp.bfloat16)
    attn_shift = gaussian(seeds[10], (D,), 0.5, 3.0, ((0, 16),))
    up_weight = gaussian(seeds[11], (D, FF), D ** -0.5, 0.21875, ((0, 16),))
    up_bias = gaussian(seeds[12], (FF,), 0.5, 3.0, ((0, 16),))
    down_weight = gaussian(seeds[13], (FF, D), (FF // 2) ** -0.5, 0.15625, ((0, 16),))
    down_bias = gaussian(seeds[14], (D,), 0.5, 3.0, ((0, 16),))
    ffn_gain = jnp.clip(1.0 + 0.1 * jax.random.normal(seeds[15], (D,), jnp.float32), 0.5, 1.5).astype(jnp.bfloat16)
    ffn_shift = gaussian(seeds[16], (D,), 0.5, 3.0, ((0, 16),))
    cotangent = heavy_noise(seeds[17], (TOKENS, D), 1.0, 6.0, ((0, 32),), (0, 1, 32, 2.75))
    return {"inputs": inputs, "block_kind": block_kind, "query_weight": query_weight, "query_bias": query_bias, "key_weight": key_weight, "value_weight": value_weight, "value_bias": value_bias, "out_weight": out_weight, "out_bias": out_bias, "attn_gain": attn_gain, "attn_shift": attn_shift, "up_weight": up_weight, "up_bias": up_bias, "down_weight": down_weight, "down_bias": down_bias, "ffn_gain": ffn_gain, "ffn_shift": ffn_shift, "cotangent": cotangent}


EPSILON = 1e-05
BLOCKED = -1e+30

@jax.custom_vjp
def low(v):
    return lax.optimization_barrier(v.astype(jnp.bfloat16)).astype(jnp.float32)

@jax.custom_vjp
def low_back(v):
    return v

def low_keep(v):
    return (low(v), None)

def low_pass(kept, grad):
    return (grad,)

def back_keep(v):
    return (v, None)

def back_low(kept, grad):
    return (low(grad),)
low.defvjp(low_keep, low_pass)
low_back.defvjp(back_keep, back_low)

def matmul(left, right):
    return jnp.dot(left, right, precision=lax.Precision.HIGHEST, preferred_element_type=jnp.float32)

def normalize(value):
    centered = value - lax.optimization_barrier(jnp.mean(value, axis=-1, keepdims=True))
    return centered * lax.rsqrt(lax.optimization_barrier(jnp.mean(centered * centered, axis=-1, keepdims=True)) + EPSILON)

def allowed_pairs(kind):
    place = lax.broadcasted_iota(jnp.int32, (LONG,), 0)
    segment = jnp.where(kind == 1, jnp.zeros_like(place), place // SHORT)
    return segment[:, None] == segment[None, :]

def attend(pieces):
    query, keys, values, kind = pieces
    raw = low_back(jnp.einsum('qhd,khd->hqk', query, keys, precision=lax.Precision.HIGHEST))
    scores = jnp.where(allowed_pairs(kind)[None], raw * HD ** (-0.5), BLOCKED)
    probs = jax.nn.softmax(scores, axis=-1)
    return jnp.einsum('hqk,khd->qhd', low(probs), values, precision=lax.Precision.HIGHEST)

def layer(tokens, kinds, weights):
    query_weight, query_bias, key_weight, value_weight, value_bias, out_weight, out_bias, attn_gain, attn_shift, up_weight, up_bias, down_weight, down_bias, ffn_gain, ffn_shift = weights
    count = tokens.shape[0]
    blocks = count // LONG
    query = low(low_back(matmul(tokens, query_weight) + query_bias))
    keys = low(low_back(matmul(tokens, key_weight)))
    values = low(low_back(matmul(tokens, value_weight) + value_bias))
    context = lax.map(jax.checkpoint(attend), (query.reshape(blocks, LONG, H, HD), keys.reshape(blocks, LONG, H, HD), values.reshape(blocks, LONG, H, HD), kinds))
    context = low(low_back(context.reshape(count, D)))
    branch = low_back(matmul(context, out_weight) + out_bias)
    hidden = normalize(tokens + branch) * attn_gain + attn_shift
    before = low_back(matmul(low(hidden), up_weight) + up_bias)
    outer = low_back(matmul(low(jax.nn.gelu(before, approximate=False)), down_weight) + down_bias)
    return normalize(hidden + outer) * ffn_gain + ffn_shift

def reference(inputs, block_kind, query_weight, query_bias, key_weight, value_weight, value_bias, out_weight, out_bias, attn_gain, attn_shift, up_weight, up_bias, down_weight, down_bias, ffn_gain, ffn_shift, cotangent):
    params = tuple((weight.astype(jnp.float32) for weight in (query_weight, query_bias, key_weight, value_weight, value_bias, out_weight, out_bias, attn_gain, attn_shift, up_weight, up_bias, down_weight, down_bias, ffn_gain, ffn_shift)))
    group = 8 * LONG
    count = TOKENS // group
    tokens = inputs.astype(jnp.float32).reshape(count, group, D)
    kinds = block_kind.reshape(count, 8)
    grads = cotangent.astype(jnp.float32).reshape(count, group, D)

    def one_group(totals, pieces):
        part_in, part_kind, part_grad = pieces

        def apply(values, weights):
            return layer(values, part_kind, weights)
        output, pull = jax.vjp(apply, part_in, params)
        grad_in, grad_params = pull(part_grad)
        return (tuple((total + piece for total, piece in zip(totals, grad_params))), (output, grad_in))
    zeros = tuple((jnp.zeros_like(weight) for weight in params))
    totals, (outputs, input_grads) = lax.scan(one_group, zeros, (tokens, kinds, grads))
    return (outputs.reshape(TOKENS, D).astype(jnp.bfloat16), input_grads.reshape(TOKENS, D), totals[0], totals[1], totals[2], totals[3], totals[4], totals[5], totals[6], totals[7], totals[8], totals[9], totals[10], totals[11], totals[12], totals[13], totals[14])
```

```python
import jax
import jax.numpy as jnp
from jax import lax
from jax.sharding import PartitionSpec as P

D = 768
H = 12
HD = 64
LONG = 512
SHORT = 128


EPSILON = 1e-05
BLOCKED = -1e30


def project(left, right):
    return jnp.dot(left, right, preferred_element_type=jnp.float32)


def contract_rows(left, right):
    return jnp.einsum("ta,tb->ab", left, right, preferred_element_type=jnp.float32)


def project_back(grad, weight):
    return jnp.einsum("tb,ab->ta", grad, weight, preferred_element_type=jnp.float32)


def heads_view(value):
    return value.reshape(value.shape[0] // LONG, LONG, H, HD)


def normalize(value):
    centered = value - jnp.mean(value, axis=-1, keepdims=True)
    inverse = lax.rsqrt(jnp.mean(centered * centered, axis=-1, keepdims=True) + EPSILON)
    return (centered * inverse, inverse)


def norm_back(grad, normed, inverse):
    return inverse * (
        grad
        - jnp.mean(grad, axis=-1, keepdims=True)
        - normed * jnp.mean(grad * normed, axis=-1, keepdims=True)
    )


def gelu_slope(value):
    return (
        0.5 * (1.0 + lax.erf(value * 0.7071067811865476))
        + value * jnp.exp(-0.5 * value * value) * 0.3989422804014327
    )


def allowed_pairs(kind):
    place = lax.broadcasted_iota(jnp.int32, (LONG,), 0)
    segment = jnp.where(kind == 1, jnp.zeros_like(place), place // SHORT)
    return segment[:, None] == segment[None, :]


def block_scores(query, keys, kind):
    raw = jnp.einsum("qhd,khd->hqk", query, keys, preferred_element_type=jnp.float32)
    allowed = allowed_pairs(kind)[None]
    return (jnp.where(allowed, raw * HD ** (-0.5), BLOCKED), allowed)


def attend_block(pieces):
    query, keys, values, kind = pieces
    scores, allowed = block_scores(query, keys, kind)
    peak = jnp.max(scores, axis=-1, keepdims=True)
    raised = jnp.exp(scores - peak)
    total = jnp.sum(raised, axis=-1, keepdims=True)
    probs = (raised / total).astype(jnp.bfloat16)
    context = jnp.einsum("hqk,khd->qhd", probs, values, preferred_element_type=jnp.float32)
    return (context.astype(jnp.bfloat16), peak + jnp.log(total))


def attend_back(pieces):
    query, keys, values, kind, logsum, grad_context = pieces
    scores, allowed = block_scores(query, keys, kind)
    probs = jnp.exp(scores - logsum)
    grad_probs = jnp.einsum(
        "qhd,khd->hqk", grad_context, values, preferred_element_type=jnp.float32
    )
    grad_values = jnp.einsum(
        "hqk,qhd->khd", probs.astype(jnp.bfloat16), grad_context, preferred_element_type=jnp.float32
    )
    grad_scores = probs * (grad_probs - jnp.sum(probs * grad_probs, axis=-1, keepdims=True))
    grad_raw = jnp.where(allowed, grad_scores * HD ** (-0.5), 0.0).astype(jnp.bfloat16)
    grad_query = jnp.einsum("hqk,khd->qhd", grad_raw, keys, preferred_element_type=jnp.float32)
    grad_keys = jnp.einsum("hqk,qhd->khd", grad_raw, query, preferred_element_type=jnp.float32)
    return (grad_query, grad_keys, grad_values)


def layer_forward(
    inputs,
    block_kind,
    query_weight,
    query_bias,
    key_weight,
    value_weight,
    value_bias,
    out_weight,
    out_bias,
    attn_gain,
    attn_shift,
    up_weight,
    up_bias,
    down_weight,
    down_bias,
    ffn_gain,
    ffn_shift,
):
    count = inputs.shape[0]
    query = (project(inputs, query_weight) + query_bias.astype(jnp.float32)).astype(jnp.bfloat16)
    keys = project(inputs, key_weight).astype(jnp.bfloat16)
    values = (project(inputs, value_weight) + value_bias.astype(jnp.float32)).astype(jnp.bfloat16)
    context, logsum = lax.map(
        attend_block, (heads_view(query), heads_view(keys), heads_view(values), block_kind)
    )
    context = context.reshape(count, D)
    branch = project(context, out_weight) + out_bias.astype(jnp.float32)
    first_norm, first_inverse = normalize(inputs.astype(jnp.float32) + branch)
    hidden = first_norm * attn_gain.astype(jnp.float32) + attn_shift.astype(jnp.float32)
    hidden_low = hidden.astype(jnp.bfloat16)
    before = project(hidden_low, up_weight) + up_bias.astype(jnp.float32)
    active = jax.nn.gelu(before, approximate=False).astype(jnp.bfloat16)
    outer = project(active, down_weight) + down_bias.astype(jnp.float32)
    second_norm, second_inverse = normalize(hidden + outer)
    output = (second_norm * ffn_gain.astype(jnp.float32) + ffn_shift.astype(jnp.float32)).astype(
        jnp.bfloat16
    )
    saved = (
        query,
        keys,
        values,
        logsum,
        context,
        first_norm,
        first_inverse,
        hidden_low,
        before,
        active,
        second_norm,
        second_inverse,
    )
    return (output, saved)


def ffn_backward(
    cotangent,
    saved,
    query_weight,
    query_bias,
    key_weight,
    value_weight,
    value_bias,
    out_weight,
    out_bias,
    attn_gain,
    attn_shift,
    up_weight,
    up_bias,
    down_weight,
    down_bias,
    ffn_gain,
    ffn_shift,
):
    (
        query,
        keys,
        values,
        logsum,
        context,
        first_norm,
        first_inverse,
        hidden_low,
        before,
        active,
        second_norm,
        second_inverse,
    ) = saved
    grad_out = cotangent.astype(jnp.float32)
    gain_grad = jnp.sum(grad_out * second_norm, axis=0)
    shift_grad = jnp.sum(grad_out, axis=0)
    grad_ffn_sum = norm_back(grad_out * ffn_gain.astype(jnp.float32), second_norm, second_inverse)
    grad_branch = grad_ffn_sum.astype(jnp.bfloat16)
    down_grad = contract_rows(active, grad_branch)
    down_bias_grad = jnp.sum(grad_branch.astype(jnp.float32), axis=0)
    grad_active = project_back(grad_branch, down_weight)
    grad_before = (grad_active * gelu_slope(before)).astype(jnp.bfloat16)
    up_grad = contract_rows(hidden_low, grad_before)
    up_bias_grad = jnp.sum(grad_before.astype(jnp.float32), axis=0)
    grad_hidden = project_back(grad_before, up_weight) + grad_ffn_sum
    return (grad_hidden, (up_grad, up_bias_grad, down_grad, down_bias_grad, gain_grad, shift_grad))


def attn_backward(
    inputs,
    block_kind,
    grad_hidden,
    saved,
    query_weight,
    query_bias,
    key_weight,
    value_weight,
    value_bias,
    out_weight,
    out_bias,
    attn_gain,
    attn_shift,
    up_weight,
    up_bias,
    down_weight,
    down_bias,
    ffn_gain,
    ffn_shift,
):
    (
        query,
        keys,
        values,
        logsum,
        context,
        first_norm,
        first_inverse,
        hidden_low,
        before,
        active,
        second_norm,
        second_inverse,
    ) = saved
    count = inputs.shape[0]
    gain_grad = jnp.sum(grad_hidden * first_norm, axis=0)
    shift_grad = jnp.sum(grad_hidden, axis=0)
    grad_attn_sum = norm_back(
        grad_hidden * attn_gain.astype(jnp.float32), first_norm, first_inverse
    )
    grad_branch = grad_attn_sum.astype(jnp.bfloat16)
    out_grad = contract_rows(context, grad_branch)
    out_bias_grad = jnp.sum(grad_branch.astype(jnp.float32), axis=0)
    grad_context = project_back(grad_branch, out_weight).astype(jnp.bfloat16)
    grad_query, grad_keys, grad_values = lax.map(
        attend_back,
        (
            heads_view(query),
            heads_view(keys),
            heads_view(values),
            block_kind,
            logsum,
            heads_view(grad_context),
        ),
    )
    grad_query = grad_query.reshape(count, D).astype(jnp.bfloat16)
    grad_keys = grad_keys.reshape(count, D).astype(jnp.bfloat16)
    grad_values = grad_values.reshape(count, D).astype(jnp.bfloat16)
    query_grad = contract_rows(inputs, grad_query)
    query_bias_grad = jnp.sum(grad_query.astype(jnp.float32), axis=0)
    key_grad = contract_rows(inputs, grad_keys)
    value_grad = contract_rows(inputs, grad_values)
    value_bias_grad = jnp.sum(grad_values.astype(jnp.float32), axis=0)
    input_grad = (
        project_back(grad_query, query_weight)
        + project_back(grad_keys, key_weight)
        + project_back(grad_values, value_weight)
        + grad_attn_sum
    )
    return (
        input_grad,
        (
            query_grad,
            query_bias_grad,
            key_grad,
            value_grad,
            value_bias_grad,
            out_grad,
            out_bias_grad,
            gain_grad,
            shift_grad,
        ),
    )


def swap(value, mask, count):
    return lax.ppermute(value, "fsdp", [(i, i ^ mask) for i in range(count)])


def gather_rows(piece, count):
    me = lax.axis_index("fsdp")
    held = piece[None]
    bit = count // 2
    while bit:
        other = swap(held, bit, count)
        mine_low = (me & bit) == 0
        held = jnp.stack(
            [jnp.where(mine_low, held, other), jnp.where(mine_low, other, held)], axis=1
        ).reshape((-1,) + piece.shape)
        bit //= 2
    return held


def scatter_sum(parts, count):
    me = lax.axis_index("fsdp")
    held = parts
    bit = 1
    while bit < count:
        pairs = held.reshape((held.shape[0] // 2, 2) + held.shape[1:])
        mine = ((me & bit) != 0).astype(jnp.int32)
        keep = lax.dynamic_index_in_dim(pairs, mine, 1, keepdims=False)
        send = lax.dynamic_index_in_dim(pairs, 1 - mine, 1, keepdims=False)
        held = (keep.astype(jnp.float32) + swap(send, bit, count).astype(jnp.float32)).astype(
            jnp.bfloat16
        )
        bit *= 2
    held = held[0]
    other = lax.ppermute(held, "rep", [(0, 1), (1, 0)])
    return held.astype(jnp.float32) + other.astype(jnp.float32)


def pack_vectors(vectors, rows):
    flat = jnp.concatenate([v.reshape(-1) for v in vectors])
    return jnp.pad(flat, (0, rows * D - flat.shape[0])).reshape(rows, D)


def shards(
    inputs,
    block_kind,
    query_weight,
    query_bias,
    key_weight,
    value_weight,
    value_bias,
    out_weight,
    out_bias,
    attn_gain,
    attn_shift,
    up_weight,
    up_bias,
    down_weight,
    down_bias,
    ffn_gain,
    ffn_shift,
    cotangent,
):
    rows = query_weight.shape[0]
    count = D // rows
    wide = up_weight.shape[1] // D
    vectors = (
        query_bias,
        value_bias,
        out_bias,
        attn_gain,
        attn_shift,
        up_bias,
        down_bias,
        ffn_gain,
        ffn_shift,
    )
    sizes = [v.shape[0] for v in vectors]
    spare = -(-sum(sizes) // D)
    first = gather_rows(
        jnp.concatenate([query_weight, key_weight, value_weight, pack_vectors(vectors, spare)]),
        count,
    )
    second = gather_rows(
        jnp.concatenate(
            [out_weight] + [up_weight[:, D * i : D * (i + 1)] for i in range(wide)]
        ),
        count,
    )
    third = gather_rows(down_weight, count)
    all_query = first[:, :rows].reshape(D, D)
    all_key = first[:, rows : 2 * rows].reshape(D, D)
    all_value = first[:, 2 * rows : 3 * rows].reshape(D, D)
    flat = first[:, 3 * rows :].reshape(count, -1)
    whole, at = [], 0
    for size in sizes:
        whole.append(flat[:, at : at + size].reshape(-1))
        at += size
    all_out = second[:, :rows].reshape(D, D)
    all_up = jnp.concatenate(
        [second[:, rows * (1 + i) : rows * (2 + i)].reshape(D, D) for i in range(wide)], axis=1
    )
    all_down = third.reshape(-1, D)
    gathered = (
        all_query,
        whole[0],
        all_key,
        all_value,
        whole[1],
        all_out,
        whole[2],
        whole[3],
        whole[4],
        all_up,
        whole[5],
        all_down,
        whole[6],
        whole[7],
        whole[8],
    )
    layer_out, saved = layer_forward(inputs, block_kind, *gathered)
    grad_hidden, ffn_terms = ffn_backward(cotangent, saved, *gathered)
    up_grad, up_bias_grad, down_grad, down_bias_grad, ffn_gain_grad, ffn_shift_grad = ffn_terms
    input_grad, attn_terms = attn_backward(inputs, block_kind, grad_hidden, saved, *gathered)
    (
        query_grad,
        query_bias_grad,
        key_grad,
        value_grad,
        value_bias_grad,
        out_grad,
        out_bias_grad,
        attn_gain_grad,
        attn_shift_grad,
    ) = attn_terms
    low = jnp.bfloat16
    sum_down = scatter_sum(down_grad.astype(low).reshape(count, -1, D), count)
    sum_second = scatter_sum(
        jnp.concatenate(
            [out_grad.astype(low).reshape(count, rows, D)]
            + [
                up_grad[:, D * i : D * (i + 1)].astype(low).reshape(count, rows, D)
                for i in range(wide)
            ],
            axis=1,
        ),
        count,
    )
    vector_grads = (
        query_bias_grad,
        value_bias_grad,
        out_bias_grad,
        attn_gain_grad,
        attn_shift_grad,
        up_bias_grad,
        down_bias_grad,
        ffn_gain_grad,
        ffn_shift_grad,
    )
    flat_grads = jnp.concatenate([v.reshape(count, -1) for v in vector_grads], axis=1)
    flat_grads = jnp.pad(flat_grads, ((0, 0), (0, spare * D - flat_grads.shape[1])))
    sum_first = scatter_sum(
        jnp.concatenate(
            [g.astype(low).reshape(count, rows, D) for g in (query_grad, key_grad, value_grad)]
            + [flat_grads.astype(low).reshape(count, spare, D)],
            axis=1,
        ),
        count,
    )
    flat_sum = sum_first[3 * rows :].reshape(-1)
    owned, at = [], 0
    for size in sizes:
        owned.append(flat_sum[at : at + size])
        at += size
    sum_up = jnp.concatenate(
        [sum_second[rows * (1 + i) : rows * (2 + i)] for i in range(wide)], axis=1
    )
    return (
        layer_out,
        input_grad,
        sum_first[:rows],
        owned[0],
        sum_first[rows : 2 * rows],
        sum_first[2 * rows : 3 * rows],
        owned[1],
        sum_second[:rows],
        owned[2],
        owned[3],
        owned[4],
        sum_up,
        owned[5],
        sum_down,
        owned[6],
        owned[7],
        owned[8],
    )


def solution(mesh):
    placed = (
        P(("rep", "fsdp"), None),
        P(("rep", "fsdp")),
        P("fsdp", None),
        P("fsdp"),
        P("fsdp", None),
        P("fsdp", None),
        P("fsdp"),
        P("fsdp", None),
        P("fsdp"),
        P("fsdp"),
        P("fsdp"),
        P("fsdp", None),
        P("fsdp"),
        P("fsdp", None),
        P("fsdp"),
        P("fsdp"),
        P("fsdp"),
        P(("rep", "fsdp"), None),
    )
    return jax.shard_map(
        shards,
        mesh=mesh,
        in_specs=placed,
        out_specs=(
            P(("rep", "fsdp"), None),
            P(("rep", "fsdp"), None),
            P("fsdp", None),
            P("fsdp"),
            P("fsdp", None),
            P("fsdp", None),
            P("fsdp"),
            P("fsdp", None),
            P("fsdp"),
            P("fsdp"),
            P("fsdp"),
            P("fsdp", None),
            P("fsdp"),
            P("fsdp", None),
            P("fsdp"),
            P("fsdp"),
            P("fsdp"),
        ),
        check_vma=False,
    )
```

```python
import jax
import jax.numpy as jnp
from jax import lax
from jax.experimental import pallas as pl
from jax.experimental.pallas import tpu as pltpu
from jax.sharding import PartitionSpec as P

D = 768
H = 12
HD = 64
LONG = 512
SHORT = 128
QUAD = 256
PAIR = 128
TILE = 768

EPSILON = 1e-05
BLOCKED = -1e30
LOW = jnp.bfloat16
WIDE = jnp.float32
ROOM = 56 << 20

QUERY_BIAS, VALUE_BIAS, OUT_BIAS, ATTN_GAIN, ATTN_SHIFT, DOWN_BIAS, FFN_GAIN, FFN_SHIFT = range(8)


def dot(left, right, left_dim, right_dim):
    return lax.dot_general(
        left, right, (((left_dim,), (right_dim,)), ((), ())), preferred_element_type=WIDE
    )


def row_mean(value):
    return jnp.mean(value, axis=-1, keepdims=True)


def token_sum(value):
    return jnp.sum(value, axis=0, keepdims=True)


def whole(shape):
    zeros = (0,) * len(shape)
    return pl.BlockSpec(shape, lambda *_: zeros, pipeline_mode=pl.Buffered(1))


def flat(ref):
    value = ref[...]
    return value.reshape(-1, value.shape[-1])


def params():
    return pltpu.CompilerParams(vmem_limit_bytes=ROOM)


def cost(flops, moved, transcendentals=0):
    return pl.CostEstimate(
        flops=int(flops), bytes_accessed=int(moved), transcendentals=int(transcendentals)
    )


def half_masks():
    lane = lax.broadcasted_iota(jnp.int32, (1, PAIR), 1)
    return [jnp.where(lane // HD == half, 1.0, 0.0) for half in range(2)]


def attend_kernel(
    kind_ref,
    x_ref,
    wq_ref,
    wk_ref,
    wv_ref,
    vec_ref,
    q_ref,
    k_ref,
    v_ref,
    ctx_ref,
    ctxt_ref,
    raised_ref,
    inv_ref,
):
    x = x_ref[...]
    q_ref[...] = (dot(x, flat(wq_ref), 1, 0) + vec_ref[QUERY_BIAS : QUERY_BIAS + 1]).astype(LOW)
    k_ref[...] = dot(x, flat(wk_ref), 1, 0).astype(LOW)
    v_ref[...] = (dot(x, flat(wv_ref), 1, 0) + vec_ref[VALUE_BIAS : VALUE_BIAS + 1]).astype(LOW)
    part = lax.broadcasted_iota(jnp.int32, (LONG, PAIR), 0) // SHORT
    lane = lax.broadcasted_iota(jnp.int32, (LONG, PAIR), 1)
    blocked = jnp.where(kind_ref[pl.program_id(1)] == 1, 0.0, BLOCKED)
    query_part = jnp.where((lane < LONG // SHORT) & (part != lane), blocked, 0.0).astype(LOW)
    key_part = jnp.where(part == lane, 1.0, 0.0).astype(LOW)
    halves = half_masks()
    for pair in range(QUAD // PAIR):
        cols = pl.ds(pair * PAIR, PAIR)
        q2 = q_ref[:, cols].astype(WIDE) * HD ** (-0.5)
        keys = jnp.concatenate([k_ref[:, cols], key_part], axis=1)
        v2t = v_ref[:, cols].T
        contexts, inverses = [], []
        for half in range(2):
            queries = jnp.concatenate([(q2 * halves[half]).astype(LOW), query_part], axis=1)
            scores = dot(keys, queries, 1, 1)
            peak = jnp.max(scores, axis=0, keepdims=True)
            raised = jnp.exp(scores - peak).astype(LOW)
            raised_ref[0, pair * 2 + half] = raised
            left = jnp.concatenate(
                [v2t[HD * half : HD * half + HD], jnp.ones((16, LONG), LOW)], axis=0
            )
            mixed = dot(left, raised, 1, 0)
            inverse = 1.0 / mixed[HD : HD + 1]
            contexts.append(mixed[:HD] * inverse)
            inverses.append(jnp.broadcast_to(inverse, (HD, LONG)))
        context = jnp.concatenate(contexts, axis=0)
        ctxt_ref[pair * PAIR : pair * PAIR + PAIR, :] = context.astype(LOW)
        ctx_ref[:, cols] = context.T.astype(LOW)
        inv_ref[:, cols] = jnp.concatenate(inverses, axis=0).T


def weight_cols(weights, rows, at):
    return pl.BlockSpec((weights.shape[0], rows, QUAD), lambda j, b, *_: (0, at, j))


def attend(kind, x, weights, rows, vec):
    count = x.shape[0]
    blocks = count // LONG
    tokens = pl.BlockSpec((LONG, QUAD), lambda j, b, *_: (b, j))
    act = jax.ShapeDtypeStruct((count, D), LOW)
    return pl.pallas_call(
        attend_kernel,
        grid_spec=pltpu.PrefetchScalarGridSpec(
            num_scalar_prefetch=1,
            grid=(D // QUAD, blocks),
            in_specs=[
                pl.BlockSpec((LONG, D), lambda j, b, *_: (b, 0)),
                weight_cols(weights, rows, 0),
                weight_cols(weights, rows, 1),
                weight_cols(weights, rows, 2),
                pl.BlockSpec((8, QUAD), lambda j, b, *_: (0, j)),
            ],
            out_specs=[
                tokens,
                tokens,
                tokens,
                tokens,
                pl.BlockSpec((QUAD, LONG), lambda j, b, *_: (j, b)),
                pl.BlockSpec((1, QUAD // HD, LONG, LONG), lambda j, b, *_: (b, j, 0, 0)),
                tokens,
            ],
        ),
        out_shape=[
            act,
            act,
            act,
            act,
            jax.ShapeDtypeStruct((D, count), LOW),
            jax.ShapeDtypeStruct((blocks, H, LONG, LONG), LOW),
            jax.ShapeDtypeStruct((count, D), WIDE),
        ],
        compiler_params=params(),
        cost_estimate=cost(6 * count * D * D + 8 * count * LONG * D, 30 << 20, count * LONG * H),
        name="attend",
    )(kind, x, weights, weights, weights, vec)


def attend_back_kernel(
    xt_ref,
    d_ref,
    ctx_ref,
    inv_ref,
    q_ref,
    k_ref,
    v_ref,
    raised_ref,
    dq_ref,
    dk_ref,
    dv_ref,
    grads_ref,
    bias_ref,
    totals,
):
    block = pl.program_id(1)
    halves = half_masks()
    minus = jnp.full((LONG, PAIR), -1.0, LOW)
    for pair in range(QUAD // PAIR):
        cols = pl.ds(pair * PAIR, PAIR)
        d2 = d_ref[:, cols].astype(WIDE) * inv_ref[:, cols] * HD ** (-0.5)
        along = d2 * ctx_ref[:, cols].astype(WIDE)
        q2 = q_ref[:, cols].astype(WIDE)
        k2t = k_ref[:, cols].T
        values = jnp.concatenate([v_ref[:, cols], minus], axis=1)
        dqt, dk, dv = [], 0, 0
        for half in range(2):
            dm = (d2 * halves[half]).astype(LOW)
            am = (along * halves[half]).astype(LOW)
            raised = raised_ref[0, pair * 2 + half]
            dp = dot(values, jnp.concatenate([dm, am], axis=1), 1, 1)
            ds = (raised.astype(WIDE) * dp).astype(LOW)
            dv = dv + dot(raised, dm, 1, 0)
            dk = dk + dot(ds, (q2 * halves[half]).astype(LOW), 1, 0)
            dqt.append(dot(k2t[HD * half : HD * half + HD], ds, 1, 0))
        dv_ref[:, cols] = (dv * HD**0.5).astype(LOW)
        dk_ref[:, cols] = dk.astype(LOW)
        dq_ref[:, cols] = jnp.concatenate(dqt, axis=0).T.astype(LOW)
    xt = xt_ref[...]
    for at, ref in enumerate((dq_ref, dk_ref, dv_ref)):
        grad = dot(xt, ref[...], 1, 0)

        @pl.when(block == 0)
        def _(grad=grad, at=at):
            totals[at] = grad

        @pl.when(block != 0)
        def _(grad=grad, at=at):
            totals[at] += grad

    @pl.when(block == pl.num_programs(1) - 1)
    def _():
        grads_ref[...] = totals[...].astype(LOW)

    sums = jnp.concatenate(
        [
            token_sum(dq_ref[...].astype(WIDE)),
            token_sum(dv_ref[...].astype(WIDE)),
            jnp.zeros((6, QUAD), WIDE),
        ],
        axis=0,
    )

    @pl.when(block == 0)
    def _():
        bias_ref[...] = sums

    @pl.when(block != 0)
    def _():
        bias_ref[...] += sums


def attend_back(xt, d, ctx, inv, q, k, v, raised):
    count = q.shape[0]
    tokens = pl.BlockSpec((LONG, QUAD), lambda j, b: (b, j))
    act = jax.ShapeDtypeStruct((count, D), LOW)
    return pl.pallas_call(
        attend_back_kernel,
        grid=(D // QUAD, count // LONG),
        in_specs=[pl.BlockSpec((D, LONG), lambda j, b: (0, b))]
        + [tokens] * 6
        + [pl.BlockSpec((1, QUAD // HD, LONG, LONG), lambda j, b: (b, j, 0, 0))],
        out_specs=[
            tokens,
            tokens,
            tokens,
            pl.BlockSpec((3, D, QUAD), lambda j, b: (0, 0, j)),
            pl.BlockSpec((8, QUAD), lambda j, b: (0, j)),
        ],
        out_shape=[
            act,
            act,
            act,
            jax.ShapeDtypeStruct((3, D, D), LOW),
            jax.ShapeDtypeStruct((8, D), WIDE),
        ],
        scratch_shapes=[pltpu.VMEM((3, D, QUAD), WIDE)],
        compiler_params=params(),
        cost_estimate=cost(6 * count * D * D + 16 * count * LONG * D, 30 << 20),
        name="attend_back",
    )(xt, d, ctx, inv, q, k, v, raised)


def up_kernel(
    ctx_ref, x_ref, wo_ref, vec_ref, wu_ref, bu_ref,
    act_ref, slope_ref, norm_ref, inv_ref, hlt_ref, hl_ref,
):
    count = ctx_ref.shape[0]
    step = 256

    @pl.when(pl.program_id(0) == 0)
    def _():
        bias = vec_ref[OUT_BIAS : OUT_BIAS + 1]
        gain = vec_ref[ATTN_GAIN : ATTN_GAIN + 1]
        shift = vec_ref[ATTN_SHIFT : ATTN_SHIFT + 1]
        wo = flat(wo_ref)
        for at in range(0, count, step):
            rows = pl.ds(at, step)
            total = x_ref[rows].astype(WIDE) + dot(ctx_ref[rows], wo, 1, 0) + bias
            centered = total - row_mean(total)
            inverse = lax.rsqrt(row_mean(centered * centered) + EPSILON)
            norm = centered * inverse
            norm_ref[rows] = norm
            inv_ref[rows] = jnp.broadcast_to(inverse, (step, 128))
            hidden = (norm * gain + shift).astype(LOW)
            hl_ref[rows] = hidden
            hlt_ref[:, rows] = hidden.T

    bias = bu_ref[...]
    weight = flat(wu_ref)
    for at in range(0, count, step):
        rows = pl.ds(at, step)
        before = dot(hl_ref[rows], weight, 1, 0) + bias
        half = 0.5 * (1.0 + lax.erf(before * 0.7071067811865476))
        act_ref[rows] = (before * half).astype(LOW)
        slope_ref[rows] = (
            half + before * jnp.exp(-0.5 * before * before) * 0.3989422804014327
        ).astype(LOW)


def up_call(ctx, x, second, rows, vec, up_bias):
    count = x.shape[0]
    hidden = up_bias.shape[1]
    cols = lambda r: pl.BlockSpec((r, TILE), lambda j: (0, j))
    return pl.pallas_call(
        up_kernel,
        grid=(hidden // TILE,),
        in_specs=[
            whole((count, D)),
            whole((count, D)),
            pl.BlockSpec(
                (second.shape[0], rows, D), lambda j: (0, 0, 0), pipeline_mode=pl.Buffered(1)
            ),
            whole((8, D)),
            pl.BlockSpec((second.shape[0], rows, D), lambda j: (0, 1 + j, 0)),
            cols(1),
        ],
        out_specs=[
            cols(count),
            cols(count),
            whole((count, D)),
            whole((count, 128)),
            whole((D, count)),
        ],
        out_shape=[
            jax.ShapeDtypeStruct((count, hidden), LOW),
            jax.ShapeDtypeStruct((count, hidden), LOW),
            jax.ShapeDtypeStruct((count, D), WIDE),
            jax.ShapeDtypeStruct((count, 128), WIDE),
            jax.ShapeDtypeStruct((D, count), LOW),
        ],
        scratch_shapes=[pltpu.VMEM((count, D), LOW)],
        compiler_params=params(),
        cost_estimate=cost(2 * count * D * (D + hidden), 30 << 20, 2 * count * hidden),
        name="up",
    )(ctx, x, second, vec, second, up_bias)


def down_kernel(
    act_ref, wd_ref, norm_ref, vec_ref, cot_ref, out_ref, grad_ref, low_ref, sums_ref
):
    row = lambda at: vec_ref[at : at + 1]
    total = (
        norm_ref[...] * row(ATTN_GAIN)
        + row(ATTN_SHIFT)
        + (dot(act_ref[...], flat(wd_ref), 1, 0) + row(DOWN_BIAS))
    )
    centered = total - row_mean(total)
    inverse = lax.rsqrt(row_mean(centered * centered) + EPSILON)
    norm = centered * inverse
    out_ref[...] = (norm * row(FFN_GAIN) + row(FFN_SHIFT)).astype(LOW)
    grad_out = cot_ref[...].astype(WIDE)
    scaled = grad_out * row(FFN_GAIN)
    grad = inverse * (scaled - row_mean(scaled) - norm * row_mean(scaled * norm))
    grad_ref[...] = grad
    low = grad.astype(LOW)
    low_ref[...] = low
    sums = jnp.concatenate(
        [
            token_sum(grad_out * norm),
            token_sum(grad_out),
            token_sum(low.astype(WIDE)),
            jnp.zeros((5, D), WIDE),
        ],
        axis=0,
    )

    @pl.when(pl.program_id(0) == 0)
    def _():
        sums_ref[...] = sums

    @pl.when(pl.program_id(0) != 0)
    def _():
        sums_ref[...] += sums


def down_call(act, third, norm, vec, cotangent):
    count, hidden = act.shape
    tile = 256
    rows = lambda c: pl.BlockSpec((tile, c), lambda i: (i, 0))
    return pl.pallas_call(
        down_kernel,
        grid=(count // tile,),
        in_specs=[rows(hidden), whole(third.shape), rows(D), whole((8, D)), rows(D)],
        out_specs=[rows(D), rows(D), rows(D), whole((8, D))],
        out_shape=[
            jax.ShapeDtypeStruct((count, D), LOW),
            jax.ShapeDtypeStruct((count, D), WIDE),
            jax.ShapeDtypeStruct((count, D), LOW),
            jax.ShapeDtypeStruct((8, D), WIDE),
        ],
        compiler_params=params(),
        cost_estimate=cost(2 * count * D * hidden, 25 << 20),
        name="down",
    )(act, third, norm, vec, cotangent)


def down_grad_kernel(act_ref, low_ref, grad_ref):
    grad_ref[...] = dot(act_ref[...], low_ref[...], 0, 0).astype(LOW)


def down_grad_call(act, low):
    count, hidden = act.shape
    return pl.pallas_call(
        down_grad_kernel,
        grid=(hidden // TILE,),
        in_specs=[pl.BlockSpec((count, TILE), lambda j: (0, j)), whole((count, D))],
        out_specs=pl.BlockSpec((TILE, D), lambda j: (j, 0)),
        out_shape=jax.ShapeDtypeStruct((hidden, D), LOW),
        compiler_params=params(),
        cost_estimate=cost(2 * count * D * hidden, 15 << 20),
        name="down_grad",
    )(act, low)


def up_grad_kernel(
    low_ref, wd_ref, slope_ref, hlt_ref, wu_ref, grad_ref,
    up_ref, bias_ref, hidden_ref, before_scr,
):
    step = pl.program_id(0)
    before_scr[...] = (dot(low_ref[...], flat(wd_ref), 1, 1) * slope_ref[...].astype(WIDE)).astype(
        LOW
    )
    before = before_scr[...]
    up_ref[0] = dot(hlt_ref[...], before, 1, 0).astype(LOW)
    bias_ref[...] = token_sum(before.astype(WIDE))
    back = dot(before, flat(wu_ref), 1, 1)

    @pl.when(step == 0)
    def _():
        hidden_ref[...] = back + grad_ref[...]

    @pl.when(step != 0)
    def _():
        hidden_ref[...] += back


def up_grad_call(low, third, slope, hlt, second, rows, grad):
    count, hidden = slope.shape
    steps = hidden // TILE
    cols = lambda r: pl.BlockSpec((r, TILE), lambda j: (0, j))
    return pl.pallas_call(
        up_grad_kernel,
        grid=(steps,),
        in_specs=[
            whole((count, D)),
            pl.BlockSpec((third.shape[0] // steps,) + third.shape[1:], lambda j: (j, 0, 0)),
            cols(count),
            whole((D, count)),
            pl.BlockSpec((second.shape[0], rows, D), lambda j: (0, 1 + j, 0)),
            whole((count, D)),
        ],
        out_specs=[
            pl.BlockSpec((1, D, TILE), lambda j: (j, 0, 0)),
            cols(1),
            whole((count, D)),
        ],
        out_shape=[
            jax.ShapeDtypeStruct((steps, D, TILE), LOW),
            jax.ShapeDtypeStruct((1, hidden), WIDE),
            jax.ShapeDtypeStruct((count, D), WIDE),
        ],
        scratch_shapes=[pltpu.VMEM((count, TILE), LOW)],
        compiler_params=params(),
        cost_estimate=cost(6 * count * D * hidden, 40 << 20),
        name="up_grad",
    )(low, third, slope, hlt, second, grad)


def norm_back_kernel(
    hidden_ref, norm_ref, inv_ref, vec_ref, ctxt_ref, wo_ref,
    grad_ref, out_ref, ctx_ref, sums_ref, low_scr,
):
    count = hidden_ref.shape[0]
    step = 256
    gain = vec_ref[ATTN_GAIN : ATTN_GAIN + 1]
    wo = flat(wo_ref)
    sums = 0
    for at in range(0, count, step):
        rows = pl.ds(at, step)
        hidden = hidden_ref[rows]
        norm = norm_ref[rows]
        scaled = hidden * gain
        grad = inv_ref[rows][:, 0:1] * (
            scaled - row_mean(scaled) - norm * row_mean(scaled * norm)
        )
        grad_ref[rows] = grad
        low = grad.astype(LOW)
        low_scr[rows] = low
        sums = sums + jnp.concatenate(
            [
                token_sum(hidden * norm),
                token_sum(hidden),
                token_sum(low.astype(WIDE)),
                jnp.zeros((5, D), WIDE),
            ],
            axis=0,
        )
        ctx_ref[rows] = dot(low, wo, 1, 1).astype(LOW)
    sums_ref[...] = sums
    out_ref[0] = dot(ctxt_ref[...], low_scr[...], 1, 0).astype(LOW)


def norm_back_call(hidden, norm, inv, vec, ctxt, second, rows):
    count = hidden.shape[0]
    return pl.pallas_call(
        norm_back_kernel,
        grid=(1,),
        in_specs=[
            whole((count, D)),
            whole((count, D)),
            whole((count, 128)),
            whole((8, D)),
            whole((D, count)),
            whole((second.shape[0], rows, D)),
        ],
        out_specs=[whole((count, D)), whole((1, D, D)), whole((count, D)), whole((8, D))],
        out_shape=[
            jax.ShapeDtypeStruct((count, D), WIDE),
            jax.ShapeDtypeStruct((1, D, D), LOW),
            jax.ShapeDtypeStruct((count, D), LOW),
            jax.ShapeDtypeStruct((8, D), WIDE),
        ],
        scratch_shapes=[pltpu.VMEM((count, D), LOW)],
        compiler_params=params(),
        cost_estimate=cost(4 * count * D * D, 20 << 20),
        name="norm_back",
    )(hidden, norm, inv, vec, ctxt, second)


def input_grad_kernel(dq_ref, dk_ref, dv_ref, wq_ref, wk_ref, wv_ref, grad_ref, out_ref):
    out_ref[...] = (
        dot(dq_ref[...], flat(wq_ref), 1, 1)
        + dot(dk_ref[...], flat(wk_ref), 1, 1)
        + dot(dv_ref[...], flat(wv_ref), 1, 1)
        + grad_ref[...]
    )


def input_grad_call(dq, dk, dv, first, rows, grad):
    count = dq.shape[0]
    tile = 512
    tokens = pl.BlockSpec((tile, D), lambda i: (i, 0))

    def weight(at):
        return pl.BlockSpec(
            (first.shape[0], rows, D), lambda i: (0, at, 0), pipeline_mode=pl.Buffered(1)
        )

    return pl.pallas_call(
        input_grad_kernel,
        grid=(count // tile,),
        in_specs=[tokens] * 3 + [weight(0), weight(1), weight(2), tokens],
        out_specs=tokens,
        out_shape=jax.ShapeDtypeStruct((count, D), WIDE),
        compiler_params=params(),
        cost_estimate=cost(6 * count * D * D, 15 << 20),
        name="input_grad",
    )(dq, dk, dv, first, first, first, grad)


def swap(value, mask, count):
    return lax.ppermute(value, "fsdp", [(i, i ^ mask) for i in range(count)])


def gather_rows(piece, count):
    me = lax.axis_index("fsdp")
    held = piece[None]
    bit = count // 2
    while bit:
        other = swap(held, bit, count)
        mine_low = (me & bit) == 0
        held = jnp.stack(
            [jnp.where(mine_low, held, other), jnp.where(mine_low, other, held)], axis=1
        ).reshape((-1,) + piece.shape)
        bit //= 2
    return held


def pick(parts, at):
    picked = []
    for part in parts:
        k, count, rows, width = part.shape
        pairs = part.reshape(k, count // 2, 2, rows, width)
        half = lax.dynamic_index_in_dim(pairs, at, 2, keepdims=False)
        picked.append(jnp.moveaxis(half, 0, 1).reshape(count // 2, k * rows, width))
    return picked[0] if len(picked) == 1 else jnp.concatenate(picked, axis=1)


def scatter_sum(parts, count):
    me = lax.axis_index("fsdp")
    held = parts
    bit = 1
    while bit < count:
        mine = ((me & bit) != 0).astype(jnp.int32)
        other = swap(pick(held, 1 - mine), bit, count)
        total = (pick(held, mine).astype(WIDE) + other.astype(WIDE)).astype(LOW)
        held = [total[None]]
        bit *= 2
    held = held[0][0, 0]
    other = lax.ppermute(held, "rep", [(0, 1), (1, 0)])
    return held.astype(WIDE) + other.astype(WIDE)


def matrices(gathered, number, rows):
    if rows % 16 == 0:
        return gathered, rows
    count = gathered.shape[0]
    parts = gathered[:, : number * rows].reshape(count, number, rows, D)
    return jnp.moveaxis(parts, 1, 0).reshape(1, number * count * rows, D), count * rows


def shards(
    inputs,
    block_kind,
    query_weight,
    query_bias,
    key_weight,
    value_weight,
    value_bias,
    out_weight,
    out_bias,
    attn_gain,
    attn_shift,
    up_weight,
    up_bias,
    down_weight,
    down_bias,
    ffn_gain,
    ffn_shift,
    cotangent,
):
    rows = query_weight.shape[0]
    count = D // rows
    hidden = up_weight.shape[1]
    steps = hidden // TILE
    vectors = (
        query_bias,
        value_bias,
        out_bias,
        attn_gain,
        attn_shift,
        down_bias,
        ffn_gain,
        ffn_shift,
    )
    used = 8 * rows + up_bias.shape[0]
    spare = -(-used // D)
    packed = jnp.concatenate(vectors + (up_bias, jnp.zeros((spare * D - used,), LOW)))
    first = gather_rows(
        jnp.concatenate([query_weight, key_weight, value_weight, packed.reshape(spare, D)]), count
    )
    second = gather_rows(
        jnp.concatenate(
            [out_weight] + [up_weight[:, TILE * i : TILE * (i + 1)] for i in range(steps)]
        ),
        count,
    )
    third = gather_rows(down_weight, count)
    whole_packed = first[:, 3 * rows :].reshape(count, spare * D)
    vec = (
        jnp.moveaxis(whole_packed[:, : 8 * rows].reshape(count, 8, rows), 1, 0)
        .reshape(8, D)
        .astype(WIDE)
    )
    all_up_bias = whole_packed[:, 8 * rows : used].reshape(1, hidden).astype(WIDE)
    first, block = matrices(first, 3, rows)
    second, _ = matrices(second, 1 + steps, rows)

    q, k, v, ctx, ctxt, raised, inv = attend(block_kind, inputs, first, block, vec)
    act, slope, norm, first_inv, hlt = up_call(ctx, inputs, second, block, vec, all_up_bias)
    layer_out, grad, low, ffn_sums = down_call(act, third, norm, vec, cotangent)
    down_grad = down_grad_call(act, low)
    up_grad, up_bias_grad, grad_hidden = up_grad_call(low, third, slope, hlt, second, block, grad)
    grad_attn, out_grad, grad_ctx, attn_sums = norm_back_call(
        grad_hidden, norm, first_inv, vec, ctxt, second, block
    )
    dq, dk, dv, qkv_grad, bias_sums = attend_back(
        inputs.T, grad_ctx, ctx, inv, q, k, v, raised
    )
    input_grad = input_grad_call(dq, dk, dv, first, block, grad_attn)

    sum_down = scatter_sum([down_grad.reshape(1, count, -1, D)], count)
    sum_second = scatter_sum(
        [out_grad.reshape(1, count, rows, D), up_grad.reshape(steps, count, rows, TILE)], count
    )
    vector_grads = jnp.concatenate([bias_sums[:2], attn_sums[2:3], attn_sums[:2], ffn_sums[2:3], ffn_sums[:2]])
    packed_grads = jnp.concatenate(
        [
            jnp.moveaxis(vector_grads.reshape(8, count, rows), 0, 1).reshape(count, 8 * rows),
            up_bias_grad.reshape(count, -1),
            jnp.zeros((count, spare * D - used), WIDE),
        ],
        axis=1,
    ).astype(LOW)
    sum_first = scatter_sum(
        [qkv_grad.reshape(3, count, rows, D), packed_grads.reshape(1, count, spare, D)], count
    )
    own = sum_first[3 * rows :].reshape(-1)
    vector = lambda at: own[at * rows : (at + 1) * rows]
    sum_up = jnp.concatenate(
        [sum_second[rows * (1 + i) : rows * (2 + i)] for i in range(steps)], axis=1
    )
    return (
        layer_out,
        input_grad,
        sum_first[:rows],
        vector(QUERY_BIAS),
        sum_first[rows : 2 * rows],
        sum_first[2 * rows : 3 * rows],
        vector(VALUE_BIAS),
        sum_second[:rows],
        vector(OUT_BIAS),
        vector(ATTN_GAIN),
        vector(ATTN_SHIFT),
        sum_up,
        own[8 * rows : used],
        sum_down,
        vector(DOWN_BIAS),
        vector(FFN_GAIN),
        vector(FFN_SHIFT),
    )


def solution(mesh):
    tokens = P(("rep", "fsdp"), None)
    matrix = P("fsdp", None)
    vector = P("fsdp")
    params_placed = (
        matrix,
        vector,
        matrix,
        matrix,
        vector,
        matrix,
        vector,
        vector,
        vector,
        matrix,
        vector,
        matrix,
        vector,
        vector,
        vector,
    )
    return jax.shard_map(
        shards,
        mesh=mesh,
        in_specs=(tokens, P(("rep", "fsdp")), *params_placed, tokens),
        out_specs=(tokens, tokens, *params_placed),
        check_vma=False,
    )
```

```python
import functools

import jax
import jax.numpy as jnp
from jax import lax
from jax.experimental import pallas as pl
from jax.experimental.pallas import tpu as pltpu
from jax.sharding import PartitionSpec as P

D = 768
H = 12
HD = 64
LONG = 512
SHORT = 128
QUAD = 256
PAIR = 128
TILE = 768

EPSILON = 1e-05
BLOCKED = -1e30
LOW = jnp.bfloat16
WIDE = jnp.float32
ROOM = 56 << 20

QUERY_BIAS, VALUE_BIAS, OUT_BIAS, ATTN_GAIN, ATTN_SHIFT, DOWN_BIAS, FFN_GAIN, FFN_SHIFT = range(8)


def dot(left, right, left_dim, right_dim):
    return lax.dot_general(
        left, right, (((left_dim,), (right_dim,)), ((), ())), preferred_element_type=WIDE
    )


def row_mean(value):
    return jnp.mean(value, axis=-1, keepdims=True)


def token_sum(value):
    return jnp.sum(value, axis=0, keepdims=True)


def whole(shape):
    zeros = (0,) * len(shape)
    return pl.BlockSpec(shape, lambda *_: zeros, pipeline_mode=pl.Buffered(1))


def place(target, sources, slots, me):
    rows = sources[0].shape[1]
    for source, distances in zip(sources, slots):
        for at, distance in enumerate(distances):
            start = pl.multiple_of((me ^ distance) * rows, rows)
            target[pl.ds(start, rows), :] = source[at]


def params():
    return pltpu.CompilerParams(vmem_limit_bytes=ROOM)


def cost(microseconds):
    return pl.CostEstimate(
        flops=int(microseconds * 1e8), bytes_accessed=1 << 20, transcendentals=0
    )


def unplace(keep, send, source, slots, me, top, rows):
    for target, distances in zip((keep, send), slots):
        for at, distance in enumerate(distances):
            start = pl.multiple_of((me ^ distance) * rows, rows)
            target[at, top : top + rows, :] = source(pl.ds(start, rows)).astype(LOW)


def half_masks():
    lane = lax.broadcasted_iota(jnp.int32, (1, PAIR), 1)
    return [jnp.where(lane // HD == half, 1.0, 0.0) for half in range(2)]


def attend_kernel(slots, kind_ref, me_ref, x_ref, vec_ref, *refs):
    pieces = len(slots)
    sources, refs = refs[: 3 * pieces], refs[3 * pieces :]
    q_ref, k_ref, v_ref, ctx_ref, ctxt_ref, raised_ref, inv_ref, weight_ref = refs

    @pl.when(pl.program_id(1) == 0)
    def _():
        for at in range(3):
            place(weight_ref.at[at], sources[at * pieces : (at + 1) * pieces], slots, me_ref[0])

    x = x_ref[...]
    q_ref[...] = (dot(x, weight_ref[0], 1, 0) + vec_ref[QUERY_BIAS : QUERY_BIAS + 1]).astype(LOW)
    k_ref[...] = dot(x, weight_ref[1], 1, 0).astype(LOW)
    v_ref[...] = (dot(x, weight_ref[2], 1, 0) + vec_ref[VALUE_BIAS : VALUE_BIAS + 1]).astype(LOW)
    part = lax.broadcasted_iota(jnp.int32, (LONG, PAIR), 0) // SHORT
    lane = lax.broadcasted_iota(jnp.int32, (LONG, PAIR), 1)
    blocked = jnp.where(kind_ref[pl.program_id(1)] == 1, 0.0, BLOCKED)
    query_part = jnp.where((lane < LONG // SHORT) & (part != lane), blocked, 0.0).astype(LOW)
    key_part = jnp.where(part == lane, 1.0, 0.0).astype(LOW)
    halves = half_masks()
    for pair in range(QUAD // PAIR):
        cols = pl.ds(pair * PAIR, PAIR)
        q2 = q_ref[:, cols].astype(WIDE) * HD ** (-0.5)
        keys = jnp.concatenate([k_ref[:, cols], key_part], axis=1)
        v2t = v_ref[:, cols].T
        contexts, inverses = [], []
        for half in range(2):
            queries = jnp.concatenate([(q2 * halves[half]).astype(LOW), query_part], axis=1)
            scores = dot(keys, queries, 1, 1)
            peak = jnp.max(scores, axis=0, keepdims=True)
            raised = jnp.exp(scores - peak).astype(LOW)
            raised_ref[0, pair * 2 + half] = raised
            left = jnp.concatenate(
                [v2t[HD * half : HD * half + HD], jnp.ones((16, LONG), LOW)], axis=0
            )
            mixed = dot(left, raised, 1, 0)
            inverse = 1.0 / mixed[HD : HD + 1]
            contexts.append(mixed[:HD] * inverse)
            inverses.append(jnp.broadcast_to(inverse, (HD, LONG)))
        context = jnp.concatenate(contexts, axis=0)
        ctxt_ref[pair * PAIR : pair * PAIR + PAIR, :] = context.astype(LOW)
        ctx_ref[:, cols] = context.T.astype(LOW)
        inv_ref[:, cols] = jnp.concatenate(inverses, axis=0).T


def attend(kind, me, x, first, vec):
    pieces, slots, rows = first
    count = x.shape[0]
    blocks = count // LONG
    tokens = pl.BlockSpec((LONG, QUAD), lambda j, b, *_: (b, j))
    act = jax.ShapeDtypeStruct((count, D), LOW)
    return pl.pallas_call(
        functools.partial(attend_kernel, slots),
        grid_spec=pltpu.PrefetchScalarGridSpec(
            num_scalar_prefetch=2,
            grid=(D // QUAD, blocks),
            in_specs=[
                pl.BlockSpec((LONG, D), lambda j, b, *_: (b, 0)),
                pl.BlockSpec((8, QUAD), lambda j, b, *_: (0, j)),
            ]
            + [
                pl.BlockSpec((piece.shape[0], rows, QUAD), lambda j, b, *_, at=at: (0, at, j))
                for at in range(3)
                for piece in pieces
            ],
            out_specs=[
                tokens,
                tokens,
                tokens,
                tokens,
                pl.BlockSpec((QUAD, LONG), lambda j, b, *_: (j, b)),
                pl.BlockSpec((1, QUAD // HD, LONG, LONG), lambda j, b, *_: (b, j, 0, 0)),
                tokens,
                pl.BlockSpec((3, D, QUAD), lambda j, b, *_: (0, 0, j)),
            ],
        ),
        out_shape=[
            act,
            act,
            act,
            act,
            jax.ShapeDtypeStruct((D, count), LOW),
            jax.ShapeDtypeStruct((blocks, H, LONG, LONG), LOW),
            jax.ShapeDtypeStruct((count, D), WIDE),
            jax.ShapeDtypeStruct((3, D, D), LOW),
        ],
        compiler_params=params(),
        cost_estimate=cost(21),
        name="attend",
    )(kind, me, x, vec, *(list(pieces) * 3))


def attend_back_kernel(
    slots,
    me_ref,
    xt_ref,
    d_ref,
    ctx_ref,
    inv_ref,
    q_ref,
    k_ref,
    v_ref,
    raised_ref,
    dq_ref,
    dk_ref,
    dv_ref,
    keep_ref,
    send_ref,
    bias_ref,
    totals,
):
    block = pl.program_id(1)
    halves = half_masks()
    minus = jnp.full((LONG, PAIR), -1.0, LOW)
    for pair in range(QUAD // PAIR):
        cols = pl.ds(pair * PAIR, PAIR)
        d2 = d_ref[:, cols].astype(WIDE) * inv_ref[:, cols] * HD ** (-0.5)
        along = d2 * ctx_ref[:, cols].astype(WIDE)
        q2 = q_ref[:, cols].astype(WIDE)
        k2t = k_ref[:, cols].T
        values = jnp.concatenate([v_ref[:, cols], minus], axis=1)
        dqt, dk, dv = [], 0, 0
        for half in range(2):
            dm = (d2 * halves[half]).astype(LOW)
            am = (along * halves[half]).astype(LOW)
            raised = raised_ref[0, pair * 2 + half]
            dp = dot(values, jnp.concatenate([dm, am], axis=1), 1, 1)
            ds = (raised.astype(WIDE) * dp).astype(LOW)
            dv = dv + dot(raised, dm, 1, 0)
            dk = dk + dot(ds, (q2 * halves[half]).astype(LOW), 1, 0)
            dqt.append(dot(k2t[HD * half : HD * half + HD], ds, 1, 0))
        dv_ref[:, cols] = (dv * HD**0.5).astype(LOW)
        dk_ref[:, cols] = dk.astype(LOW)
        dq_ref[:, cols] = jnp.concatenate(dqt, axis=0).T.astype(LOW)
    xt = xt_ref[...]
    for at, ref in enumerate((dq_ref, dk_ref, dv_ref)):
        grad = dot(xt, ref[...], 1, 0)

        @pl.when(block == 0)
        def _(grad=grad, at=at):
            totals[at] = grad

        @pl.when(block != 0)
        def _(grad=grad, at=at):
            totals[at] += grad

    @pl.when(block == pl.num_programs(1) - 1)
    def _():
        rows = keep_ref.shape[1] // 3
        for at in range(3):
            unplace(
                keep_ref, send_ref, lambda part, at=at: totals[at, part], slots, me_ref[0], at * rows, rows
            )

    sums = jnp.concatenate(
        [
            token_sum(dq_ref[...].astype(WIDE)),
            token_sum(dv_ref[...].astype(WIDE)),
            jnp.zeros((6, QUAD), WIDE),
        ],
        axis=0,
    )

    @pl.when(block == 0)
    def _():
        bias_ref[...] = sums

    @pl.when(block != 0)
    def _():
        bias_ref[...] += sums


def attend_back(me, slots, quads, xt, d, ctx, inv, q, k, v, raised):
    count = q.shape[0]
    low, number = quads[0], len(quads)
    tokens = pl.BlockSpec((LONG, QUAD), lambda j, b, *_: (b, j + low))
    grads = pl.BlockSpec((LONG, QUAD), lambda j, b, *_: (b, j))
    act = jax.ShapeDtypeStruct((count, number * QUAD), LOW)
    kept, rows = len(slots[0]), D // (len(slots[0]) + len(slots[1]))
    part = pl.BlockSpec((kept, 3 * rows, QUAD), lambda j, b, *_: (0, 0, j))
    half = jax.ShapeDtypeStruct((kept, 3 * rows, number * QUAD), LOW)
    return pl.pallas_call(
        functools.partial(attend_back_kernel, slots),
        grid_spec=pltpu.PrefetchScalarGridSpec(
            num_scalar_prefetch=1,
            grid=(number, count // LONG),
            in_specs=[pl.BlockSpec((D, LONG), lambda j, b, *_: (0, b))]
            + [tokens] * 6
            + [pl.BlockSpec((1, QUAD // HD, LONG, LONG), lambda j, b, *_: (b, j + low, 0, 0))],
            out_specs=[
                grads,
                grads,
                grads,
                part,
                part,
                pl.BlockSpec((8, QUAD), lambda j, b, *_: (0, j)),
            ],
            scratch_shapes=[pltpu.VMEM((3, D, QUAD), WIDE)],
        ),
        out_shape=[
            act,
            act,
            act,
            half,
            half,
            jax.ShapeDtypeStruct((8, number * QUAD), WIDE),
        ],
        compiler_params=params(),
        cost_estimate=cost(10 * number),
        name="attend_back",
    )(me, xt, d, ctx, inv, q, k, v, raised)


def up_kernel(slots, me_ref, ctx_ref, x_ref, vec_ref, bu_ref, *refs):
    pieces = len(slots)
    outs, ups, refs = refs[:pieces], refs[pieces : 2 * pieces], refs[2 * pieces :]
    act_ref, slope_ref, norm_ref, inv_ref, hlt_ref, wo_ref, wu_ref, hl_ref = refs
    count = ctx_ref.shape[0]
    step = 256
    place(wu_ref.at[0], ups, slots, me_ref[0])

    @pl.when(pl.program_id(0) == 0)
    def _():
        bias = vec_ref[OUT_BIAS : OUT_BIAS + 1]
        gain = vec_ref[ATTN_GAIN : ATTN_GAIN + 1]
        shift = vec_ref[ATTN_SHIFT : ATTN_SHIFT + 1]
        place(wo_ref, outs, slots, me_ref[0])
        wo = wo_ref[...]
        for at in range(0, count, step):
            rows = pl.ds(at, step)
            total = x_ref[rows].astype(WIDE) + dot(ctx_ref[rows], wo, 1, 0) + bias
            centered = total - row_mean(total)
            inverse = lax.rsqrt(row_mean(centered * centered) + EPSILON)
            norm = centered * inverse
            norm_ref[rows] = norm
            inv_ref[rows] = jnp.broadcast_to(inverse, (step, 128))
            hidden = (norm * gain + shift).astype(LOW)
            hl_ref[rows] = hidden
            hlt_ref[:, rows] = hidden.T

    bias = bu_ref[...]
    weight = wu_ref[0]
    for at in range(0, count, step):
        rows = pl.ds(at, step)
        before = dot(hl_ref[rows], weight, 1, 0) + bias
        half = 0.5 * (1.0 + lax.erf(before * 0.7071067811865476))
        act_ref[rows] = (before * half).astype(LOW)
        slope_ref[rows] = (
            half + before * jnp.exp(-0.5 * before * before) * 0.3989422804014327
        ).astype(LOW)


def up_call(me, ctx, x, second, vec, up_bias):
    pieces, slots, rows = second
    count = x.shape[0]
    hidden = up_bias.shape[1]
    steps = hidden // TILE
    cols = lambda r: pl.BlockSpec((r, TILE), lambda j, *_: (0, j))
    return pl.pallas_call(
        functools.partial(up_kernel, slots),
        grid_spec=pltpu.PrefetchScalarGridSpec(
            num_scalar_prefetch=1,
            grid=(steps,),
            in_specs=[whole((count, D)), whole((count, D)), whole((8, D)), cols(1)]
            + [
                pl.BlockSpec(
                    (piece.shape[0], rows, D),
                    lambda j, *_: (0, 0, 0),
                    pipeline_mode=pl.Buffered(1),
                )
                for piece in pieces
            ]
            + [
                pl.BlockSpec((piece.shape[0], rows, D), lambda j, *_: (0, 1 + j, 0))
                for piece in pieces
            ],
            out_specs=[
                cols(count),
                cols(count),
                whole((count, D)),
                whole((count, 128)),
                whole((D, count)),
                whole((D, D)),
                pl.BlockSpec((1, D, TILE), lambda j, *_: (j, 0, 0)),
            ],
            scratch_shapes=[pltpu.VMEM((count, D), LOW)],
        ),
        out_shape=[
            jax.ShapeDtypeStruct((count, hidden), LOW),
            jax.ShapeDtypeStruct((count, hidden), LOW),
            jax.ShapeDtypeStruct((count, D), WIDE),
            jax.ShapeDtypeStruct((count, 128), WIDE),
            jax.ShapeDtypeStruct((D, count), LOW),
            jax.ShapeDtypeStruct((D, D), LOW),
            jax.ShapeDtypeStruct((steps, D, TILE), LOW),
        ],
        compiler_params=params(),
        cost_estimate=cost(15),
        name="up",
    )(me, ctx, x, vec, up_bias, *pieces, *pieces)


def down_kernel(slots, me_ref, act_ref, norm_ref, vec_ref, cot_ref, *refs):
    sources = refs[: len(slots)]
    out_ref, grad_ref, low_ref, sums_ref, wd_ref = refs[len(slots) :]

    @pl.when(pl.program_id(0) == 0)
    def _():
        place(wd_ref, sources, slots, me_ref[0])

    row = lambda at: vec_ref[at : at + 1]
    total = (
        norm_ref[...] * row(ATTN_GAIN)
        + row(ATTN_SHIFT)
        + (dot(act_ref[...], wd_ref[...], 1, 0) + row(DOWN_BIAS))
    )
    centered = total - row_mean(total)
    inverse = lax.rsqrt(row_mean(centered * centered) + EPSILON)
    norm = centered * inverse
    out_ref[...] = (norm * row(FFN_GAIN) + row(FFN_SHIFT)).astype(LOW)
    grad_out = cot_ref[...].astype(WIDE)
    scaled = grad_out * row(FFN_GAIN)
    grad = inverse * (scaled - row_mean(scaled) - norm * row_mean(scaled * norm))
    grad_ref[...] = grad
    low = grad.astype(LOW)
    low_ref[...] = low
    sums = jnp.concatenate(
        [
            token_sum(grad_out * norm),
            token_sum(grad_out),
            token_sum(low.astype(WIDE)),
            jnp.zeros((5, D), WIDE),
        ],
        axis=0,
    )

    @pl.when(pl.program_id(0) == 0)
    def _():
        sums_ref[...] = sums

    @pl.when(pl.program_id(0) != 0)
    def _():
        sums_ref[...] += sums


def down_call(me, act, third, norm, vec, cotangent):
    pieces, slots, _ = third
    count, hidden = act.shape
    tile = 256
    rows = lambda c: pl.BlockSpec((tile, c), lambda i, *_: (i, 0))
    return pl.pallas_call(
        functools.partial(down_kernel, slots),
        grid_spec=pltpu.PrefetchScalarGridSpec(
            num_scalar_prefetch=1,
            grid=(count // tile,),
            in_specs=[rows(hidden), rows(D), whole((8, D)), rows(D)]
            + [whole(piece.shape) for piece in pieces],
            out_specs=[rows(D), rows(D), rows(D), whole((8, D)), whole((hidden, D))],
        ),
        out_shape=[
            jax.ShapeDtypeStruct((count, D), LOW),
            jax.ShapeDtypeStruct((count, D), WIDE),
            jax.ShapeDtypeStruct((count, D), LOW),
            jax.ShapeDtypeStruct((8, D), WIDE),
            jax.ShapeDtypeStruct((hidden, D), LOW),
        ],
        compiler_params=params(),
        cost_estimate=cost(13),
        name="down",
    )(me, act, norm, vec, cotangent, *pieces)


def down_grad_kernel(owner_ref, me_ref, act_ref, low_ref, keep_ref, send_ref, scratch):
    rows = keep_ref.shape[1]
    scratch[...] = dot(act_ref[...], low_ref[...], 0, 0).astype(LOW)
    mine = lax.rem(me_ref[0], 2) * rows
    keep_ref[0] = scratch[pl.ds(pl.multiple_of(mine, rows), rows)]
    send_ref[0] = scratch[pl.ds(pl.multiple_of(rows - mine, rows), rows)]


def down_grad_plain_kernel(act_ref, low_ref, grad_ref):
    grad_ref[...] = dot(act_ref[...], low_ref[...], 0, 0).astype(LOW)


def down_grad_plain_call(act, low):
    count, hidden = act.shape
    return pl.pallas_call(
        down_grad_plain_kernel,
        grid=(hidden // TILE,),
        in_specs=[pl.BlockSpec((count, TILE), lambda j: (0, j)), whole((count, D))],
        out_specs=pl.BlockSpec((TILE, D), lambda j: (j, 0)),
        out_shape=jax.ShapeDtypeStruct((hidden, D), LOW),
        compiler_params=params(),
        cost_estimate=cost(9),
        name="down_grad",
    )(act, low)


def down_grad_call(me, slots, rows, act, low):
    count, hidden = act.shape
    number = len(slots[0])
    pair = 2 * rows
    owners = (me // 2) ^ (jnp.array(slots[0], jnp.int32) // 2)
    part = pl.BlockSpec((1, rows, D), lambda j, *_: (j, 0, 0))
    half = jax.ShapeDtypeStruct((number, rows, D), LOW)
    return pl.pallas_call(
        down_grad_kernel,
        grid_spec=pltpu.PrefetchScalarGridSpec(
            num_scalar_prefetch=2,
            grid=(number,),
            in_specs=[
                pl.BlockSpec((count, pair), lambda j, owner, _: (0, owner[j])),
                whole((count, D)),
            ],
            out_specs=[part, part],
            scratch_shapes=[pltpu.VMEM((pair, D), LOW)],
        ),
        out_shape=[half, half],
        compiler_params=params(),
        cost_estimate=cost(number),
        name="down_grad",
    )(owners, me, act, low)


def up_grad_kernel(
    slots, me_ref, low_ref, wd_ref, slope_ref, hlt_ref, wu_ref, grad_ref,
    keep_ref, send_ref, bias_ref, hidden_ref, before_scr, grad_scr,
):
    step = pl.program_id(0)
    before_scr[...] = (dot(low_ref[...], wd_ref[...], 1, 1) * slope_ref[...].astype(WIDE)).astype(
        LOW
    )
    before = before_scr[...]
    grad_scr[...] = dot(hlt_ref[...], before, 1, 0).astype(LOW)
    unplace(
        keep_ref, send_ref, lambda part: grad_scr[part], slots, me_ref[0], 0, keep_ref.shape[1]
    )
    bias_ref[...] = token_sum(before.astype(WIDE))
    back = dot(before, wu_ref[0], 1, 1)

    @pl.when(step == 0)
    def _():
        hidden_ref[...] = back + grad_ref[...]

    @pl.when(step != 0)
    def _():
        hidden_ref[...] += back


def up_grad_call(me, slots, tiles, low, down, slope, hlt, up, grad):
    count = slope.shape[0]
    first, steps = tiles[0], len(tiles)
    kept, rows = len(slots[0]), D // (len(slots[0]) + len(slots[1]))
    part = pl.BlockSpec((kept, rows, TILE), lambda j, *_: (0, j, 0))
    half = jax.ShapeDtypeStruct((kept, steps * rows, TILE), LOW)
    return pl.pallas_call(
        functools.partial(up_grad_kernel, slots),
        grid_spec=pltpu.PrefetchScalarGridSpec(
            num_scalar_prefetch=1,
            grid=(steps,),
            in_specs=[
                whole((count, D)),
                pl.BlockSpec((TILE, D), lambda j, *_: (j + first, 0)),
                pl.BlockSpec((count, TILE), lambda j, *_: (0, j + first)),
                whole((D, count)),
                pl.BlockSpec((1, D, TILE), lambda j, *_: (j + first, 0, 0)),
                whole((count, D)),
            ],
            out_specs=[
                part,
                part,
                pl.BlockSpec((1, TILE), lambda j, *_: (0, j)),
                whole((count, D)),
            ],
            scratch_shapes=[pltpu.VMEM((count, TILE), LOW), pltpu.VMEM((D, TILE), LOW)],
        ),
        out_shape=[
            half,
            half,
            jax.ShapeDtypeStruct((1, steps * TILE), WIDE),
            jax.ShapeDtypeStruct((count, D), WIDE),
        ],
        compiler_params=params(),
        cost_estimate=cost(6 * steps),
        name="up_grad",
    )(me, low, down, slope, hlt, up, grad)


def norm_back_kernel(
    slots, me_ref, hidden_ref, norm_ref, inv_ref, vec_ref, ctxt_ref, wo_ref,
    grad_ref, keep_ref, send_ref, ctx_ref, sums_ref, low_scr, out_scr,
):
    count = hidden_ref.shape[0]
    step = 256
    gain = vec_ref[ATTN_GAIN : ATTN_GAIN + 1]
    wo = wo_ref[...]
    sums = 0
    for at in range(0, count, step):
        rows = pl.ds(at, step)
        hidden = hidden_ref[rows]
        norm = norm_ref[rows]
        scaled = hidden * gain
        grad = inv_ref[rows][:, 0:1] * (
            scaled - row_mean(scaled) - norm * row_mean(scaled * norm)
        )
        grad_ref[rows] = grad
        low = grad.astype(LOW)
        low_scr[rows] = low
        sums = sums + jnp.concatenate(
            [
                token_sum(hidden * norm),
                token_sum(hidden),
                token_sum(low.astype(WIDE)),
                jnp.zeros((5, D), WIDE),
            ],
            axis=0,
        )
        ctx_ref[rows] = dot(low, wo, 1, 1).astype(LOW)
    sums_ref[...] = sums
    out_scr[...] = dot(ctxt_ref[...], low_scr[...], 1, 0).astype(LOW)
    unplace(
        keep_ref, send_ref, lambda part: out_scr[part], slots, me_ref[0], 0, keep_ref.shape[1]
    )


def norm_back_call(me, slots, hidden, norm, inv, vec, ctxt, wo):
    count = hidden.shape[0]
    kept, rows = len(slots[0]), D // (len(slots[0]) + len(slots[1]))
    half = (kept, rows, D)
    return pl.pallas_call(
        functools.partial(norm_back_kernel, slots),
        grid_spec=pltpu.PrefetchScalarGridSpec(
            num_scalar_prefetch=1,
            grid=(1,),
            in_specs=[
                whole((count, D)),
                whole((count, D)),
                whole((count, 128)),
                whole((8, D)),
                whole((D, count)),
                whole((D, D)),
            ],
            out_specs=[
                whole((count, D)),
                whole(half),
                whole(half),
                whole((count, D)),
                whole((8, D)),
            ],
            scratch_shapes=[pltpu.VMEM((count, D), LOW), pltpu.VMEM((D, D), LOW)],
        ),
        out_shape=[
            jax.ShapeDtypeStruct((count, D), WIDE),
            jax.ShapeDtypeStruct(half, LOW),
            jax.ShapeDtypeStruct(half, LOW),
            jax.ShapeDtypeStruct((count, D), LOW),
            jax.ShapeDtypeStruct((8, D), WIDE),
        ],
        compiler_params=params(),
        cost_estimate=cost(9),
        name="norm_back",
    )(me, hidden, norm, inv, vec, ctxt, wo)


def input_grad_kernel(pieces, weight_ref, grad_ref, *refs):
    total = grad_ref[...]
    at = 0
    for piece in range(pieces):
        width = refs[3 * piece].shape[1]
        for matrix in range(3):
            total = total + dot(
                refs[3 * piece + matrix][...], weight_ref[matrix, :, at : at + width], 1, 1
            )
        at += width
    refs[-1][...] = total


def input_grad_call(pieces, weights, grad):
    count = grad.shape[0]
    tile = 512
    tokens = lambda width: pl.BlockSpec((tile, width), lambda i: (i, 0))
    flat = [value for piece in pieces for value in piece]
    return pl.pallas_call(
        functools.partial(input_grad_kernel, len(pieces)),
        grid=(count // tile,),
        in_specs=[whole((3, D, D)), tokens(D)] + [tokens(value.shape[1]) for value in flat],
        out_specs=tokens(D),
        out_shape=jax.ShapeDtypeStruct((count, D), WIDE),
        compiler_params=params(),
        cost_estimate=cost(8),
        name="input_grad",
    )(weights, grad, *flat)


def pack_kernel(*refs):
    target, at = refs[-1], 0
    for ref in refs[:-1]:
        target[at : at + ref.shape[0], :] = ref[...]
        at += ref.shape[0]


def pack(parts):
    if any(part.shape[0] % 16 for part in parts[:-1]):
        return jnp.concatenate(parts)
    rows = sum(part.shape[0] for part in parts)
    return pl.pallas_call(
        pack_kernel,
        out_shape=jax.ShapeDtypeStruct((rows, D), LOW),
        compiler_params=params(),
        cost_estimate=cost(1),
        name="pack",
    )(*parts)


def swap(value, mask, count):
    return lax.ppermute(value, "fsdp", [(i, i ^ mask) for i in range(count)])


def after(value, *others):
    return lax.optimization_barrier((value,) + others)[0]


class Gather:
    def __init__(self, piece, count):
        self.held, self.bit, self.count = piece[None], count // 2, count

    def start(self, *others):
        held = after(self.held, *others) if others else self.held
        self.other = swap(held, self.bit, self.count)
        self.bit //= 2

    def land(self, *others):
        other = after(self.other, *others) if others else self.other
        self.held = jnp.concatenate([self.held, other], axis=0)
        return self.held

    def far(self, *others):
        while self.bit > 2:
            self.start(*others)
            self.land()
        return self.held


def slot_order(count):
    order, bit = [0], count // 2
    while bit > 1:
        order = order + [at ^ bit for at in order]
        bit //= 2
    return order, [at ^ 1 for at in order]


def matrices(halves, number, rows, me):
    count = 2 * halves[0].shape[0]
    slots = slot_order(count)
    if rows % 16 == 0:
        return halves, slots, rows
    parts = in_order(jnp.concatenate(halves)[:, : number * rows], slots, me)
    parts = jnp.moveaxis(parts.reshape(count, number, rows, D), 1, 0)
    return (parts.reshape(1, number * count * rows, D),), ([0],), count * rows


def in_order(held, slots, me):
    count = held.shape[0]
    place_of = [0] * count
    for at, distance in enumerate(slots[0] + slots[1]):
        place_of[distance] = at
    held = jnp.concatenate([held[at : at + 1] for at in place_of])
    bit = 1
    while bit < count:
        pairs = held.reshape((count // (2 * bit), 2, bit) + held.shape[1:])
        held = jnp.where((me & bit) != 0, pairs[:, ::-1], pairs).reshape(held.shape)
        bit *= 2
    return held


def to_slots(parts, slots, me):
    count = parts.shape[0]
    bit = 1
    while bit < count:
        pairs = parts.reshape((count // (2 * bit), 2, bit) + parts.shape[1:])
        parts = jnp.where((me & bit) != 0, pairs[:, ::-1], pairs).reshape(parts.shape)
        bit *= 2
    return tuple(
        jnp.concatenate([parts[at : at + 1] for at in distances]) for distances in slots
    )


def sum_order(count):
    bits = count.bit_length() - 2
    order = [
        sum(2 << place for place in range(bits) if at >> (bits - 1 - place) & 1)
        for at in range(count // 2)
    ]
    return order, [at ^ 1 for at in order]


class Sum:
    def __init__(self, keep, send, count, half=False):
        self.terms, self.send, self.count = [keep], send, count
        self.half, self.bit, self.total = half, 1, None

    def start(self, *others):
        send = after(self.send, *others) if others else self.send
        if self.half == "now" or self.bit == self.count:
            self.other = lax.ppermute(send, "rep", [(0, 1), (1, 0)])
        else:
            self.other = swap(send, self.bit, self.count)

    def added(self, part=lambda term: term):
        total = 0
        for term in self.terms:
            total = total + part(term).astype(WIDE)
        return total

    def land(self, *others):
        other = after(self.other, *others) if others else self.other
        if self.bit == self.count:
            if self.half:
                low = lax.axis_index("rep") == 0
                both = jnp.where(low, self.send, other), jnp.where(low, other, self.send)
                self.total = jnp.concatenate(both, axis=1)[0].astype(WIDE)
            else:
                self.total = (self.send.astype(WIDE) + other.astype(WIDE))[0]
            return self.total
        self.terms.append(other)
        if self.half == "now":
            self.half = "done"
        else:
            self.bit *= 2
            if self.half is True:
                return self.halve()
        if self.bit == self.count:
            self.send = self.added().astype(LOW)
            return self.send
        middle = self.terms[0].shape[0] // 2
        self.send = self.added(lambda term: term[middle:]).astype(LOW)
        self.terms = [term[:middle] for term in self.terms]
        return self.send

    def halve(self):
        mine = lax.axis_index("rep")
        slots, rows, width = self.terms[0].shape
        pick = lambda term, at: lax.dynamic_index_in_dim(
            term.reshape(slots, 2, rows // 2, width), at, 1, keepdims=False
        )
        self.send = self.added(lambda term: pick(term, 1 - mine)).astype(LOW)
        self.terms = [pick(term, mine) for term in self.terms]
        self.half = "now"
        return self.send

    def finish(self):
        while self.total is None:
            self.start()
            self.land()


def joined(sums):
    first = sums[0]
    whole = Sum(None, jnp.concatenate([item.send for item in sums], axis=1), first.count, first.half)
    whole.bit = first.bit
    whole.terms = [jnp.concatenate(terms, axis=1) for terms in zip(*(item.terms for item in sums))]
    return whole


def shards(
    inputs,
    block_kind,
    query_weight,
    query_bias,
    key_weight,
    value_weight,
    value_bias,
    out_weight,
    out_bias,
    attn_gain,
    attn_shift,
    up_weight,
    up_bias,
    down_weight,
    down_bias,
    ffn_gain,
    ffn_shift,
    cotangent,
):
    rows = query_weight.shape[0]
    count = D // rows
    hidden = up_weight.shape[1]
    steps = hidden // TILE
    vectors = (
        query_bias,
        value_bias,
        out_bias,
        attn_gain,
        attn_shift,
        down_bias,
        ffn_gain,
        ffn_shift,
    )
    used = 8 * rows + up_bias.shape[0]
    spare = 8
    packed, at = 0, 0
    for value in vectors + (up_bias,):
        packed = packed + jnp.pad(value, (at, spare * D - at - value.shape[0]))
        at += value.shape[0]
    me = lax.axis_index("fsdp").astype(jnp.int32)
    mine = me.reshape(1)

    first = Gather(pack([query_weight, key_weight, value_weight, packed.reshape(spare, D)]), count)
    second = Gather(
        pack([out_weight] + [up_weight[:, TILE * i : TILE * (i + 1)] for i in range(steps)]), count
    )
    third = Gather(down_weight, count)
    first.start()
    at = first.land()
    second.start(at)
    first.start()
    at = second.land(first.land())
    while first.bit > 2:
        first.start()
        at = first.land()
    first.start()
    third.start(at)
    while second.bit > 2:
        second.start()
        at = second.land()
    at = third.land(first.land(at))
    first.start()
    second.start()
    while third.bit > 4:
        third.start()
        at = third.land()
    third.start()
    halves = first.held, first.other
    inputs_t = inputs.T

    slots = slot_order(count)
    whole_packed = in_order(
        jnp.concatenate([half[:, 3 * rows] for half in halves]), slots, me
    )
    vec = (
        jnp.moveaxis(whole_packed[:, : 8 * rows].reshape(count, 8, rows), 1, 0)
        .reshape(8, D)
        .astype(WIDE)
    )
    all_up_bias = whole_packed[:, 8 * rows : used].reshape(1, hidden).astype(WIDE)
    none = jnp.zeros((1,), jnp.int32)
    me_or_none = mine if rows % 16 == 0 else none

    q, k, v, ctx, ctxt, raised, inv, qkv = attend(
        block_kind, me_or_none, after(inputs, at), matrices(halves, 3, rows, me), vec
    )
    at = third.land(ctx)
    third.start()
    at = second.land(at)
    second.start()
    second = matrices((second.held, second.other), 1 + steps, rows, me)
    act, slope, norm, first_inv, hlt, wo, up = up_call(
        me_or_none, after(ctx, at), inputs, second, vec, all_up_bias
    )
    third.land(act)
    third.start()
    third = matrices((third.held, third.other), 1, down_weight.shape[0], me)
    layer_out, grad, low, ffn_sums, down = down_call(
        mine if down_weight.shape[0] % 16 == 0 else none, act, third, norm, vec, cotangent
    )

    order = sum_order(count)
    own_rows = rows % 16 == 0
    quads = D // QUAD
    split = lambda grad, k: grad.reshape(1, k * D, grad.shape[-1])

    def halves_of(keep, send, k):
        if own_rows:
            return keep, send
        parts = jnp.moveaxis(keep.reshape(k, count, rows, keep.shape[-1]), 0, 1)
        return to_slots(parts.reshape(count, k * rows, keep.shape[-1]), order, me)

    kernel_order = order if own_rows else ([0], [])
    down_rows = down_weight.shape[0]
    if 2 * down_rows % 128 == 0:
        middle = count // 4
        near, far = ([part[at] for part in order] for at in (slice(middle), slice(middle, None)))
        far_keep, far_send = down_grad_call(mine, far, down_rows, act, low)
        far_other = swap(far_send, 1, count)
        near_keep, near_send = down_grad_call(mine, near, down_rows, act, after(low, far_keep))
        sum_down = Sum(near_keep, None, count)
        sum_down.bit = 2
        far_other = after(far_other, near_keep)
        sum_down.send = (far_keep.astype(WIDE) + far_other.astype(WIDE)).astype(LOW)
        at = sum_down.send
        sum_down.start()
        sum_down.terms.append(swap(near_send, 1, count))
    else:
        parts = down_grad_plain_call(act, low).reshape(count, down_rows, D)
        sum_down = Sum(*to_slots(parts, order, me), count)
        sum_down.start()
        at = sum_down.land()
        sum_down.start()

    keep, send, up_bias_grad, grad_hidden = up_grad_call(
        me_or_none, kernel_order, list(range(steps)), low, down, slope, hlt, up, after(grad, at)
    )
    sum_up = Sum(*halves_of(keep, send, steps), count, half=True)
    sum_up.start()
    grad_attn, keep, send, grad_ctx, attn_sums = norm_back_call(
        me_or_none, kernel_order, grad_hidden, norm, first_inv, vec, ctxt, wo
    )
    at = sum_up.land(grad_attn)
    sum_up.start()
    at = sum_down.land(at)
    sum_down.start()
    sum_out = Sum(*halves_of(keep, send, 1), count)
    sum_out.start(at)

    parts, sum_qkv, biases = [], [], []
    for quad in range(quads):
        *part, keep, send, bias = attend_back(
            me_or_none, kernel_order, [quad], inputs_t, after(grad_ctx, at), ctx, inv, q, k, v, raised
        )
        parts.append(part)
        biases.append(bias)
        sum_qkv.append(Sum(*halves_of(keep, send, 3), count))
        sum_qkv[-1].start()
        at = bias
        if sum_down.total is None:
            at = sum_down.land(at)
        if sum_down.total is None:
            sum_down.start()
        if quad == 0:
            at = sum_out.land(at)
        if quad > 0:
            at = sum_qkv[quad - 1].land(at)
            sum_qkv[quad - 1].start()
        if quad == quads - 2:
            at = sum_up.land(at)
            sum_up.start()
    bias_sums = jnp.concatenate(biases, axis=1)
    vector_grads = jnp.concatenate(
        [bias_sums[:2], attn_sums[2:3], attn_sums[:2], ffn_sums[2:3], ffn_sums[:2]]
    )
    packed_grads = jnp.concatenate(
        [
            jnp.moveaxis(vector_grads.reshape(8, count, rows), 0, 1).reshape(count, 8 * rows),
            up_bias_grad.reshape(count, -1),
            jnp.zeros((count, spare * D - used), WIDE),
        ],
        axis=1,
    ).astype(LOW)
    sum_vec = Sum(*to_slots(packed_grads.reshape(count, spare, D), order, me), count)
    sum_vec.start()
    sum_vec.land()
    sum_rest = joined([sum_out, sum_vec])
    sum_rest.start()
    at = sum_qkv[-1].land()
    sum_qkv[-1].start()
    input_grad = input_grad_call(parts, qkv, after(grad_attn, at, sum_rest.send))
    for item in [sum_down, sum_up, *sum_qkv, sum_rest]:
        if item.total is None:
            item.land()
        item.finish()
    grad_out = sum_rest.total[:rows]
    own = sum_rest.total[rows:].reshape(-1)
    vector = lambda at: own[at * rows : (at + 1) * rows]
    matrix = lambda at: jnp.concatenate(
        [item.total[at * rows : (at + 1) * rows] for item in sum_qkv], axis=1
    )
    grad_up = sum_up.total
    return (
        layer_out,
        input_grad,
        matrix(0),
        vector(QUERY_BIAS),
        matrix(1),
        matrix(2),
        vector(VALUE_BIAS),
        grad_out,
        vector(OUT_BIAS),
        vector(ATTN_GAIN),
        vector(ATTN_SHIFT),
        jnp.concatenate([grad_up[rows * i : rows * (i + 1)] for i in range(steps)], axis=1),
        own[8 * rows : used],
        sum_down.total,
        vector(DOWN_BIAS),
        vector(FFN_GAIN),
        vector(FFN_SHIFT),
    )


def solution(mesh):
    tokens = P(("rep", "fsdp"), None)
    matrix = P("fsdp", None)
    vector = P("fsdp")
    params_placed = (
        matrix,
        vector,
        matrix,
        matrix,
        vector,
        matrix,
        vector,
        vector,
        vector,
        matrix,
        vector,
        matrix,
        vector,
        vector,
        vector,
    )
    return jax.shard_map(
        shards,
        mesh=mesh,
        in_specs=(tokens, P(("rep", "fsdp")), *params_placed, tokens),
        out_specs=(tokens, tokens, *params_placed),
        check_vma=False,
    )
```

```python
import functools

import jax
import jax.numpy as jnp
from jax import lax
from jax.experimental import pallas as pl
from jax.experimental.pallas import tpu as pltpu
from jax.sharding import PartitionSpec as P

D = 768
H = 12
HD = 64
LONG = 512
SHORT = 128
QUAD = 256
PAIR = 128
TILE = 768

EPSILON = 1e-05
BLOCKED = -1e30
LOW = jnp.bfloat16
WIDE = jnp.float32
ROOM = 56 << 20
EXTRA = 16

QUERY_BIAS, VALUE_BIAS, OUT_BIAS, ATTN_GAIN, ATTN_SHIFT, DOWN_BIAS, FFN_GAIN, FFN_SHIFT = range(8)


def dot(left, right, left_dim, right_dim):
    return lax.dot_general(
        left, right, (((left_dim,), (right_dim,)), ((), ())), preferred_element_type=WIDE
    )


def row_mean(value):
    return jnp.mean(value, axis=-1, keepdims=True)


def token_sum(value):
    return jnp.sum(value, axis=0, keepdims=True)


def whole(shape):
    zeros = (0,) * len(shape)
    return pl.BlockSpec(shape, lambda *_: zeros, pipeline_mode=pl.Buffered(1))


def place(target, sources, slots, me):
    rows = sources[0].shape[1]
    for source, distances in zip(sources, slots):
        for at, distance in enumerate(distances):
            start = pl.multiple_of((me ^ distance) * rows, rows)
            target[pl.ds(start, rows), :] = source[at]


def params():
    return pltpu.CompilerParams(vmem_limit_bytes=ROOM)


def cost(microseconds):
    return pl.CostEstimate(
        flops=int(microseconds * 1.1e9), bytes_accessed=1 << 20, transcendentals=0
    )


def unplace(keep, send, source, slots, me, top, rows):
    for target, distances in zip((keep, send), slots):
        for at, distance in enumerate(distances):
            start = pl.multiple_of((me ^ distance) * rows, rows)
            target[at, top : top + rows, :] = source(pl.ds(start, rows)).astype(LOW)


def to_all(keep, send, slots, top, rows):
    low = rows.astype(LOW)
    for target, distances in zip((keep, send), slots):
        for at in range(len(distances)):
            target[at, top : top + EXTRA, :] = low


def half_masks():
    lane = lax.broadcasted_iota(jnp.int32, (1, PAIR), 1)
    return [jnp.where(lane // HD == half, 1.0, 0.0) for half in range(2)]


def attend_kernel(slots, kind_ref, me_ref, x_ref, vec_ref, *refs):
    pieces = len(slots)
    sources, refs = refs[: 3 * pieces], refs[3 * pieces :]
    q_ref, k_ref, v_ref, ctx_ref, ctxt_ref, raised_ref, inv_ref, weight_ref = refs

    @pl.when(pl.program_id(1) == 0)
    def _():
        for at in range(3):
            place(weight_ref.at[at], sources[at * pieces : (at + 1) * pieces], slots, me_ref[0])

    x = x_ref[...]
    q_ref[...] = (dot(x, weight_ref[0], 1, 0) + vec_ref[QUERY_BIAS : QUERY_BIAS + 1]).astype(LOW)
    k_ref[...] = dot(x, weight_ref[1], 1, 0).astype(LOW)
    v_ref[...] = (dot(x, weight_ref[2], 1, 0) + vec_ref[VALUE_BIAS : VALUE_BIAS + 1]).astype(LOW)
    part = lax.broadcasted_iota(jnp.int32, (LONG, PAIR), 0) // SHORT
    lane = lax.broadcasted_iota(jnp.int32, (LONG, PAIR), 1)
    blocked = jnp.where(kind_ref[pl.program_id(1)] == 1, 0.0, BLOCKED)
    query_part = jnp.where((lane < LONG // SHORT) & (part != lane), blocked, 0.0).astype(LOW)
    key_part = jnp.where(part == lane, 1.0, 0.0).astype(LOW)
    halves = half_masks()
    for pair in range(QUAD // PAIR):
        cols = pl.ds(pair * PAIR, PAIR)
        q2 = q_ref[:, cols].astype(WIDE) * HD ** (-0.5)
        keys = jnp.concatenate([k_ref[:, cols], key_part], axis=1)
        v2t = v_ref[:, cols].T
        contexts, inverses = [], []
        for half in range(2):
            queries = jnp.concatenate([(q2 * halves[half]).astype(LOW), query_part], axis=1)
            scores = dot(keys, queries, 1, 1)
            peak = jnp.max(scores, axis=0, keepdims=True)
            raised = jnp.exp(scores - peak).astype(LOW)
            raised_ref[0, pair * 2 + half] = raised
            left = jnp.concatenate(
                [v2t[HD * half : HD * half + HD], jnp.ones((16, LONG), LOW)], axis=0
            )
            mixed = dot(left, raised, 1, 0)
            inverse = 1.0 / mixed[HD : HD + 1]
            contexts.append(mixed[:HD] * inverse)
            inverses.append(jnp.broadcast_to(inverse, (HD, LONG)))
        context = jnp.concatenate(contexts, axis=0)
        ctxt_ref[pair * PAIR : pair * PAIR + PAIR, :] = context.astype(LOW)
        ctx_ref[:, cols] = context.T.astype(LOW)
        inv_ref[:, cols] = jnp.concatenate(inverses, axis=0).T


def attend(kind, me, quads, x, weights, vec):
    pieces, slots, rows = weights
    count = x.shape[0]
    blocks, number, low = count // LONG, len(quads), quads[0]
    tokens = pl.BlockSpec((LONG, QUAD), lambda j, b, *_: (b, j))
    act = jax.ShapeDtypeStruct((count, number * QUAD), LOW)
    return pl.pallas_call(
        functools.partial(attend_kernel, slots),
        grid_spec=pltpu.PrefetchScalarGridSpec(
            num_scalar_prefetch=2,
            grid=(number, blocks),
            in_specs=[
                pl.BlockSpec((LONG, D), lambda j, b, *_: (b, 0)),
                pl.BlockSpec((8, QUAD), lambda j, b, *_: (0, j + low)),
            ]
            + [
                pl.BlockSpec((piece.shape[0], rows, QUAD), lambda j, b, *_, at=at: (0, at, j))
                for at in range(3)
                for piece in pieces
            ],
            out_specs=[
                tokens,
                tokens,
                tokens,
                tokens,
                pl.BlockSpec((QUAD, LONG), lambda j, b, *_: (j, b)),
                pl.BlockSpec((1, QUAD // HD, LONG, LONG), lambda j, b, *_: (b, j, 0, 0)),
                tokens,
                pl.BlockSpec((3, D, QUAD), lambda j, b, *_: (0, 0, j)),
            ],
        ),
        out_shape=[
            act,
            act,
            act,
            act,
            jax.ShapeDtypeStruct((number * QUAD, count), LOW),
            jax.ShapeDtypeStruct((blocks, number * QUAD // HD, LONG, LONG), LOW),
            jax.ShapeDtypeStruct((count, number * QUAD), WIDE),
            jax.ShapeDtypeStruct((3, D, number * QUAD), LOW),
        ],
        compiler_params=params(),
        cost_estimate=cost(0.1),
        name="attend",
    )(kind, me, x, vec, *(list(pieces) * 3))


def attend_back_kernel(
    slots,
    me_ref,
    xt_ref,
    d_ref,
    ctx_ref,
    inv_ref,
    q_ref,
    k_ref,
    v_ref,
    raised_ref,
    dq_ref,
    dk_ref,
    dv_ref,
    keep_ref,
    send_ref,
    totals,
    biases,
):
    block = pl.program_id(0)
    halves = half_masks()
    minus = jnp.full((LONG, PAIR), -1.0, LOW)
    for pair in range(QUAD // PAIR):
        cols = pl.ds(pair * PAIR, PAIR)
        d2 = d_ref[:, cols].astype(WIDE) * inv_ref[:, cols] * HD ** (-0.5)
        along = d2 * ctx_ref[:, cols].astype(WIDE)
        q2 = q_ref[:, cols].astype(WIDE)
        k2t = k_ref[:, cols].T
        values = jnp.concatenate([v_ref[:, cols], minus], axis=1)
        dqt, dk, dv = [], 0, 0
        for half in range(2):
            dm = (d2 * halves[half]).astype(LOW)
            am = (along * halves[half]).astype(LOW)
            raised = raised_ref[0, pair * 2 + half]
            dp = dot(values, jnp.concatenate([dm, am], axis=1), 1, 1)
            ds = (raised.astype(WIDE) * dp).astype(LOW)
            dv = dv + dot(raised, dm, 1, 0)
            dk = dk + dot(ds, (q2 * halves[half]).astype(LOW), 1, 0)
            dqt.append(dot(k2t[HD * half : HD * half + HD], ds, 1, 0))
        dv_ref[:, cols] = (dv * HD**0.5).astype(LOW)
        dk_ref[:, cols] = dk.astype(LOW)
        dq_ref[:, cols] = jnp.concatenate(dqt, axis=0).T.astype(LOW)
    xt = xt_ref[...]
    for at, ref in enumerate((dq_ref, dk_ref, dv_ref)):
        grad = dot(xt, ref[...], 1, 0)

        @pl.when(block == 0)
        def _(grad=grad, at=at):
            totals[at] = grad

        @pl.when(block != 0)
        def _(grad=grad, at=at):
            totals[at] += grad

    sums = jnp.concatenate(
        [
            token_sum(dq_ref[...].astype(WIDE)),
            token_sum(dv_ref[...].astype(WIDE)),
            jnp.zeros((EXTRA - 2, QUAD), WIDE),
        ],
        axis=0,
    )

    @pl.when(block == 0)
    def _():
        biases[...] = sums

    @pl.when(block != 0)
    def _():
        biases[...] += sums

    @pl.when(block == pl.num_programs(0) - 1)
    def _():
        rows = (keep_ref.shape[1] - EXTRA) // 3
        for at in range(3):
            unplace(
                keep_ref, send_ref, lambda part, at=at: totals[at, part], slots, me_ref[0], at * rows, rows
            )
        to_all(keep_ref, send_ref, slots, 3 * rows, biases[...])


def attend_back(me, slots, quad, at, xt, d, ctx, inv, q, k, v, raised):
    count = q.shape[0]
    tokens = pl.BlockSpec((LONG, QUAD), lambda b, *_: (b, at))
    grads = pl.BlockSpec((LONG, QUAD), lambda b, *_: (b, 0))
    act = jax.ShapeDtypeStruct((count, QUAD), LOW)
    kept, rows = len(slots[0]), D // (len(slots[0]) + len(slots[1]))
    half = (kept, 3 * rows + EXTRA, QUAD)
    return pl.pallas_call(
        functools.partial(attend_back_kernel, slots),
        grid_spec=pltpu.PrefetchScalarGridSpec(
            num_scalar_prefetch=1,
            grid=(count // LONG,),
            in_specs=[
                pl.BlockSpec((D, LONG), lambda b, *_: (0, b)),
                pl.BlockSpec((LONG, QUAD), lambda b, *_: (b, quad)),
            ]
            + [tokens] * 5
            + [pl.BlockSpec((1, QUAD // HD, LONG, LONG), lambda b, *_: (b, at, 0, 0))],
            out_specs=[grads, grads, grads, whole(half), whole(half)],
            scratch_shapes=[pltpu.VMEM((3, D, QUAD), WIDE), pltpu.VMEM((EXTRA, QUAD), WIDE)],
        ),
        out_shape=[act, act, act, jax.ShapeDtypeStruct(half, LOW), jax.ShapeDtypeStruct(half, LOW)],
        compiler_params=params(),
        cost_estimate=cost(2),
        name="attend_back",
    )(me, xt, d, ctx, inv, q, k, v, raised)


def up_kernel(slots, groups, me_ref, x_ref, vec_ref, bu_ref, *refs):
    contexts, refs = refs[:groups], refs[groups:]
    pieces = len(slots)
    outs, ups, refs = refs[:pieces], refs[pieces : 2 * pieces], refs[2 * pieces :]
    act_ref, slope_ref, norm_ref, inv_ref, hlt_ref, wo_ref, wu_ref, hl_ref = refs
    count = x_ref.shape[0]
    step = 256
    place(wu_ref.at[0], ups, slots, me_ref[0])

    @pl.when(pl.program_id(0) == 0)
    def _():
        bias = vec_ref[OUT_BIAS : OUT_BIAS + 1]
        gain = vec_ref[ATTN_GAIN : ATTN_GAIN + 1]
        shift = vec_ref[ATTN_SHIFT : ATTN_SHIFT + 1]
        place(wo_ref, outs, slots, me_ref[0])
        wo = wo_ref[...]
        for at in range(0, count, step):
            rows = pl.ds(at, step)
            context = jnp.concatenate([ref[rows] for ref in contexts], axis=1)
            total = x_ref[rows].astype(WIDE) + dot(context, wo, 1, 0) + bias
            centered = total - row_mean(total)
            inverse = lax.rsqrt(row_mean(centered * centered) + EPSILON)
            norm = centered * inverse
            norm_ref[rows] = norm
            inv_ref[rows] = jnp.broadcast_to(inverse, (step, 128))
            hidden = (norm * gain + shift).astype(LOW)
            hl_ref[rows] = hidden
            hlt_ref[:, rows] = hidden.T

    bias = bu_ref[...]
    weight = wu_ref[0]
    for at in range(0, count, step):
        rows = pl.ds(at, step)
        before = dot(hl_ref[rows], weight, 1, 0) + bias
        half = 0.5 * (1.0 + lax.erf(before * 0.7071067811865476))
        act_ref[rows] = (before * half).astype(LOW)
        slope_ref[rows] = (
            half + before * jnp.exp(-0.5 * before * before) * 0.3989422804014327
        ).astype(LOW)


def up_call(me, contexts, x, second, vec, up_bias):
    pieces, slots, rows = second
    count = x.shape[0]
    hidden = up_bias.shape[1]
    steps = hidden // TILE
    cols = lambda r: pl.BlockSpec((r, TILE), lambda j, *_: (0, j))
    return pl.pallas_call(
        functools.partial(up_kernel, slots, len(contexts)),
        grid_spec=pltpu.PrefetchScalarGridSpec(
            num_scalar_prefetch=1,
            grid=(steps,),
            in_specs=[whole((count, D)), whole((8, D)), cols(1)]
            + [whole(context.shape) for context in contexts]
            + [
                pl.BlockSpec(
                    (piece.shape[0], rows, D),
                    lambda j, *_: (0, 0, 0),
                    pipeline_mode=pl.Buffered(1),
                )
                for piece in pieces
            ]
            + [
                pl.BlockSpec((piece.shape[0], rows, D), lambda j, *_: (0, 1 + j, 0))
                for piece in pieces
            ],
            out_specs=[
                cols(count),
                cols(count),
                whole((count, D)),
                whole((count, 128)),
                whole((D, count)),
                whole((D, D)),
                pl.BlockSpec((1, D, TILE), lambda j, *_: (j, 0, 0)),
            ],
            scratch_shapes=[pltpu.VMEM((count, D), LOW)],
        ),
        out_shape=[
            jax.ShapeDtypeStruct((count, hidden), LOW),
            jax.ShapeDtypeStruct((count, hidden), LOW),
            jax.ShapeDtypeStruct((count, D), WIDE),
            jax.ShapeDtypeStruct((count, 128), WIDE),
            jax.ShapeDtypeStruct((D, count), LOW),
            jax.ShapeDtypeStruct((D, D), LOW),
            jax.ShapeDtypeStruct((steps, D, TILE), LOW),
        ],
        compiler_params=params(),
        cost_estimate=cost(0.1),
        name="up",
    )(me, x, vec, up_bias, *contexts, *pieces, *pieces)


def down_kernel(slots, me_ref, act_ref, norm_ref, vec_ref, cot_ref, *refs):
    sources = refs[: len(slots)]
    out_ref, grad_ref, low_ref, sums_ref, wd_ref = refs[len(slots) :]

    @pl.when(pl.program_id(0) == 0)
    def _():
        place(wd_ref, sources, slots, me_ref[0])

    row = lambda at: vec_ref[at : at + 1]
    total = (
        norm_ref[...] * row(ATTN_GAIN)
        + row(ATTN_SHIFT)
        + (dot(act_ref[...], wd_ref[...], 1, 0) + row(DOWN_BIAS))
    )
    centered = total - row_mean(total)
    inverse = lax.rsqrt(row_mean(centered * centered) + EPSILON)
    norm = centered * inverse
    out_ref[...] = (norm * row(FFN_GAIN) + row(FFN_SHIFT)).astype(LOW)
    grad_out = cot_ref[...].astype(WIDE)
    scaled = grad_out * row(FFN_GAIN)
    grad = inverse * (scaled - row_mean(scaled) - norm * row_mean(scaled * norm))
    grad_ref[...] = grad
    low = grad.astype(LOW)
    low_ref[...] = low
    sums = jnp.concatenate(
        [
            token_sum(grad_out * norm),
            token_sum(grad_out),
            token_sum(low.astype(WIDE)),
            jnp.zeros((5, D), WIDE),
        ],
        axis=0,
    )

    @pl.when(pl.program_id(0) == 0)
    def _():
        sums_ref[...] = sums

    @pl.when(pl.program_id(0) != 0)
    def _():
        sums_ref[...] += sums


def down_call(me, act, third, norm, vec, cotangent):
    pieces, slots, _ = third
    count, hidden = act.shape
    tile = 256
    rows = lambda c: pl.BlockSpec((tile, c), lambda i, *_: (i, 0))
    return pl.pallas_call(
        functools.partial(down_kernel, slots),
        grid_spec=pltpu.PrefetchScalarGridSpec(
            num_scalar_prefetch=1,
            grid=(count // tile,),
            in_specs=[rows(hidden), rows(D), whole((8, D)), rows(D)]
            + [whole(piece.shape) for piece in pieces],
            out_specs=[rows(D), rows(D), rows(D), whole((8, D)), whole((hidden, D))],
        ),
        out_shape=[
            jax.ShapeDtypeStruct((count, D), LOW),
            jax.ShapeDtypeStruct((count, D), WIDE),
            jax.ShapeDtypeStruct((count, D), LOW),
            jax.ShapeDtypeStruct((8, D), WIDE),
            jax.ShapeDtypeStruct((hidden, D), LOW),
        ],
        compiler_params=params(),
        cost_estimate=cost(13),
        name="down",
    )(me, act, norm, vec, cotangent, *pieces)


def down_grad_kernel(owner_ref, me_ref, act_ref, low_ref, keep_ref, send_ref, scratch):
    rows = keep_ref.shape[1]
    scratch[...] = dot(act_ref[...], low_ref[...], 0, 0).astype(LOW)
    mine = lax.rem(me_ref[0], 2) * rows
    keep_ref[0] = scratch[pl.ds(pl.multiple_of(mine, rows), rows)]
    send_ref[0] = scratch[pl.ds(pl.multiple_of(rows - mine, rows), rows)]


def down_grad_plain_kernel(act_ref, low_ref, grad_ref):
    grad_ref[...] = dot(act_ref[...], low_ref[...], 0, 0).astype(LOW)


def down_grad_plain_call(act, low):
    count, hidden = act.shape
    return pl.pallas_call(
        down_grad_plain_kernel,
        grid=(hidden // TILE,),
        in_specs=[pl.BlockSpec((count, TILE), lambda j: (0, j)), whole((count, D))],
        out_specs=pl.BlockSpec((TILE, D), lambda j: (j, 0)),
        out_shape=jax.ShapeDtypeStruct((hidden, D), LOW),
        compiler_params=params(),
        cost_estimate=cost(9),
        name="down_grad",
    )(act, low)


def down_grad_call(me, slots, rows, act, low):
    count, hidden = act.shape
    number = len(slots[0])
    pair = 2 * rows
    owners = (me // 2) ^ (jnp.array(slots[0], jnp.int32) // 2)
    part = pl.BlockSpec((1, rows, D), lambda j, *_: (j, 0, 0))
    half = jax.ShapeDtypeStruct((number, rows, D), LOW)
    return pl.pallas_call(
        down_grad_kernel,
        grid_spec=pltpu.PrefetchScalarGridSpec(
            num_scalar_prefetch=2,
            grid=(number,),
            in_specs=[
                pl.BlockSpec((count, pair), lambda j, owner, _: (0, owner[j])),
                whole((count, D)),
            ],
            out_specs=[part, part],
            scratch_shapes=[pltpu.VMEM((pair, D), LOW)],
        ),
        out_shape=[half, half],
        compiler_params=params(),
        cost_estimate=cost(number),
        name="down_grad",
    )(owners, me, act, low)


def up_grad_kernel(
    slots, me_ref, low_ref, wd_ref, slope_ref, hlt_ref, wu_ref, grad_ref,
    keep_ref, send_ref, bias_ref, hidden_ref, before_scr, grad_scr,
):
    step = pl.program_id(0)
    before_scr[...] = (dot(low_ref[...], wd_ref[...], 1, 1) * slope_ref[...].astype(WIDE)).astype(
        LOW
    )
    before = before_scr[...]
    grad_scr[...] = dot(hlt_ref[...], before, 1, 0).astype(LOW)
    unplace(
        keep_ref, send_ref, lambda part: grad_scr[part], slots, me_ref[0], 0, keep_ref.shape[1]
    )
    bias_ref[...] = jnp.broadcast_to(token_sum(before.astype(WIDE)), (8, TILE))
    back = dot(before, wu_ref[0], 1, 1)

    @pl.when(step == 0)
    def _():
        hidden_ref[...] = back + grad_ref[...]

    @pl.when(step != 0)
    def _():
        hidden_ref[...] += back


def up_grad_call(me, slots, tiles, low, down, slope, hlt, up, grad):
    count = slope.shape[0]
    first, steps = tiles[0], len(tiles)
    kept, rows = len(slots[0]), D // (len(slots[0]) + len(slots[1]))
    part = pl.BlockSpec((kept, rows, TILE), lambda j, *_: (0, j, 0))
    half = jax.ShapeDtypeStruct((kept, steps * rows, TILE), LOW)
    return pl.pallas_call(
        functools.partial(up_grad_kernel, slots),
        grid_spec=pltpu.PrefetchScalarGridSpec(
            num_scalar_prefetch=1,
            grid=(steps,),
            in_specs=[
                whole((count, D)),
                pl.BlockSpec((TILE, D), lambda j, *_: (j + first, 0)),
                pl.BlockSpec((count, TILE), lambda j, *_: (0, j + first)),
                whole((D, count)),
                pl.BlockSpec((1, D, TILE), lambda j, *_: (j + first, 0, 0)),
                whole((count, D)),
            ],
            out_specs=[
                part,
                part,
                pl.BlockSpec((8, TILE), lambda j, *_: (j, 0)),
                whole((count, D)),
            ],
            scratch_shapes=[pltpu.VMEM((count, TILE), LOW), pltpu.VMEM((D, TILE), LOW)],
        ),
        out_shape=[
            half,
            half,
            jax.ShapeDtypeStruct((8 * steps, TILE), WIDE),
            jax.ShapeDtypeStruct((count, D), WIDE),
        ],
        compiler_params=params(),
        cost_estimate=cost(6 * steps),
        name="up_grad",
    )(me, low, down, slope, hlt, up, grad)


def norm_back_kernel(
    slots, groups, me_ref, hidden_ref, norm_ref, inv_ref, vec_ref, wo_ref, ffn_ref, up_ref, *refs
):
    contexts, refs = refs[:groups], refs[groups:]
    grad_ref, keep_ref, send_ref, ctx_ref, low_scr, out_scr = refs
    count = hidden_ref.shape[0]
    step = 256
    gain = vec_ref[ATTN_GAIN : ATTN_GAIN + 1]
    wo = wo_ref[...]
    sums = 0
    for at in range(0, count, step):
        rows = pl.ds(at, step)
        hidden = hidden_ref[rows]
        norm = norm_ref[rows]
        scaled = hidden * gain
        grad = inv_ref[rows][:, 0:1] * (
            scaled - row_mean(scaled) - norm * row_mean(scaled * norm)
        )
        grad_ref[rows] = grad
        low = grad.astype(LOW)
        low_scr[rows] = low
        sums = sums + jnp.concatenate(
            [
                token_sum(hidden * norm),
                token_sum(hidden),
                token_sum(low.astype(WIDE)),
                jnp.zeros((5, D), WIDE),
            ],
            axis=0,
        )
        ctx_ref[rows] = dot(low, wo, 1, 1).astype(LOW)
    at = 0
    for ref in contexts:
        out_scr[at : at + ref.shape[0], :] = dot(ref[...], low_scr[...], 1, 0).astype(LOW)
        at += ref.shape[0]
    quads = D // QUAD
    rows = keep_ref.shape[1] // quads - EXTRA
    steps = up_ref.shape[0] // 8
    extra = [sums[2:3], sums[:2], ffn_ref[2:3], ffn_ref[:2]]
    extra += [up_ref[8 * at : 8 * at + 1] for at in range(steps)]
    extra.append(jnp.zeros((EXTRA - 6 - steps, D), WIDE))
    extra = jnp.concatenate(extra, axis=0)
    for quad in range(quads):
        cols = slice(quad * QUAD, quad * QUAD + QUAD)
        top = quad * (rows + EXTRA)
        unplace(keep_ref, send_ref, lambda part: out_scr[part, cols], slots, me_ref[0], top, rows)
        to_all(keep_ref, send_ref, slots, top + rows, extra[:, cols])


def norm_back_call(me, slots, hidden, norm, inv, vec, contexts, wo, ffn_sums, up_sums):
    count = hidden.shape[0]
    kept, rows = len(slots[0]), D // (len(slots[0]) + len(slots[1]))
    half = (kept, (rows + EXTRA) * (D // QUAD), QUAD)
    return pl.pallas_call(
        functools.partial(norm_back_kernel, slots, len(contexts)),
        grid_spec=pltpu.PrefetchScalarGridSpec(
            num_scalar_prefetch=1,
            grid=(1,),
            in_specs=[
                whole((count, D)),
                whole((count, D)),
                whole((count, 128)),
                whole((8, D)),
                whole((D, D)),
                whole((8, D)),
                whole(up_sums.shape),
            ]
            + [whole(context.shape) for context in contexts],
            out_specs=[whole((count, D)), whole(half), whole(half), whole((count, D))],
            scratch_shapes=[pltpu.VMEM((count, D), LOW), pltpu.VMEM((D, D), LOW)],
        ),
        out_shape=[
            jax.ShapeDtypeStruct((count, D), WIDE),
            jax.ShapeDtypeStruct(half, LOW),
            jax.ShapeDtypeStruct(half, LOW),
            jax.ShapeDtypeStruct((count, D), LOW),
        ],
        compiler_params=params(),
        cost_estimate=cost(12),
        name="norm_back",
    )(me, hidden, norm, inv, vec, wo, ffn_sums, up_sums, *contexts)


def input_grad_kernel(places, groups, grad_ref, *refs):
    weights, refs = refs[:groups], refs[groups:]
    total = grad_ref[...]
    for quad, (group, at) in enumerate(places):
        for matrix in range(3):
            total = total + dot(
                refs[3 * quad + matrix][...],
                weights[group][matrix, :, at * QUAD : at * QUAD + QUAD],
                1,
                1,
            )
    refs[-1][...] = total


def input_grad_call(pieces, places, weights, grad):
    count = grad.shape[0]
    tile = 512
    tokens = lambda width: pl.BlockSpec((tile, width), lambda i: (i, 0))
    values = [value for piece in pieces for value in piece]
    return pl.pallas_call(
        functools.partial(input_grad_kernel, places, len(weights)),
        grid=(count // tile,),
        in_specs=[tokens(D)]
        + [whole(weight.shape) for weight in weights]
        + [tokens(QUAD) for _ in values],
        out_specs=tokens(D),
        out_shape=jax.ShapeDtypeStruct((count, D), WIDE),
        compiler_params=params(),
        cost_estimate=cost(8),
        name="input_grad",
    )(grad, *weights, *values)


def pack_kernel(places, *refs):
    for ref, (row, col) in zip(refs, places):
        refs[-1][row : row + ref.shape[0], col : col + ref.shape[1]] = ref[...]


def pack(parts, width):
    if any(array.shape[0] % 16 for line in parts for array, _ in line):
        return jnp.concatenate(
            [
                jnp.concatenate([a[:, width * at : width * (at + 1)] for a, at in line], axis=1)
                for line in parts
            ]
        )
    places, specs, row = [], [], 0
    for line in parts:
        for at, (array, block) in enumerate(line):
            places.append((row, at * width))
            specs.append(pl.BlockSpec((array.shape[0], width), lambda i, block=block: (0, block)))
        row += line[0][0].shape[0]
    shape = (row, width * len(parts[0]))
    return pl.pallas_call(
        functools.partial(pack_kernel, places),
        grid=(1,),
        in_specs=specs,
        out_specs=pl.BlockSpec(shape, lambda i: (0, 0)),
        out_shape=jax.ShapeDtypeStruct(shape, LOW),
        compiler_params=params(),
        cost_estimate=cost(1),
        name="pack",
    )(*(array for line in parts for array, _ in line))


def swap(value, mask, count):
    return lax.ppermute(value, "fsdp", [(i, i ^ mask) for i in range(count)])


def after(value, *others):
    return lax.optimization_barrier((value,) + others)[0]


class Gather:
    def __init__(self, piece, count, half=False):
        self.unit = 1
        if half:
            rows = piece.shape[0] // 2
            piece = lax.dynamic_slice_in_dim(piece, lax.axis_index("rep") * rows, rows, 0)
            self.unit = 2
        self.held, self.count, self.order = piece[None], count, [0]
        self.hops = [count >> at for at in range(1, count.bit_length() - 1)]
        self.hops += ["rep"] * half + [1]

    def start(self, *others):
        held = after(self.held, *others) if others else self.held
        self.hop = self.hops.pop(0)
        if self.hop == "rep":
            self.other = lax.ppermute(held, "rep", [(0, 1), (1, 0)])
        else:
            self.other = swap(held, self.hop, self.count)

    def land(self, *others):
        other = after(self.other, *others) if others else self.other
        self.held = jnp.concatenate([self.held, other], axis=0)
        mask = 1 if self.hop == "rep" else self.hop * self.unit
        self.order = self.order + [at ^ mask for at in self.order]
        return self.held

    def until(self, hop):
        while self.hops[0] != hop:
            self.start()
            self.land()
        return self.held

    def pieces(self):
        return (self.held, self.other), (self.order, [at ^ self.unit for at in self.order])


def matrices(gather, number, rows, me):
    halves, slots = gather.pieces()
    if rows % 16 == 0:
        return halves, slots, rows
    count = 2 * halves[0].shape[0]
    parts = in_order(jnp.concatenate(halves)[:, : number * rows], slots, me)
    width = parts.shape[-1]
    parts = jnp.moveaxis(parts.reshape(count, number, rows, width), 1, 0)
    return (parts.reshape(1, number * count * rows, width),), ([0],), count * rows


def in_order(held, slots, me):
    count = held.shape[0]
    distance = jnp.array(slots[0] + slots[1], jnp.int32)
    chosen = (jnp.arange(count, dtype=jnp.int32) ^ me)[:, None] == distance[None]
    return jnp.einsum(
        "ij,jrc->irc", chosen.astype(LOW), held, preferred_element_type=WIDE
    ).astype(LOW)


def to_slots(parts, slots, me):
    count = parts.shape[0]
    bit = 1
    while bit < count:
        pairs = parts.reshape((count // (2 * bit), 2, bit) + parts.shape[1:])
        parts = jnp.where((me & bit) != 0, pairs[:, ::-1], pairs).reshape(parts.shape)
        bit *= 2
    return tuple(
        jnp.concatenate([parts[at : at + 1] for at in distances]) for distances in slots
    )


def sum_order(count):
    bits = count.bit_length() - 2
    order = [
        sum(2 << place for place in range(bits) if at >> (bits - 1 - place) & 1)
        for at in range(count // 2)
    ]
    return order, [at ^ 1 for at in order]


class Sum:
    def __init__(self, keep, send, count, half=False):
        self.terms, self.send, self.count = [(keep, ())], send, count
        self.slots = keep.shape[0]
        self.half, self.bit, self.total = half, 1, None

    def start(self, *others):
        send = after(self.send, *others) if others else self.send
        if self.half == "now" or self.bit == self.count:
            self.other = lax.ppermute(send, "rep", [(0, 1), (1, 0)])
        else:
            self.other = swap(send, self.bit, self.count)

    def added(self, *cuts):
        total = 0
        for array, before in self.terms:
            for each in (*before, *cuts):
                array = each(array)
            total = total + array.astype(WIDE)
        return total

    def cut(self, each):
        self.terms = [(array, (*before, each)) for array, before in self.terms]

    def land(self, *others):
        other = after(self.other, *others) if others else self.other
        if self.bit == self.count:
            if self.half:
                low = lax.axis_index("rep") == 0
                both = jnp.where(low, self.send, other), jnp.where(low, other, self.send)
                self.total = jnp.concatenate(both, axis=1)[0].astype(WIDE)
            else:
                self.total = (self.send.astype(WIDE) + other.astype(WIDE))[0]
            return self.total
        self.terms.append((other, ()))
        if self.half == "now":
            self.half = "done"
        else:
            self.bit *= 2
            if self.half is True:
                return self.halve()
        if self.bit == self.count:
            self.send = self.added().astype(LOW)
            return self.send
        middle = self.slots // 2
        self.send = self.added(lambda term: term[middle:]).astype(LOW)
        self.cut(lambda term: term[:middle])
        self.slots = middle
        return self.send

    def halve(self):
        mine = lax.axis_index("rep")
        _, rows, width = self.send.shape

        def pick(at):
            return lambda term: lax.dynamic_slice_in_dim(term, at * (rows // 2), rows // 2, 1)

        self.send = self.added(pick(1 - mine)).astype(LOW)
        self.cut(pick(mine))
        self.half = "now"
        return self.send

    def finish(self):
        while self.total is None:
            self.start()
            self.land()


def joined(sums):
    first = sums[0]
    whole = Sum(first.send, jnp.concatenate([item.send for item in sums], axis=1), first.count)
    whole.bit, whole.slots = first.bit, first.slots
    whole.terms = [(jnp.concatenate([item.added() for item in sums], axis=1), ())]
    return whole


def shards(
    inputs,
    block_kind,
    query_weight,
    query_bias,
    key_weight,
    value_weight,
    value_bias,
    out_weight,
    out_bias,
    attn_gain,
    attn_shift,
    up_weight,
    up_bias,
    down_weight,
    down_bias,
    ffn_gain,
    ffn_shift,
    cotangent,
):
    rows = query_weight.shape[0]
    count = D // rows
    hidden = up_weight.shape[1]
    steps = hidden // TILE
    vectors = (
        query_bias,
        value_bias,
        out_bias,
        attn_gain,
        attn_shift,
        down_bias,
        ffn_gain,
        ffn_shift,
    )
    down_rows = down_weight.shape[0]
    used = 8 * rows + up_bias.shape[0]
    spare = 16 * QUAD
    packed, at = 0, 0
    for value in vectors + (up_bias,):
        packed = packed + jnp.pad(value, (at, spare - at - value.shape[0]))
        at += value.shape[0]
    me = lax.axis_index("fsdp").astype(jnp.int32)
    own_rows = rows % 16 == 0
    mine = me.reshape(1)
    none = jnp.zeros((1,), jnp.int32)
    me_or_none = mine if own_rows else none
    qkv_weights = (query_weight, key_weight, value_weight)

    first = Gather(
        pack([[(w, 0)] for w in qkv_weights] + [[(packed.reshape(16, QUAD), 0)]], QUAD), count
    )
    first.start()
    at = first.land()
    rest = Gather(pack([[(w, 1), (w, 2)] for w in qkv_weights], QUAD), count)
    rest.start(at)
    at = rest.land(first.until(2))
    third = Gather(down_weight, count, half=True)
    first.start()
    rest.until(2)
    third.start(at)
    at = third.land(first.land(rest.held))
    second = Gather(
        pack([[(out_weight, 0)]] + [[(up_weight, at)] for at in range(steps)], TILE), count
    )
    first.start()
    rest.start()
    second.start(at)
    while third.hops[0] > 4:
        third.start()
        third.land()
    third.start()
    inputs_t = inputs.T

    halves, slots = first.pieces()
    columns = -(-used // QUAD)
    whole_packed = in_order(
        jnp.concatenate([half[:, 3 * rows : 3 * rows + columns] for half in halves]), slots, me
    ).reshape(count, columns * QUAD)
    vec = (
        jnp.moveaxis(whole_packed[:, : 8 * rows].reshape(count, 8, rows), 1, 0)
        .reshape(8, D)
        .astype(WIDE)
    )
    all_up_bias = whole_packed[:, 8 * rows : used].reshape(1, hidden).astype(WIDE)

    places = [(0, 0), (1, 0), (1, 1)]
    at = rest.land()
    at = third.land(at)
    at = second.land(at)
    rest.start()
    third.start()
    while second.hops[0] > 4:
        second.start()
        at = second.land()
    second.start()
    heads = [
        attend(
            block_kind, me_or_none, [0], after(inputs, at), matrices(first, 3, rows, me), vec
        )
    ]
    at = third.land(heads[0][3])
    third.start()
    at = second.land(at)
    second.start()
    heads.append(
        attend(
            block_kind, me_or_none, [1, 2], after(inputs, at), matrices(rest, 3, rows, me), vec
        )
    )
    at = second.land(heads[1][3])
    second.start()
    contexts = [group[3] for group in heads]
    contexts_t = [group[4] for group in heads]
    third.land(at)
    third.start()
    act, slope, norm, first_inv, hlt, wo, up = up_call(
        me_or_none, contexts, inputs, matrices(second, 1 + steps, rows, me), vec, all_up_bias
    )
    side = 2 * me + lax.axis_index("rep").astype(jnp.int32)
    pieces = matrices(third, 1, down_rows // 2, side)
    layer_out, grad, low, ffn_sums, down = down_call(
        side.reshape(1) if down_rows % 32 == 0 else none, act, pieces, norm, vec, cotangent
    )

    order = sum_order(count)
    quads = D // QUAD

    def halves_of(keep, send, k, groups=1):
        if own_rows:
            return keep, send
        width = keep.shape[-1]
        tall = keep.shape[1] // groups
        everything = []
        for group in jnp.split(keep[0], groups):
            parts = jnp.moveaxis(group[: k * D].reshape(k, count, rows, width), 0, 1)
            everything.append(parts.reshape(count, k * rows, width))
            everything.append(jnp.broadcast_to(group[None, k * D :], (count, tall - k * D, width)))
        return to_slots(jnp.concatenate(everything, axis=1), order, me)

    kernel_order = order if own_rows else ([0], [])
    if 2 * down_rows % 128 == 0:
        middle = count // 4
        near, far = ([part[at] for part in order] for at in (slice(middle), slice(middle, None)))
        far_keep, far_send = down_grad_call(mine, far, down_rows, act, low)
        far_other = swap(far_send, 1, count)
        near_keep, near_send = down_grad_call(mine, near, down_rows, act, after(low, far_keep))
        sum_down = Sum(near_keep, None, count)
        sum_down.bit, sum_down.slots = 2, middle
        far_other = after(far_other, near_keep)
        sum_down.send = (far_keep.astype(WIDE) + far_other.astype(WIDE)).astype(LOW)
        at = sum_down.send
        sum_down.start()
        sum_down.terms.append((swap(near_send, 1, count), ()))
    else:
        parts = down_grad_plain_call(act, low).reshape(count, down_rows, D)
        sum_down = Sum(*to_slots(parts, order, me), count)
        sum_down.start()
        at = sum_down.land()
        sum_down.start()

    keep, send, up_sums, grad_hidden = up_grad_call(
        me_or_none, kernel_order, list(range(steps)), low, down, slope, hlt, up, after(grad, at)
    )
    sum_up = Sum(*halves_of(keep, send, steps), count, half=True)
    sum_up.start()
    at = sum_down.land(grad_hidden)
    sum_down.start()
    grad_attn, keep, send, grad_ctx = norm_back_call(
        me_or_none, kernel_order, after(grad_hidden, at), norm, first_inv, vec, contexts_t, wo,
        ffn_sums, up_sums,
    )
    sum_out = Sum(*halves_of(keep, send, 1, quads), count)
    sum_out.start()
    at = sum_up.land(grad_attn)
    sum_up.start()

    def back(quad, *others):
        group, at = places[quad]
        q, k, v, ctx, _, raised, inv, _ = heads[group]
        *part, keep, send = attend_back(
            me_or_none, kernel_order, quad, at, inputs_t, after(grad_ctx, *others), ctx, inv, q, k, v,
            raised,
        )
        return part, Sum(*halves_of(keep, send, 3), count)

    part_0, sum_0 = back(0, at)
    sum_0.start()
    at = sum_down.land(part_0[0])
    sum_down.start()
    at = sum_out.land(at)
    part_1, sum_1 = back(1, at)
    sum_1.start()
    at = sum_0.land(part_1[0])
    sum_0 = joined([sum_out, sum_0])
    sum_0.start()
    at = sum_down.land(at)
    if sum_down.total is None:
        sum_down.start()
    at = sum_up.land(at)
    sum_up.start()
    part_2, sum_2 = back(2, at, sum_0.send)
    sum_2.start()
    at = sum_1.land(part_2[0])
    sum_1.start()
    at = sum_up.land(at)
    sum_up.start()
    at = sum_0.land(at)
    at = sum_2.land(at)
    sum_2.start()
    weights = [group[7] for group in heads]
    input_grad = input_grad_call([part_0, part_1, part_2], places, weights, after(grad_attn, at))
    at = sum_1.land(input_grad)
    sum_1 = joined([sum_0, sum_1])
    sum_1.start()
    at = sum_2.land(at, sum_1.send)
    sum_2.start()
    at = sum_up.land(at)
    for item in (sum_1, sum_2, sum_up, sum_down):
        if item.total is None and item is sum_up:
            item.start()
    while sum_2.total is None:
        for item in (sum_1, sum_2, sum_up):
            if item.total is None:
                at = item.land(at)
            if item.total is None:
                item.start()
    for item in (sum_1, sum_up, sum_down):
        if item.total is None and item is not sum_down:
            item.land()
        item.finish()
    tall = 3 * rows + EXTRA
    above, last = sum_1.total[-2 * tall :], sum_2.total
    grad_qkv = jnp.concatenate([above[:tall], above[tall:], last], axis=1)
    grad_out = jnp.concatenate(jnp.split(sum_1.total[: -2 * tall], quads), axis=1)
    of_mine = lambda value, size: lax.dynamic_slice_in_dim(value, me * size, size, value.ndim - 1)
    own = of_mine(
        jnp.concatenate([grad_qkv[3 * rows : 3 * rows + 2], grad_out[rows : rows + 6]]), rows
    )
    grad_up_bias = of_mine(grad_out[rows + 6 : rows + 6 + steps].reshape(-1), up_bias.shape[0])
    grad_up = sum_up.total
    return (
        layer_out,
        input_grad,
        grad_qkv[:rows],
        own[QUERY_BIAS],
        grad_qkv[rows : 2 * rows],
        grad_qkv[2 * rows : 3 * rows],
        own[VALUE_BIAS],
        grad_out[:rows],
        own[OUT_BIAS],
        own[ATTN_GAIN],
        own[ATTN_SHIFT],
        jnp.concatenate([grad_up[rows * i : rows * (i + 1)] for i in range(steps)], axis=1),
        grad_up_bias,
        sum_down.total,
        own[DOWN_BIAS],
        own[FFN_GAIN],
        own[FFN_SHIFT],
    )


def solution(mesh):
    tokens = P(("rep", "fsdp"), None)
    matrix = P("fsdp", None)
    vector = P("fsdp")
    params_placed = (
        matrix,
        vector,
        matrix,
        matrix,
        vector,
        matrix,
        vector,
        vector,
        vector,
        matrix,
        vector,
        matrix,
        vector,
        vector,
        vector,
    )
    return jax.shard_map(
        shards,
        mesh=mesh,
        in_specs=(tokens, P(("rep", "fsdp")), *params_placed, tokens),
        out_specs=(tokens, tokens, *params_placed),
        check_vma=False,
    )
```

```python
import functools

import jax
import jax.numpy as jnp
from jax import lax
from jax.experimental import pallas as pl
from jax.experimental.pallas import tpu as pltpu
from jax.sharding import PartitionSpec as P

D = 768
H = 12
HD = 64
LONG = 512
SHORT = 128
QUAD = 256
PAIR = 128
TILE = 768

EPSILON = 1e-05
BLOCKED = -1e30
LOW = jnp.bfloat16
WIDE = jnp.float32
ROOM = 56 << 20
EXTRA = 16

QUERY_BIAS, VALUE_BIAS, OUT_BIAS, ATTN_GAIN, ATTN_SHIFT, DOWN_BIAS, FFN_GAIN, FFN_SHIFT = range(8)


def dot(left, right, left_dim, right_dim):
    return lax.dot_general(
        left, right, (((left_dim,), (right_dim,)), ((), ())), preferred_element_type=WIDE
    )


def row_mean(value):
    return jnp.mean(value, axis=-1, keepdims=True)


def token_sum(value):
    return jnp.sum(value, axis=0, keepdims=True)


def whole(shape):
    zeros = (0,) * len(shape)
    return pl.BlockSpec(shape, lambda *_: zeros, pipeline_mode=pl.Buffered(1))


def place(target, sources, slots, me):
    rows = sources[0].shape[1]
    for source, distances in zip(sources, slots):
        for at, distance in enumerate(distances):
            start = pl.multiple_of((me ^ distance) * rows, rows)
            target[pl.ds(start, rows), :] = source[at]


def params():
    return pltpu.CompilerParams(vmem_limit_bytes=ROOM)


def cost(microseconds):
    return pl.CostEstimate(
        flops=int(microseconds * 1.1e9), bytes_accessed=1 << 20, transcendentals=0
    )


def unplace(keep, send, source, slots, me, top, rows):
    for target, distances in zip((keep, send), slots):
        for at, distance in enumerate(distances):
            start = pl.multiple_of((me ^ distance) * rows, rows)
            target[at, top : top + rows, :] = source(pl.ds(start, rows)).astype(LOW)


def to_all(keep, send, slots, top, rows):
    low = rows.astype(LOW)
    for target, distances in zip((keep, send), slots):
        for at in range(len(distances)):
            target[at, top : top + EXTRA, :] = low


def half_masks():
    lane = lax.broadcasted_iota(jnp.int32, (1, PAIR), 1)
    return [jnp.where(lane // HD == half, 1.0, 0.0) for half in range(2)]


def attend_kernel(slots, kind_ref, me_ref, x_ref, vec_ref, *refs):
    pieces = len(slots)
    sources, refs = refs[: 3 * pieces], refs[3 * pieces :]
    q_ref, k_ref, v_ref, ctx_ref, ctxt_ref, raised_ref, inv_ref, weight_ref = refs

    @pl.when(pl.program_id(1) == 0)
    def _():
        for at in range(3):
            place(weight_ref.at[at], sources[at * pieces : (at + 1) * pieces], slots, me_ref[0])

    x = x_ref[...]
    q_ref[...] = (dot(x, weight_ref[0], 1, 0) + vec_ref[QUERY_BIAS : QUERY_BIAS + 1]).astype(LOW)
    k_ref[...] = dot(x, weight_ref[1], 1, 0).astype(LOW)
    v_ref[...] = (dot(x, weight_ref[2], 1, 0) + vec_ref[VALUE_BIAS : VALUE_BIAS + 1]).astype(LOW)
    part = lax.broadcasted_iota(jnp.int32, (LONG, PAIR), 0) // SHORT
    lane = lax.broadcasted_iota(jnp.int32, (LONG, PAIR), 1)
    blocked = jnp.where(kind_ref[pl.program_id(1)] == 1, 0.0, BLOCKED)
    query_part = jnp.where((lane < LONG // SHORT) & (part != lane), blocked, 0.0).astype(LOW)
    key_part = jnp.where(part == lane, 1.0, 0.0).astype(LOW)
    halves = half_masks()
    for pair in range(QUAD // PAIR):
        cols = pl.ds(pair * PAIR, PAIR)
        q2 = q_ref[:, cols].astype(WIDE) * HD ** (-0.5)
        keys = jnp.concatenate([k_ref[:, cols], key_part], axis=1)
        v2t = v_ref[:, cols].T
        contexts, inverses = [], []
        for half in range(2):
            queries = jnp.concatenate([(q2 * halves[half]).astype(LOW), query_part], axis=1)
            scores = dot(keys, queries, 1, 1)
            peak = jnp.max(scores, axis=0, keepdims=True)
            raised = jnp.exp(scores - peak).astype(LOW)
            raised_ref[0, pair * 2 + half] = raised
            left = jnp.concatenate(
                [v2t[HD * half : HD * half + HD], jnp.ones((16, LONG), LOW)], axis=0
            )
            mixed = dot(left, raised, 1, 0)
            inverse = 1.0 / mixed[HD : HD + 1]
            contexts.append(mixed[:HD] * inverse)
            inverses.append(jnp.broadcast_to(inverse, (HD, LONG)))
        context = jnp.concatenate(contexts, axis=0)
        ctxt_ref[pair * PAIR : pair * PAIR + PAIR, :] = context.astype(LOW)
        ctx_ref[:, cols] = context.T.astype(LOW)
        inv_ref[:, cols] = jnp.concatenate(inverses, axis=0).T


def attend(kind, me, quads, x, weights, vec):
    pieces, slots, rows = weights
    count = x.shape[0]
    blocks, number, low = count // LONG, len(quads), quads[0]
    tokens = pl.BlockSpec((LONG, QUAD), lambda j, b, *_: (b, j))
    act = jax.ShapeDtypeStruct((count, number * QUAD), LOW)
    return pl.pallas_call(
        functools.partial(attend_kernel, slots),
        grid_spec=pltpu.PrefetchScalarGridSpec(
            num_scalar_prefetch=2,
            grid=(number, blocks),
            in_specs=[
                pl.BlockSpec((LONG, D), lambda j, b, *_: (b, 0)),
                pl.BlockSpec((8, QUAD), lambda j, b, *_: (0, j + low)),
            ]
            + [
                pl.BlockSpec((piece.shape[0], rows, QUAD), lambda j, b, *_, at=at: (0, at, j))
                for at in range(3)
                for piece in pieces
            ],
            out_specs=[
                tokens,
                tokens,
                tokens,
                tokens,
                pl.BlockSpec((QUAD, LONG), lambda j, b, *_: (j, b)),
                pl.BlockSpec((1, QUAD // HD, LONG, LONG), lambda j, b, *_: (b, j, 0, 0)),
                tokens,
                pl.BlockSpec((3, D, QUAD), lambda j, b, *_: (0, 0, j)),
            ],
        ),
        out_shape=[
            act,
            act,
            act,
            act,
            jax.ShapeDtypeStruct((number * QUAD, count), LOW),
            jax.ShapeDtypeStruct((blocks, number * QUAD // HD, LONG, LONG), LOW),
            jax.ShapeDtypeStruct((count, number * QUAD), WIDE),
            jax.ShapeDtypeStruct((3, D, number * QUAD), LOW),
        ],
        compiler_params=params(),
        cost_estimate=cost(0.1),
        name="attend",
    )(kind, me, x, vec, *(list(pieces) * 3))


def attend_back_kernel(
    slots,
    me_ref,
    xt_ref,
    d_ref,
    ctx_ref,
    inv_ref,
    q_ref,
    k_ref,
    v_ref,
    raised_ref,
    dq_ref,
    dk_ref,
    dv_ref,
    keep_ref,
    send_ref,
    totals,
    biases,
):
    block = pl.program_id(0)
    halves = half_masks()
    minus = jnp.full((LONG, PAIR), -1.0, LOW)
    work = []
    for pair in range(QUAD // PAIR):
        cols = pl.ds(pair * PAIR, PAIR)
        d2 = d_ref[:, cols].astype(WIDE) * inv_ref[:, cols] * HD ** (-0.5)
        along = d2 * ctx_ref[:, cols].astype(WIDE)
        q2 = q_ref[:, cols].astype(WIDE)
        values = jnp.concatenate([v_ref[:, cols], minus], axis=1)
        for half in range(2):
            dm = (d2 * halves[half]).astype(LOW)
            am = (along * halves[half]).astype(LOW)
            qm = (q2 * halves[half]).astype(LOW)
            dp = dot(values, jnp.concatenate([dm, am], axis=1), 1, 1)
            work.append((pair, half, dm, qm, dp))
    k2ts = [k_ref[:, pl.ds(pair * PAIR, PAIR)].T for pair in range(QUAD // PAIR)]
    done = []
    for pair, half, dm, qm, dp in work:
        raised = raised_ref[0, pair * 2 + half]
        ds = (raised.astype(WIDE) * dp).astype(LOW)
        done.append((pair, half, raised, ds, dm, qm))
    for pair in range(QUAD // PAIR):
        cols = pl.ds(pair * PAIR, PAIR)
        dqt, dk, dv = [], 0, 0
        for p, half, raised, ds, dm, qm in done:
            if p == pair:
                dqt.append(dot(k2ts[pair][HD * half : HD * half + HD], ds, 1, 0))
        both = [item for item in done if item[0] == pair]
        wide = lambda at, axis: jnp.concatenate([item[at] for item in both], axis=axis)
        dv = dot(wide(2, 1), wide(4, 0), 1, 0)
        dk = dot(wide(3, 1), wide(5, 0), 1, 0)
        dv_ref[:, cols] = (dv * HD**0.5).astype(LOW)
        dk_ref[:, cols] = dk.astype(LOW)
        dq_ref[:, cols] = jnp.concatenate(dqt, axis=0).T.astype(LOW)
    xt = xt_ref[...]
    for at, ref in enumerate((dq_ref, dk_ref, dv_ref)):
        grad = dot(xt, ref[...], 1, 0)

        @pl.when(block == 0)
        def _(grad=grad, at=at):
            totals[at] = grad

        @pl.when(block != 0)
        def _(grad=grad, at=at):
            totals[at] += grad

    sums = jnp.concatenate(
        [
            token_sum(dq_ref[...].astype(WIDE)),
            token_sum(dv_ref[...].astype(WIDE)),
            jnp.zeros((EXTRA - 2, QUAD), WIDE),
        ],
        axis=0,
    )

    @pl.when(block == 0)
    def _():
        biases[...] = sums

    @pl.when(block != 0)
    def _():
        biases[...] += sums

    @pl.when(block == pl.num_programs(0) - 1)
    def _():
        rows = (keep_ref.shape[1] - EXTRA) // 3
        for at in range(3):
            unplace(
                keep_ref, send_ref, lambda part, at=at: totals[at, part], slots, me_ref[0], at * rows, rows
            )
        to_all(keep_ref, send_ref, slots, 3 * rows, biases[...])


def attend_back(me, slots, quad, at, xt, d, ctx, inv, q, k, v, raised):
    count = q.shape[0]
    tokens = pl.BlockSpec((LONG, QUAD), lambda b, *_: (b, at))
    grads = pl.BlockSpec((LONG, QUAD), lambda b, *_: (b, 0))
    act = jax.ShapeDtypeStruct((count, QUAD), LOW)
    kept, rows = len(slots[0]), D // (len(slots[0]) + len(slots[1]))
    half = (kept, 3 * rows + EXTRA, QUAD)
    return pl.pallas_call(
        functools.partial(attend_back_kernel, slots),
        grid_spec=pltpu.PrefetchScalarGridSpec(
            num_scalar_prefetch=1,
            grid=(count // LONG,),
            in_specs=[
                pl.BlockSpec((D, LONG), lambda b, *_: (0, b)),
                pl.BlockSpec((LONG, QUAD), lambda b, *_: (b, quad)),
            ]
            + [tokens] * 5
            + [pl.BlockSpec((1, QUAD // HD, LONG, LONG), lambda b, *_: (b, at, 0, 0))],
            out_specs=[grads, grads, grads, whole(half), whole(half)],
            scratch_shapes=[pltpu.VMEM((3, D, QUAD), WIDE), pltpu.VMEM((EXTRA, QUAD), WIDE)],
        ),
        out_shape=[act, act, act, jax.ShapeDtypeStruct(half, LOW), jax.ShapeDtypeStruct(half, LOW)],
        compiler_params=params(),
        cost_estimate=cost(2),
        name="attend_back",
    )(me, xt, d, ctx, inv, q, k, v, raised)


def up_kernel(slots, groups, me_ref, x_ref, vec_ref, bu_ref, *refs):
    contexts, refs = refs[:groups], refs[groups:]
    pieces = len(slots)
    outs, ups, refs = refs[:pieces], refs[pieces : 2 * pieces], refs[2 * pieces :]
    act_ref, slope_ref, norm_ref, inv_ref, hlt_ref, wo_ref, wu_ref, hl_ref = refs
    count = x_ref.shape[0]
    step = 256
    place(wu_ref.at[0], ups, slots, me_ref[0])

    @pl.when(pl.program_id(0) == 0)
    def _():
        bias = vec_ref[OUT_BIAS : OUT_BIAS + 1]
        gain = vec_ref[ATTN_GAIN : ATTN_GAIN + 1]
        shift = vec_ref[ATTN_SHIFT : ATTN_SHIFT + 1]
        place(wo_ref, outs, slots, me_ref[0])
        wo = wo_ref[...]
        for at in range(0, count, step):
            rows = pl.ds(at, step)
            context = jnp.concatenate([ref[rows] for ref in contexts], axis=1)
            total = x_ref[rows].astype(WIDE) + dot(context, wo, 1, 0) + bias
            centered = total - row_mean(total)
            inverse = lax.rsqrt(row_mean(centered * centered) + EPSILON)
            norm = centered * inverse
            norm_ref[rows] = norm
            inv_ref[rows] = jnp.broadcast_to(inverse, (step, 128))
            hidden = (norm * gain + shift).astype(LOW)
            hl_ref[rows] = hidden
            hlt_ref[:, rows] = hidden.T

    bias = bu_ref[...]
    weight = wu_ref[0]
    for at in range(0, count, step):
        rows = pl.ds(at, step)
        before = dot(hl_ref[rows], weight, 1, 0) + bias
        half = 0.5 * (1.0 + lax.erf(before * 0.7071067811865476))
        act_ref[rows] = (before * half).astype(LOW)
        slope_ref[rows] = (
            half + before * jnp.exp(-0.5 * before * before) * 0.3989422804014327
        ).astype(LOW)


def up_call(me, contexts, x, second, vec, up_bias):
    pieces, slots, rows = second
    count = x.shape[0]
    hidden = up_bias.shape[1]
    steps = hidden // TILE
    cols = lambda r: pl.BlockSpec((r, TILE), lambda j, *_: (0, j))
    return pl.pallas_call(
        functools.partial(up_kernel, slots, len(contexts)),
        grid_spec=pltpu.PrefetchScalarGridSpec(
            num_scalar_prefetch=1,
            grid=(steps,),
            in_specs=[whole((count, D)), whole((8, D)), cols(1)]
            + [whole(context.shape) for context in contexts]
            + [
                pl.BlockSpec(
                    (piece.shape[0], rows, D),
                    lambda j, *_: (0, 0, 0),
                    pipeline_mode=pl.Buffered(1),
                )
                for piece in pieces
            ]
            + [
                pl.BlockSpec((piece.shape[0], rows, D), lambda j, *_: (0, 1 + j, 0))
                for piece in pieces
            ],
            out_specs=[
                cols(count),
                cols(count),
                whole((count, D)),
                whole((count, 128)),
                whole((D, count)),
                whole((D, D)),
                pl.BlockSpec((1, D, TILE), lambda j, *_: (j, 0, 0)),
            ],
            scratch_shapes=[pltpu.VMEM((count, D), LOW)],
        ),
        out_shape=[
            jax.ShapeDtypeStruct((count, hidden), LOW),
            jax.ShapeDtypeStruct((count, hidden), LOW),
            jax.ShapeDtypeStruct((count, D), WIDE),
            jax.ShapeDtypeStruct((count, 128), WIDE),
            jax.ShapeDtypeStruct((D, count), LOW),
            jax.ShapeDtypeStruct((D, D), LOW),
            jax.ShapeDtypeStruct((steps, D, TILE), LOW),
        ],
        compiler_params=params(),
        cost_estimate=cost(0.1),
        name="up",
    )(me, x, vec, up_bias, *contexts, *pieces, *pieces)


def down_kernel(slots, me_ref, act_ref, norm_ref, vec_ref, cot_ref, *refs):
    sources = refs[: len(slots)]
    out_ref, grad_ref, low_ref, sums_ref, wd_ref = refs[len(slots) :]

    @pl.when(pl.program_id(0) == 0)
    def _():
        place(wd_ref, sources, slots, me_ref[0])

    row = lambda at: vec_ref[at : at + 1]
    total = (
        norm_ref[...] * row(ATTN_GAIN)
        + row(ATTN_SHIFT)
        + (dot(act_ref[...], wd_ref[...], 1, 0) + row(DOWN_BIAS))
    )
    centered = total - row_mean(total)
    inverse = lax.rsqrt(row_mean(centered * centered) + EPSILON)
    norm = centered * inverse
    out_ref[...] = (norm * row(FFN_GAIN) + row(FFN_SHIFT)).astype(LOW)
    grad_out = cot_ref[...].astype(WIDE)
    scaled = grad_out * row(FFN_GAIN)
    grad = inverse * (scaled - row_mean(scaled) - norm * row_mean(scaled * norm))
    grad_ref[...] = grad
    low = grad.astype(LOW)
    low_ref[...] = low
    sums = jnp.concatenate(
        [
            token_sum(grad_out * norm),
            token_sum(grad_out),
            token_sum(low.astype(WIDE)),
            jnp.zeros((5, D), WIDE),
        ],
        axis=0,
    )

    @pl.when(pl.program_id(0) == 0)
    def _():
        sums_ref[...] = sums

    @pl.when(pl.program_id(0) != 0)
    def _():
        sums_ref[...] += sums


def down_call(me, act, third, norm, vec, cotangent):
    pieces, slots, _ = third
    count, hidden = act.shape
    tile = 256
    rows = lambda c: pl.BlockSpec((tile, c), lambda i, *_: (i, 0))
    return pl.pallas_call(
        functools.partial(down_kernel, slots),
        grid_spec=pltpu.PrefetchScalarGridSpec(
            num_scalar_prefetch=1,
            grid=(count // tile,),
            in_specs=[rows(hidden), rows(D), whole((8, D)), rows(D)]
            + [whole(piece.shape) for piece in pieces],
            out_specs=[rows(D), rows(D), rows(D), whole((8, D)), whole((hidden, D))],
        ),
        out_shape=[
            jax.ShapeDtypeStruct((count, D), LOW),
            jax.ShapeDtypeStruct((count, D), WIDE),
            jax.ShapeDtypeStruct((count, D), LOW),
            jax.ShapeDtypeStruct((8, D), WIDE),
            jax.ShapeDtypeStruct((hidden, D), LOW),
        ],
        compiler_params=params(),
        cost_estimate=cost(13),
        name="down",
    )(me, act, norm, vec, cotangent, *pieces)


def down_grad_kernel(owner_ref, me_ref, act_ref, low_ref, keep_ref, send_ref, scratch):
    rows = keep_ref.shape[1]
    scratch[...] = dot(act_ref[...], low_ref[...], 0, 0).astype(LOW)
    mine = lax.rem(me_ref[0], 2) * rows
    keep_ref[0] = scratch[pl.ds(pl.multiple_of(mine, rows), rows)]
    send_ref[0] = scratch[pl.ds(pl.multiple_of(rows - mine, rows), rows)]


def down_grad_plain_kernel(act_ref, low_ref, grad_ref):
    grad_ref[...] = dot(act_ref[...], low_ref[...], 0, 0).astype(LOW)


def down_grad_plain_call(act, low):
    count, hidden = act.shape
    return pl.pallas_call(
        down_grad_plain_kernel,
        grid=(hidden // TILE,),
        in_specs=[pl.BlockSpec((count, TILE), lambda j: (0, j)), whole((count, D))],
        out_specs=pl.BlockSpec((TILE, D), lambda j: (j, 0)),
        out_shape=jax.ShapeDtypeStruct((hidden, D), LOW),
        compiler_params=params(),
        cost_estimate=cost(9),
        name="down_grad",
    )(act, low)


def down_grad_call(me, slots, rows, act, low):
    count, hidden = act.shape
    number = len(slots[0])
    pair = 2 * rows
    owners = (me // 2) ^ (jnp.array(slots[0], jnp.int32) // 2)
    part = pl.BlockSpec((1, rows, D), lambda j, *_: (j, 0, 0))
    half = jax.ShapeDtypeStruct((number, rows, D), LOW)
    return pl.pallas_call(
        down_grad_kernel,
        grid_spec=pltpu.PrefetchScalarGridSpec(
            num_scalar_prefetch=2,
            grid=(number,),
            in_specs=[
                pl.BlockSpec((count, pair), lambda j, owner, _: (0, owner[j])),
                whole((count, D)),
            ],
            out_specs=[part, part],
            scratch_shapes=[pltpu.VMEM((pair, D), LOW)],
        ),
        out_shape=[half, half],
        compiler_params=params(),
        cost_estimate=cost(number),
        name="down_grad",
    )(owners, me, act, low)


def up_grad_kernel(
    slots, me_ref, low_ref, wd_ref, slope_ref, hlt_ref, wu_ref, grad_ref,
    keep_ref, send_ref, bias_ref, hidden_ref, before_scr, grad_scr,
):
    step = pl.program_id(0)
    before_scr[...] = (dot(low_ref[...], wd_ref[...], 1, 1) * slope_ref[...].astype(WIDE)).astype(
        LOW
    )
    before = before_scr[...]
    grad_scr[...] = dot(hlt_ref[...], before, 1, 0).astype(LOW)
    unplace(
        keep_ref, send_ref, lambda part: grad_scr[part], slots, me_ref[0], 0, keep_ref.shape[1]
    )
    bias_ref[...] = jnp.broadcast_to(token_sum(before.astype(WIDE)), (8, TILE))
    back = dot(before, wu_ref[0], 1, 1)

    @pl.when(step == 0)
    def _():
        hidden_ref[...] = back + grad_ref[...]

    @pl.when(step != 0)
    def _():
        hidden_ref[...] += back


def up_grad_call(me, slots, tiles, low, down, slope, hlt, up, grad):
    count = slope.shape[0]
    first, steps = tiles[0], len(tiles)
    kept, rows = len(slots[0]), D // (len(slots[0]) + len(slots[1]))
    part = pl.BlockSpec((kept, rows, TILE), lambda j, *_: (0, j, 0))
    half = jax.ShapeDtypeStruct((kept, steps * rows, TILE), LOW)
    return pl.pallas_call(
        functools.partial(up_grad_kernel, slots),
        grid_spec=pltpu.PrefetchScalarGridSpec(
            num_scalar_prefetch=1,
            grid=(steps,),
            in_specs=[
                whole((count, D)),
                pl.BlockSpec((TILE, D), lambda j, *_: (j + first, 0)),
                pl.BlockSpec((count, TILE), lambda j, *_: (0, j + first)),
                whole((D, count)),
                pl.BlockSpec((1, D, TILE), lambda j, *_: (j + first, 0, 0)),
                whole((count, D)),
            ],
            out_specs=[
                part,
                part,
                pl.BlockSpec((8, TILE), lambda j, *_: (j, 0)),
                whole((count, D)),
            ],
            scratch_shapes=[pltpu.VMEM((count, TILE), LOW), pltpu.VMEM((D, TILE), LOW)],
        ),
        out_shape=[
            half,
            half,
            jax.ShapeDtypeStruct((8 * steps, TILE), WIDE),
            jax.ShapeDtypeStruct((count, D), WIDE),
        ],
        compiler_params=params(),
        cost_estimate=cost(6 * steps),
        name="up_grad",
    )(me, low, down, slope, hlt, up, grad)


def norm_back_kernel(
    slots, groups, me_ref, hidden_ref, norm_ref, inv_ref, vec_ref, wo_ref, ffn_ref, up_ref, *refs
):
    contexts, refs = refs[:groups], refs[groups:]
    grad_ref, keep_ref, send_ref, ctx_ref, low_scr, out_scr = refs
    count = hidden_ref.shape[0]
    step = 256
    gain = vec_ref[ATTN_GAIN : ATTN_GAIN + 1]
    wo = wo_ref[...]
    sums = 0
    for at in range(0, count, step):
        rows = pl.ds(at, step)
        hidden = hidden_ref[rows]
        norm = norm_ref[rows]
        scaled = hidden * gain
        grad = inv_ref[rows][:, 0:1] * (
            scaled - row_mean(scaled) - norm * row_mean(scaled * norm)
        )
        grad_ref[rows] = grad
        low = grad.astype(LOW)
        low_scr[rows] = low
        sums = sums + jnp.concatenate(
            [
                token_sum(hidden * norm),
                token_sum(hidden),
                token_sum(low.astype(WIDE)),
                jnp.zeros((5, D), WIDE),
            ],
            axis=0,
        )
        ctx_ref[rows] = dot(low, wo, 1, 1).astype(LOW)
    at = 0
    for ref in contexts:
        out_scr[at : at + ref.shape[0], :] = dot(ref[...], low_scr[...], 1, 0).astype(LOW)
        at += ref.shape[0]
    quads = D // QUAD
    rows = keep_ref.shape[1] // quads - EXTRA
    steps = up_ref.shape[0] // 8
    extra = [sums[2:3], sums[:2], ffn_ref[2:3], ffn_ref[:2]]
    extra += [up_ref[8 * at : 8 * at + 1] for at in range(steps)]
    extra.append(jnp.zeros((EXTRA - 6 - steps, D), WIDE))
    extra = jnp.concatenate(extra, axis=0)
    for quad in range(quads):
        cols = slice(quad * QUAD, quad * QUAD + QUAD)
        top = quad * (rows + EXTRA)
        unplace(keep_ref, send_ref, lambda part: out_scr[part, cols], slots, me_ref[0], top, rows)
        to_all(keep_ref, send_ref, slots, top + rows, extra[:, cols])


def norm_back_call(me, slots, hidden, norm, inv, vec, contexts, wo, ffn_sums, up_sums):
    count = hidden.shape[0]
    kept, rows = len(slots[0]), D // (len(slots[0]) + len(slots[1]))
    half = (kept, (rows + EXTRA) * (D // QUAD), QUAD)
    return pl.pallas_call(
        functools.partial(norm_back_kernel, slots, len(contexts)),
        grid_spec=pltpu.PrefetchScalarGridSpec(
            num_scalar_prefetch=1,
            grid=(1,),
            in_specs=[
                whole((count, D)),
                whole((count, D)),
                whole((count, 128)),
                whole((8, D)),
                whole((D, D)),
                whole((8, D)),
                whole(up_sums.shape),
            ]
            + [whole(context.shape) for context in contexts],
            out_specs=[whole((count, D)), whole(half), whole(half), whole((count, D))],
            scratch_shapes=[pltpu.VMEM((count, D), LOW), pltpu.VMEM((D, D), LOW)],
        ),
        out_shape=[
            jax.ShapeDtypeStruct((count, D), WIDE),
            jax.ShapeDtypeStruct(half, LOW),
            jax.ShapeDtypeStruct(half, LOW),
            jax.ShapeDtypeStruct((count, D), LOW),
        ],
        compiler_params=params(),
        cost_estimate=cost(12),
        name="norm_back",
    )(me, hidden, norm, inv, vec, wo, ffn_sums, up_sums, *contexts)


def input_grad_kernel(places, groups, grad_ref, *refs):
    weights, refs = refs[:groups], refs[groups:]
    total = grad_ref[...]
    for quad, (group, at) in enumerate(places):
        for matrix in range(3):
            total = total + dot(
                refs[3 * quad + matrix][...],
                weights[group][matrix, :, at * QUAD : at * QUAD + QUAD],
                1,
                1,
            )
    refs[-1][...] = total


def input_grad_call(pieces, places, weights, grad):
    count = grad.shape[0]
    tile = 512
    tokens = lambda width: pl.BlockSpec((tile, width), lambda i: (i, 0))
    values = [value for piece in pieces for value in piece]
    return pl.pallas_call(
        functools.partial(input_grad_kernel, places, len(weights)),
        grid=(count // tile,),
        in_specs=[tokens(D)]
        + [whole(weight.shape) for weight in weights]
        + [tokens(QUAD) for _ in values],
        out_specs=tokens(D),
        out_shape=jax.ShapeDtypeStruct((count, D), WIDE),
        compiler_params=params(),
        cost_estimate=cost(8),
        name="input_grad",
    )(grad, *weights, *values)


def pack_kernel(places, *refs):
    for ref, (row, col) in zip(refs, places):
        refs[-1][row : row + ref.shape[0], col : col + ref.shape[1]] = ref[...]


def pack(parts, width):
    if any(array.shape[0] % 16 for line in parts for array, _ in line):
        return jnp.concatenate(
            [
                jnp.concatenate([a[:, width * at : width * (at + 1)] for a, at in line], axis=1)
                for line in parts
            ]
        )
    places, specs, row = [], [], 0
    for line in parts:
        for at, (array, block) in enumerate(line):
            places.append((row, at * width))
            specs.append(pl.BlockSpec((array.shape[0], width), lambda i, block=block: (0, block)))
        row += line[0][0].shape[0]
    shape = (row, width * len(parts[0]))
    return pl.pallas_call(
        functools.partial(pack_kernel, places),
        grid=(1,),
        in_specs=specs,
        out_specs=pl.BlockSpec(shape, lambda i: (0, 0)),
        out_shape=jax.ShapeDtypeStruct(shape, LOW),
        compiler_params=params(),
        cost_estimate=cost(1),
        name="pack",
    )(*(array for line in parts for array, _ in line))


def swap(value, mask, count):
    return lax.ppermute(value, "fsdp", [(i, i ^ mask) for i in range(count)])


def after(value, *others):
    return lax.optimization_barrier((value,) + others)[0] if others else value


class Gather:
    def __init__(self, piece, count, half=False):
        self.unit = 1
        if half:
            rows = piece.shape[0] // 2
            piece = lax.dynamic_slice_in_dim(piece, lax.axis_index("rep") * rows, rows, 0)
            self.unit = 2
        self.parts, self.count = [(piece[None], [0])], count
        self.hops = [count >> at for at in range(1, count.bit_length() - 2)]

    def far(self, *others):
        held, _ = self.parts[0]
        self.other = swap(after(held, *others), self.hops[0], self.count)

    def land(self, *others):
        held, order = self.parts[0]
        held = jnp.concatenate([held, after(self.other, *others)], axis=0)
        mask = self.hops.pop(0) * self.unit
        self.parts = [(held, order + [at ^ mask for at in order])]
        return held

    def far_but(self, last):
        while len(self.hops) > last:
            self.far()
            self.land()
        return self.parts[0][0]

    def send(self, part, hop):
        held, order = self.parts[part]
        if hop == "rep":
            other, mask = lax.ppermute(held, "rep", [(0, 1), (1, 0)]), 1
        else:
            other, mask = swap(held, hop, self.count), hop * self.unit
        self.parts.append((other, [at ^ mask for at in order]))

    def tie(self, part, *others):
        held, order = self.parts[part]
        self.parts[part] = (after(held, *others), order)
        return self.parts[part][0]


def matrices(gather, number, rows, me):
    pieces, slots = zip(*gather.parts)
    if rows % 16 == 0:
        return pieces, slots, rows
    parts = in_order(jnp.concatenate(pieces)[:, : number * rows], slots, me)
    count, _, width = parts.shape
    parts = jnp.moveaxis(parts.reshape(count, number, rows, width), 1, 0)
    return (parts.reshape(1, number * count * rows, width),), ([0],), count * rows


def in_order(held, slots, me):
    count = held.shape[0]
    distance = jnp.array([at for order in slots for at in order], jnp.int32)
    chosen = (jnp.arange(count, dtype=jnp.int32) ^ me)[:, None] == distance[None]
    return jnp.einsum(
        "ij,jrc->irc", chosen.astype(LOW), held, preferred_element_type=WIDE
    ).astype(LOW)


def to_slots(parts, slots, me):
    count = parts.shape[0]
    bit = 1
    while bit < count:
        pairs = parts.reshape((count // (2 * bit), 2, bit) + parts.shape[1:])
        parts = jnp.where((me & bit) != 0, pairs[:, ::-1], pairs).reshape(parts.shape)
        bit *= 2
    return tuple(
        jnp.concatenate([parts[at : at + 1] for at in distances]) for distances in slots
    )


def sum_order(count):
    bits = count.bit_length() - 2
    order = [
        sum(2 << place for place in range(bits) if at >> (bits - 1 - place) & 1)
        for at in range(count // 2)
    ]
    return order, [at ^ 1 for at in order]


class Sum:
    def __init__(self, keep, send, count, half=False):
        self.terms, self.send, self.count = [(keep, ())], send, count
        self.slots, self.kernel = keep.shape[0], False
        self.half, self.bit, self.total = half, 1, None

    def start(self, *others):
        send = after(self.send, *others) if others else self.send
        if self.half == "now" or self.bit == self.count:
            self.other = lax.ppermute(send, "rep", [(0, 1), (1, 0)])
        else:
            self.other = swap(send, self.bit, self.count)

    def added(self, *cuts):
        total = 0
        for array, before in self.terms:
            for each in (*before, *cuts):
                array = each(array)
            total = total + array.astype(WIDE)
        return total

    def cut(self, each):
        self.terms = [(array, (*before, each)) for array, before in self.terms]

    def land(self, *others):
        other = after(self.other, *others) if others else self.other
        if self.bit == self.count:
            if self.half:
                low = lax.axis_index("rep") == 0
                both = jnp.where(low, self.send, other), jnp.where(low, other, self.send)
                self.total = jnp.concatenate(both, axis=1)[0].astype(WIDE)
            else:
                self.total = (self.send.astype(WIDE) + other.astype(WIDE))[0]
            return self.total
        self.terms.append((other, ()))
        if self.half == "now":
            self.half = "done"
        else:
            self.bit *= 2
            if self.half is True:
                return self.halve()
        if self.bit == self.count:
            self.send = self.added().astype(LOW)
            return self.send
        middle = self.slots // 2
        if self.kernel and self.slots > 1:
            self.send = add_upper([array for array, _ in self.terms])
            self.kernel = False
        else:
            self.send = self.added(lambda term: term[middle:]).astype(LOW)
        self.cut(lambda term: term[:middle])
        self.slots = middle
        return self.send

    def halve(self):
        mine = lax.axis_index("rep")
        _, rows, width = self.send.shape

        def pick(at):
            return lambda term: lax.dynamic_slice_in_dim(term, at * (rows // 2), rows // 2, 1)

        self.send = self.added(pick(1 - mine)).astype(LOW)
        self.cut(pick(mine))
        self.half = "now"
        return self.send

    def finish(self):
        while self.total is None:
            self.start()
            self.land()


def add_kernel(*refs):
    total = 0
    for ref in refs[:-1]:
        total = total + ref[...].astype(WIDE)
    refs[-1][...] = total.astype(LOW)


def add_upper(terms):
    slots, rows, width = terms[0].shape
    upper = pl.BlockSpec((1, rows, width), lambda at: (at + slots // 2, 0, 0))
    return pl.pallas_call(
        add_kernel,
        grid=(slots // 2,),
        in_specs=[upper] * len(terms),
        out_specs=pl.BlockSpec((1, rows, width), lambda at: (at, 0, 0)),
        out_shape=jax.ShapeDtypeStruct((slots // 2, rows, width), LOW),
        compiler_params=params(),
        cost_estimate=cost(12),
        name="add",
    )(*terms)


def joined(sums):
    first = sums[0]
    whole = Sum(first.send, jnp.concatenate([item.send for item in sums], axis=1), first.count)
    whole.bit, whole.slots = first.bit, first.slots
    whole.terms = [(jnp.concatenate([item.added() for item in sums], axis=1), ())]
    return whole


def shards(
    inputs,
    block_kind,
    query_weight,
    query_bias,
    key_weight,
    value_weight,
    value_bias,
    out_weight,
    out_bias,
    attn_gain,
    attn_shift,
    up_weight,
    up_bias,
    down_weight,
    down_bias,
    ffn_gain,
    ffn_shift,
    cotangent,
):
    rows = query_weight.shape[0]
    count = D // rows
    hidden = up_weight.shape[1]
    steps = hidden // TILE
    vectors = (
        query_bias,
        value_bias,
        out_bias,
        attn_gain,
        attn_shift,
        down_bias,
        ffn_gain,
        ffn_shift,
    )
    down_rows = down_weight.shape[0]
    used = 8 * rows + up_bias.shape[0]
    spare = 16 * QUAD
    packed, at = 0, 0
    for value in vectors + (up_bias,):
        packed = packed + jnp.pad(value, (at, spare - at - value.shape[0]))
        at += value.shape[0]
    me = lax.axis_index("fsdp").astype(jnp.int32)
    own_rows = rows % 16 == 0
    mine = me.reshape(1)
    none = jnp.zeros((1,), jnp.int32)
    me_or_none = mine if own_rows else none
    qkv_weights = (query_weight, key_weight, value_weight)

    first = Gather(
        pack([[(w, 0)] for w in qkv_weights] + [[(packed.reshape(16, QUAD), 0)]], QUAD), count
    )
    inputs_t = inputs.T
    first.far()
    at = first.land()
    rest = Gather(pack([[(w, 1), (w, 2)] for w in qkv_weights], QUAD), count)
    rest.far(at)
    at = rest.land(first.far_but(0))
    third = Gather(down_weight, count, half=True)
    first.send(0, 2)
    first.send(0, 1)
    third.far(at)
    at = rest.far_but(0)
    at = first.tie(1, at)
    at = third.land(at)
    second = Gather(
        pack([[(out_weight, 0)]] + [[(up_weight, at)] for at in range(steps)], TILE), count
    )
    first.send(1, 1)
    rest.send(0, 2)
    rest.send(0, 1)
    second.far(at)
    third.far_but(1)
    third.far()

    pieces, slots = zip(*first.parts)
    columns = -(-used // QUAD)
    whole_packed = in_order(
        jnp.concatenate([piece[:, 3 * rows : 3 * rows + columns] for piece in pieces]), slots, me
    ).reshape(count, columns * QUAD)
    vec = (
        jnp.moveaxis(whole_packed[:, : 8 * rows].reshape(count, 8, rows), 1, 0)
        .reshape(8, D)
        .astype(WIDE)
    )
    all_up_bias = whole_packed[:, 8 * rows : used].reshape(1, hidden).astype(WIDE)

    places = [(0, 0), (1, 0), (1, 1)]
    at = rest.tie(1)
    at = third.land(at)
    at = second.land(at)
    rest.send(1, 1)
    third.send(0, 2)
    third.send(0, "rep")
    third.send(0, 1)
    second.far_but(1)
    second.far()
    heads = [
        attend(
            block_kind, me_or_none, [0], after(inputs, at, inputs_t), matrices(first, 3, rows, me), vec
        )
    ]
    at = third.tie(1, heads[0][3])
    third.send(1, "rep")
    third.send(1, 1)
    at = second.land(at)
    second.send(0, 2)
    second.send(0, 1)
    heads.append(
        attend(
            block_kind, me_or_none, [1, 2], after(inputs, at), matrices(rest, 3, rows, me), vec
        )
    )
    contexts = [group[3] for group in heads]
    contexts_t = [group[4] for group in heads]
    at = third.tie(2, heads[1][3])
    at = third.tie(4, at)
    second.tie(1, at)
    second.send(1, 1)
    third.send(2, 1)
    third.send(4, 1)
    act, slope, norm, first_inv, hlt, wo, up = up_call(
        me_or_none, contexts, inputs, matrices(second, 1 + steps, rows, me), vec, all_up_bias
    )
    side = 2 * me + lax.axis_index("rep").astype(jnp.int32)
    pieces = matrices(third, 1, down_rows // 2, side)
    layer_out, grad, low, ffn_sums, down = down_call(
        side.reshape(1) if down_rows % 32 == 0 else none, act, pieces, norm, vec, cotangent
    )

    order = sum_order(count)
    quads = D // QUAD

    def halves_of(keep, send, k, groups=1):
        if own_rows:
            return keep, send
        width = keep.shape[-1]
        tall = keep.shape[1] // groups
        everything = []
        for group in jnp.split(keep[0], groups):
            parts = jnp.moveaxis(group[: k * D].reshape(k, count, rows, width), 0, 1)
            everything.append(parts.reshape(count, k * rows, width))
            everything.append(jnp.broadcast_to(group[None, k * D :], (count, tall - k * D, width)))
        return to_slots(jnp.concatenate(everything, axis=1), order, me)

    kernel_order = order if own_rows else ([0], [])
    if 2 * down_rows % 128 == 0:
        middle = count // 4
        near, far = ([part[at] for part in order] for at in (slice(middle), slice(middle, None)))
        far_keep, far_send = down_grad_call(mine, far, down_rows, act, low)
        far_other = swap(far_send, 1, count)
        near_keep, near_send = down_grad_call(mine, near, down_rows, act, after(low, far_keep))
        sum_down = Sum(near_keep, None, count)
        sum_down.bit, sum_down.slots, sum_down.kernel = 2, middle, True
        far_other = after(far_other, near_keep)
        sum_down.send = (far_keep.astype(WIDE) + far_other.astype(WIDE)).astype(LOW)
        at = sum_down.send
        sum_down.start()
        sum_down.terms.append((swap(near_send, 1, count), ()))
    else:
        parts = down_grad_plain_call(act, low).reshape(count, down_rows, D)
        sum_down = Sum(*to_slots(parts, order, me), count)
        sum_down.start()
        at = sum_down.land()
        sum_down.start()

    keep, send, up_sums, grad_hidden = up_grad_call(
        me_or_none, kernel_order, list(range(steps)), low, down, slope, hlt, up, after(grad, at)
    )
    sum_up = Sum(*halves_of(keep, send, steps), count, half=True)
    sum_up.start()
    at = sum_down.land(grad_hidden)
    sum_down.start()
    at = sum_up.land(at)
    sum_up.start()
    grad_attn, keep, send, grad_ctx = norm_back_call(
        me_or_none, kernel_order, after(grad_hidden, at), norm, first_inv, vec, contexts_t, wo,
        ffn_sums, up_sums,
    )
    sum_out = Sum(*halves_of(keep, send, 1, quads), count)
    sum_out.start()
    at = grad_attn

    def back(quad, *others):
        group, at = places[quad]
        q, k, v, ctx, _, raised, inv, _ = heads[group]
        *part, keep, send = attend_back(
            me_or_none, kernel_order, quad, at, inputs_t, after(grad_ctx, *others), ctx, inv, q, k, v,
            raised,
        )
        return part, Sum(*halves_of(keep, send, 3), count)

    part_0, sum_0 = back(0, at)
    sum_0.start()
    at = sum_down.land(part_0[0])
    sum_down.start()
    at = sum_out.land(at)
    at = sum_up.land(at)
    sum_up.start()
    part_1, sum_1 = back(1, at)
    sum_1.start()
    at = sum_0.land(part_1[0])
    sum_0 = joined([sum_out, sum_0])
    sum_0.start()
    at = sum_down.land(at, sum_0.send)
    if sum_down.total is None:
        sum_down.start()
    at = sum_up.land(at)
    sum_up.start()
    part_2, sum_2 = back(2, at)
    sum_2.start()
    at = sum_1.land(part_2[0])
    sum_1.start()
    at = sum_2.land(at)
    sum_2.start()
    at = sum_up.land(at)
    sum_up.start()
    at = sum_0.land(at)
    sum_0.start()
    weights = [group[7] for group in heads]
    input_grad = input_grad_call([part_0, part_1, part_2], places, weights, after(grad_attn, at))
    at = sum_1.land(input_grad)
    at = sum_2.land(at)
    sum_1 = joined([sum_1, sum_2])
    sum_1.start()
    at = sum_0.land(at, sum_1.send)
    sum_0.start()
    if sum_up.total is None:
        at = sum_up.land(at)
        sum_up.start()
    while sum_1.total is None:
        for item in (sum_1, sum_0, sum_up, sum_down):
            if item.total is None:
                at = item.land(at)
            if item.total is None:
                item.start()
    for item in (sum_0, sum_up, sum_down):
        while item.total is None:
            item.land()
            if item.total is None:
                item.start()
    tall = 3 * rows + EXTRA
    grad_qkv = jnp.concatenate([sum_0.total[-tall:], sum_1.total[:tall], sum_1.total[tall:]], axis=1)
    grad_out = jnp.concatenate(jnp.split(sum_0.total[:-tall], quads), axis=1)
    of_mine = lambda value, size: lax.dynamic_slice_in_dim(value, me * size, size, value.ndim - 1)
    own = of_mine(
        jnp.concatenate([grad_qkv[3 * rows : 3 * rows + 2], grad_out[rows : rows + 6]]), rows
    )
    grad_up_bias = of_mine(grad_out[rows + 6 : rows + 6 + steps].reshape(-1), up_bias.shape[0])
    grad_up = sum_up.total
    return (
        layer_out,
        input_grad,
        grad_qkv[:rows],
        own[QUERY_BIAS],
        grad_qkv[rows : 2 * rows],
        grad_qkv[2 * rows : 3 * rows],
        own[VALUE_BIAS],
        grad_out[:rows],
        own[OUT_BIAS],
        own[ATTN_GAIN],
        own[ATTN_SHIFT],
        jnp.concatenate([grad_up[rows * i : rows * (i + 1)] for i in range(steps)], axis=1),
        grad_up_bias,
        sum_down.total,
        own[DOWN_BIAS],
        own[FFN_GAIN],
        own[FFN_SHIFT],
    )


def solution(mesh):
    tokens = P(("rep", "fsdp"), None)
    matrix = P("fsdp", None)
    vector = P("fsdp")
    params_placed = (
        matrix,
        vector,
        matrix,
        matrix,
        vector,
        matrix,
        vector,
        vector,
        vector,
        matrix,
        vector,
        matrix,
        vector,
        vector,
        vector,
    )
    return jax.shard_map(
        shards,
        mesh=mesh,
        in_specs=(tokens, P(("rep", "fsdp")), *params_placed, tokens),
        out_specs=(tokens, tokens, *params_placed),
        check_vma=False,
    )
```

```python
import functools

import jax
import jax.numpy as jnp
from jax import lax
from jax.experimental import pallas as pl
from jax.experimental.pallas import tpu as pltpu
from jax.sharding import PartitionSpec as P

D = 768
H = 12
HD = 64
LONG = 512
SHORT = 128
QUAD = 256
PAIR = 128
TILE = 768

EPSILON = 1e-05
BLOCKED = -1e30
LOW = jnp.bfloat16
WIDE = jnp.float32
ROOM = 56 << 20
EXTRA = 16

QUERY_BIAS, VALUE_BIAS, OUT_BIAS, ATTN_GAIN, ATTN_SHIFT, DOWN_BIAS, FFN_GAIN, FFN_SHIFT = range(8)


def dot(left, right, left_dim, right_dim):
    return lax.dot_general(
        left, right, (((left_dim,), (right_dim,)), ((), ())), preferred_element_type=WIDE
    )


def row_mean(value):
    return jnp.mean(value, axis=-1, keepdims=True)


def token_sum(value):
    return jnp.sum(value, axis=0, keepdims=True)


def whole(shape):
    zeros = (0,) * len(shape)
    return pl.BlockSpec(shape, lambda *_: zeros, pipeline_mode=pl.Buffered(1))


def place(target, sources, slots, me):
    rows = sources[0].shape[1]
    for source, distances in zip(sources, slots):
        for at, distance in enumerate(distances):
            start = pl.multiple_of((me ^ distance) * rows, rows)
            target[pl.ds(start, rows), :] = source[at]


def params():
    return pltpu.CompilerParams(vmem_limit_bytes=ROOM)


def cost(microseconds):
    return pl.CostEstimate(
        flops=int(microseconds * 1.1e9), bytes_accessed=1 << 20, transcendentals=0
    )


def unplace(targets, source, slots, me, top, rows):
    for target, distances in zip(targets, slots):
        for at, distance in enumerate(distances):
            start = pl.multiple_of((me ^ distance) * rows, rows)
            target[at, top : top + rows, :] = source(pl.ds(start, rows)).astype(LOW)


def to_all(targets, slots, top, rows):
    low = rows.astype(LOW)
    for target, distances in zip(targets, slots):
        for at in range(len(distances)):
            target[at, top : top + EXTRA, :] = low


def half_masks():
    lane = lax.broadcasted_iota(jnp.int32, (1, PAIR), 1)
    return [jnp.where(lane // HD == half, 1.0, 0.0) for half in range(2)]


def attend_kernel(slots, kind_ref, me_ref, x_ref, vec_ref, *refs):
    pieces = len(slots)
    sources, refs = refs[: 3 * pieces], refs[3 * pieces :]
    q_ref, k_ref, v_ref, ctx_ref, ctxt_ref, raised_ref, inv_ref, weight_ref = refs

    @pl.when(pl.program_id(1) == 0)
    def _():
        for at in range(3):
            place(weight_ref.at[at], sources[at * pieces : (at + 1) * pieces], slots, me_ref[0])

    x = x_ref[...]
    q_ref[...] = (dot(x, weight_ref[0], 1, 0) + vec_ref[QUERY_BIAS : QUERY_BIAS + 1]).astype(LOW)
    k_ref[...] = dot(x, weight_ref[1], 1, 0).astype(LOW)
    v_ref[...] = (dot(x, weight_ref[2], 1, 0) + vec_ref[VALUE_BIAS : VALUE_BIAS + 1]).astype(LOW)
    part = lax.broadcasted_iota(jnp.int32, (LONG, PAIR), 0) // SHORT
    lane = lax.broadcasted_iota(jnp.int32, (LONG, PAIR), 1)
    blocked = jnp.where(kind_ref[pl.program_id(1)] == 1, 0.0, BLOCKED)
    query_part = jnp.where((lane < LONG // SHORT) & (part != lane), blocked, 0.0).astype(LOW)
    key_part = jnp.where(part == lane, 1.0, 0.0).astype(LOW)
    halves = half_masks()
    for pair in range(QUAD // PAIR):
        cols = pl.ds(pair * PAIR, PAIR)
        q2 = q_ref[:, cols].astype(WIDE) * HD ** (-0.5)
        keys = jnp.concatenate([k_ref[:, cols], key_part], axis=1)
        v2t = v_ref[:, cols].T
        contexts, inverses = [], []
        for half in range(2):
            queries = jnp.concatenate([(q2 * halves[half]).astype(LOW), query_part], axis=1)
            scores = dot(keys, queries, 1, 1)
            peak = jnp.max(scores, axis=0, keepdims=True)
            raised = jnp.exp(scores - peak).astype(LOW)
            raised_ref[0, pair * 2 + half] = raised
            left = jnp.concatenate(
                [v2t[HD * half : HD * half + HD], jnp.ones((16, LONG), LOW)], axis=0
            )
            mixed = dot(left, raised, 1, 0)
            inverse = 1.0 / mixed[HD : HD + 1]
            contexts.append(mixed[:HD] * inverse)
            inverses.append(jnp.broadcast_to(inverse, (HD, LONG)))
        context = jnp.concatenate(contexts, axis=0)
        ctxt_ref[pair * PAIR : pair * PAIR + PAIR, :] = context.astype(LOW)
        ctx_ref[:, cols] = context.T.astype(LOW)
        inv_ref[:, cols] = jnp.concatenate(inverses, axis=0).T


def attend(kind, me, quads, x, weights, vec):
    pieces, slots, rows = weights
    count = x.shape[0]
    blocks, number, low = count // LONG, len(quads), quads[0]
    tokens = pl.BlockSpec((LONG, QUAD), lambda j, b, *_: (b, j))
    act = jax.ShapeDtypeStruct((count, number * QUAD), LOW)
    return pl.pallas_call(
        functools.partial(attend_kernel, slots),
        grid_spec=pltpu.PrefetchScalarGridSpec(
            num_scalar_prefetch=2,
            grid=(number, blocks),
            in_specs=[
                pl.BlockSpec((LONG, D), lambda j, b, *_: (b, 0)),
                pl.BlockSpec((8, QUAD), lambda j, b, *_: (0, j + low)),
            ]
            + [
                pl.BlockSpec((piece.shape[0], rows, QUAD), lambda j, b, *_, at=at: (0, at, j))
                for at in range(3)
                for piece in pieces
            ],
            out_specs=[
                tokens,
                tokens,
                tokens,
                tokens,
                pl.BlockSpec((QUAD, LONG), lambda j, b, *_: (j, b)),
                pl.BlockSpec((1, QUAD // HD, LONG, LONG), lambda j, b, *_: (b, j, 0, 0)),
                tokens,
                pl.BlockSpec((3, D, QUAD), lambda j, b, *_: (0, 0, j)),
            ],
        ),
        out_shape=[
            act,
            act,
            act,
            act,
            jax.ShapeDtypeStruct((number * QUAD, count), LOW),
            jax.ShapeDtypeStruct((blocks, number * QUAD // HD, LONG, LONG), LOW),
            jax.ShapeDtypeStruct((count, number * QUAD), WIDE),
            jax.ShapeDtypeStruct((3, D, number * QUAD), LOW),
        ],
        compiler_params=params(),
        cost_estimate=cost(0.1),
        name="attend",
    )(kind, me, x, vec, *(list(pieces) * 3))


def attend_back_kernel(
    slots,
    me_ref,
    xt_ref,
    d_ref,
    ctx_ref,
    inv_ref,
    q_ref,
    k_ref,
    v_ref,
    raised_ref,
    dq_ref,
    dk_ref,
    dv_ref,
    *refs,
):
    targets, (totals, biases) = refs[:-2], refs[-2:]
    block = pl.program_id(0)
    halves = half_masks()
    minus = jnp.full((LONG, PAIR), -1.0, LOW)
    work = []
    for pair in range(QUAD // PAIR):
        cols = pl.ds(pair * PAIR, PAIR)
        d2 = d_ref[:, cols].astype(WIDE) * inv_ref[:, cols] * HD ** (-0.5)
        along = d2 * ctx_ref[:, cols].astype(WIDE)
        q2 = q_ref[:, cols].astype(WIDE)
        values = jnp.concatenate([v_ref[:, cols], minus], axis=1)
        for half in range(2):
            dm = (d2 * halves[half]).astype(LOW)
            am = (along * halves[half]).astype(LOW)
            qm = (q2 * halves[half]).astype(LOW)
            dp = dot(values, jnp.concatenate([dm, am], axis=1), 1, 1)
            work.append((pair, half, dm, qm, dp))
    k2ts = [k_ref[:, pl.ds(pair * PAIR, PAIR)].T for pair in range(QUAD // PAIR)]
    done = []
    for pair, half, dm, qm, dp in work:
        raised = raised_ref[0, pair * 2 + half]
        ds = (raised.astype(WIDE) * dp).astype(LOW)
        done.append((pair, half, raised, ds, dm, qm))
    for pair in range(QUAD // PAIR):
        cols = pl.ds(pair * PAIR, PAIR)
        dqt, dk, dv = [], 0, 0
        for p, half, raised, ds, dm, qm in done:
            if p == pair:
                dqt.append(dot(k2ts[pair][HD * half : HD * half + HD], ds, 1, 0))
        both = [item for item in done if item[0] == pair]
        wide = lambda at, axis: jnp.concatenate([item[at] for item in both], axis=axis)
        dv = dot(wide(2, 1), wide(4, 0), 1, 0)
        dk = dot(wide(3, 1), wide(5, 0), 1, 0)
        dv_ref[:, cols] = (dv * HD**0.5).astype(LOW)
        dk_ref[:, cols] = dk.astype(LOW)
        dq_ref[:, cols] = jnp.concatenate(dqt, axis=0).T.astype(LOW)
    xt = xt_ref[...]
    for at, ref in enumerate((dq_ref, dk_ref, dv_ref)):
        grad = dot(xt, ref[...], 1, 0)

        @pl.when(block == 0)
        def _(grad=grad, at=at):
            totals[at] = grad

        @pl.when(block != 0)
        def _(grad=grad, at=at):
            totals[at] += grad

    sums = jnp.concatenate(
        [
            token_sum(dq_ref[...].astype(WIDE)),
            token_sum(dv_ref[...].astype(WIDE)),
            jnp.zeros((EXTRA - 2, QUAD), WIDE),
        ],
        axis=0,
    )

    @pl.when(block == 0)
    def _():
        biases[...] = sums

    @pl.when(block != 0)
    def _():
        biases[...] += sums

    @pl.when(block == pl.num_programs(0) - 1)
    def _():
        rows = (targets[0].shape[1] - EXTRA) // 3
        for at in range(3):
            unplace(
                targets, lambda part, at=at: totals[at, part], slots, me_ref[0], at * rows, rows
            )
        to_all(targets, slots, 3 * rows, biases[...])


def attend_back(me, slots, quad, at, xt, d, ctx, inv, q, k, v, raised):
    count = q.shape[0]
    tokens = pl.BlockSpec((LONG, QUAD), lambda b, *_: (b, at))
    grads = pl.BlockSpec((LONG, QUAD), lambda b, *_: (b, 0))
    act = jax.ShapeDtypeStruct((count, QUAD), LOW)
    rows = D // sum(map(len, slots))
    halves = [(max(len(part), 1), 3 * rows + EXTRA, QUAD) for part in slots]
    return pl.pallas_call(
        functools.partial(attend_back_kernel, slots),
        grid_spec=pltpu.PrefetchScalarGridSpec(
            num_scalar_prefetch=1,
            grid=(count // LONG,),
            in_specs=[
                pl.BlockSpec((D, LONG), lambda b, *_: (0, b)),
                pl.BlockSpec((LONG, QUAD), lambda b, *_: (b, quad)),
            ]
            + [tokens] * 5
            + [pl.BlockSpec((1, QUAD // HD, LONG, LONG), lambda b, *_: (b, at, 0, 0))],
            out_specs=[grads, grads, grads] + [whole(half) for half in halves],
            scratch_shapes=[pltpu.VMEM((3, D, QUAD), WIDE), pltpu.VMEM((EXTRA, QUAD), WIDE)],
        ),
        out_shape=[act, act, act] + [jax.ShapeDtypeStruct(half, LOW) for half in halves],
        compiler_params=params(),
        cost_estimate=cost(2),
        name="attend_back",
    )(me, xt, d, ctx, inv, q, k, v, raised)


def out_kernel(places, groups, me_ref, x_ref, vec_ref, *refs):
    contexts, refs = refs[:groups], refs[groups:]
    norm_ref, inv_ref, hl_ref, hlt_ref, wo_ref = refs[-5:]
    at, col = 0, 0
    for slots in places:
        sources = refs[at : at + len(slots)]
        at += len(slots)
        width = sources[0].shape[2]
        place(wo_ref.at[:, col : col + width], sources, slots, me_ref[0])
        col += width
    bias = vec_ref[OUT_BIAS : OUT_BIAS + 1]
    gain = vec_ref[ATTN_GAIN : ATTN_GAIN + 1]
    shift = vec_ref[ATTN_SHIFT : ATTN_SHIFT + 1]
    wo = wo_ref[...]
    step = 256
    for at in range(0, x_ref.shape[0], step):
        rows = pl.ds(at, step)
        context = jnp.concatenate([ref[rows] for ref in contexts], axis=1)
        total = x_ref[rows].astype(WIDE) + dot(context, wo, 1, 0) + bias
        centered = total - row_mean(total)
        inverse = lax.rsqrt(row_mean(centered * centered) + EPSILON)
        norm = centered * inverse
        norm_ref[rows] = norm
        inv_ref[rows] = jnp.broadcast_to(inverse, (step, 128))
        hidden = (norm * gain + shift).astype(LOW)
        hl_ref[rows] = hidden
        hlt_ref[:, rows] = hidden.T


def out_call(me, contexts, x, weights, vec):
    count = x.shape[0]
    specs, values = [], []
    for pieces, _, rows in weights:
        for piece in pieces:
            specs.append(pl.BlockSpec((piece.shape[0], rows, piece.shape[2]), lambda *_: (0, 3, 0)))
            values.append(piece)
    shapes = [((count, D), WIDE), ((count, 128), WIDE), ((count, D), LOW), ((D, count), LOW), ((D, D), LOW)]
    return pl.pallas_call(
        functools.partial(out_kernel, [slots for _, slots, _ in weights], len(contexts)),
        grid_spec=pltpu.PrefetchScalarGridSpec(
            num_scalar_prefetch=1,
            grid=(1,),
            in_specs=[whole((count, D)), whole((8, D))]
            + [whole(context.shape) for context in contexts]
            + specs,
            out_specs=[whole(shape) for shape, _ in shapes],
        ),
        out_shape=[jax.ShapeDtypeStruct(shape, dtype) for shape, dtype in shapes],
        compiler_params=params(),
        cost_estimate=cost(0.1),
        name="out",
    )(me, x, vec, *contexts, *values)


def up_kernel(slots, me_ref, hl_ref, bu_ref, *refs):
    own, other = slots
    ups, (act_ref, slope_ref, wu_ref) = refs[:-3], refs[-3:]
    step = 256
    first_half = pl.program_id(0) < pl.num_programs(0) // 2

    @pl.when(first_half)
    def _():
        place(wu_ref.at[0], ups[: len(own)], own, me_ref[0])

    @pl.when(jnp.logical_not(first_half))
    def _():
        place(wu_ref.at[0], ups[len(own) :], other, me_ref[0])

    bias = bu_ref[...]
    weight = wu_ref[0]
    for at in range(0, hl_ref.shape[0], step):
        rows = pl.ds(at, step)
        before = dot(hl_ref[rows], weight, 1, 0) + bias
        half = 0.5 * (1.0 + lax.erf(before * 0.7071067811865476))
        act_ref[rows] = (before * half).astype(LOW)
        slope_ref[rows] = (
            half + before * jnp.exp(-0.5 * before * before) * 0.3989422804014327
        ).astype(LOW)


def up_call(me, hl, own, other, rows, up_bias):
    count = hl.shape[0]
    hidden = up_bias.shape[1]
    steps = hidden // TILE
    half = steps // 2
    cols = lambda r: pl.BlockSpec((r, TILE), lambda j, me: (0, j ^ me[1]))
    early = lambda j, *_: (0, jnp.minimum(j, half - 1), 0)
    late = lambda j, *_: (0, jnp.maximum(j - half, 0), 0)
    return pl.pallas_call(
        functools.partial(up_kernel, (own[1], other[1])),
        grid_spec=pltpu.PrefetchScalarGridSpec(
            num_scalar_prefetch=1,
            grid=(steps,),
            in_specs=[whole((count, D)), cols(1)]
            + [pl.BlockSpec((piece.shape[0], rows, D), early) for piece in own[0]]
            + [pl.BlockSpec((piece.shape[0], rows, D), late) for piece in other[0]],
            out_specs=[
                cols(count),
                cols(count),
                pl.BlockSpec((1, D, TILE), lambda j, me: (j ^ me[1], 0, 0)),
            ],
        ),
        out_shape=[
            jax.ShapeDtypeStruct((count, hidden), LOW),
            jax.ShapeDtypeStruct((count, hidden), LOW),
            jax.ShapeDtypeStruct((steps, D, TILE), LOW),
        ],
        compiler_params=params(),
        cost_estimate=cost(0.1),
        name="up",
    )(me, hl, up_bias, *own[0], *other[0])


def down_kernel(slots, me_ref, act_ref, norm_ref, vec_ref, cot_ref, *refs):
    sources = refs[: len(slots)]
    out_ref, grad_ref, low_ref, sums_ref, wd_ref = refs[len(slots) :]

    @pl.when(pl.program_id(0) == 0)
    def _():
        place(wd_ref, sources, slots, me_ref[0])

    row = lambda at: vec_ref[at : at + 1]
    total = (
        norm_ref[...] * row(ATTN_GAIN)
        + row(ATTN_SHIFT)
        + (dot(act_ref[...], wd_ref[...], 1, 0) + row(DOWN_BIAS))
    )
    centered = total - row_mean(total)
    inverse = lax.rsqrt(row_mean(centered * centered) + EPSILON)
    norm = centered * inverse
    out_ref[...] = (norm * row(FFN_GAIN) + row(FFN_SHIFT)).astype(LOW)
    grad_out = cot_ref[...].astype(WIDE)
    scaled = grad_out * row(FFN_GAIN)
    grad = inverse * (scaled - row_mean(scaled) - norm * row_mean(scaled * norm))
    grad_ref[...] = grad
    low = grad.astype(LOW)
    low_ref[...] = low
    sums = jnp.concatenate(
        [
            token_sum(grad_out * norm),
            token_sum(grad_out),
            token_sum(low.astype(WIDE)),
            jnp.zeros((5, D), WIDE),
        ],
        axis=0,
    )

    @pl.when(pl.program_id(0) == 0)
    def _():
        sums_ref[...] = sums

    @pl.when(pl.program_id(0) != 0)
    def _():
        sums_ref[...] += sums


def down_call(me, act, third, norm, vec, cotangent):
    pieces, slots, _ = third
    count, hidden = act.shape
    tile = 256
    rows = lambda c: pl.BlockSpec((tile, c), lambda i, *_: (i, 0))
    return pl.pallas_call(
        functools.partial(down_kernel, slots),
        grid_spec=pltpu.PrefetchScalarGridSpec(
            num_scalar_prefetch=1,
            grid=(count // tile,),
            in_specs=[rows(hidden), rows(D), whole((8, D)), rows(D)]
            + [whole(piece.shape) for piece in pieces],
            out_specs=[rows(D), rows(D), rows(D), whole((8, D)), whole((hidden, D))],
        ),
        out_shape=[
            jax.ShapeDtypeStruct((count, D), LOW),
            jax.ShapeDtypeStruct((count, D), WIDE),
            jax.ShapeDtypeStruct((count, D), LOW),
            jax.ShapeDtypeStruct((8, D), WIDE),
            jax.ShapeDtypeStruct((hidden, D), LOW),
        ],
        compiler_params=params(),
        cost_estimate=cost(13),
        name="down",
    )(me, act, norm, vec, cotangent, *pieces)


def down_grad_kernel(owner_ref, me_ref, act_ref, low_ref, keep_ref, send_ref, scratch):
    rows = keep_ref.shape[1]
    scratch[...] = dot(act_ref[...], low_ref[...], 0, 0).astype(LOW)
    mine = lax.rem(me_ref[0], 2) * rows
    keep_ref[0] = scratch[pl.ds(pl.multiple_of(mine, rows), rows)]
    send_ref[0] = scratch[pl.ds(pl.multiple_of(rows - mine, rows), rows)]


def down_grad_plain_kernel(act_ref, low_ref, grad_ref):
    grad_ref[...] = dot(act_ref[...], low_ref[...], 0, 0).astype(LOW)


def down_grad_plain_call(act, low):
    count, hidden = act.shape
    return pl.pallas_call(
        down_grad_plain_kernel,
        grid=(hidden // TILE,),
        in_specs=[pl.BlockSpec((count, TILE), lambda j: (0, j)), whole((count, D))],
        out_specs=pl.BlockSpec((TILE, D), lambda j: (j, 0)),
        out_shape=jax.ShapeDtypeStruct((hidden, D), LOW),
        compiler_params=params(),
        cost_estimate=cost(9),
        name="down_grad",
    )(act, low)


def down_grad_call(me, slots, rows, act, low):
    count, hidden = act.shape
    number = len(slots[0])
    pair = 2 * rows
    owners = (me // 2) ^ (jnp.array(slots[0], jnp.int32) // 2)
    part = pl.BlockSpec((1, rows, D), lambda j, *_: (j, 0, 0))
    half = jax.ShapeDtypeStruct((number, rows, D), LOW)
    return pl.pallas_call(
        down_grad_kernel,
        grid_spec=pltpu.PrefetchScalarGridSpec(
            num_scalar_prefetch=2,
            grid=(number,),
            in_specs=[
                pl.BlockSpec((count, pair), lambda j, owner, _: (0, owner[j])),
                whole((count, D)),
            ],
            out_specs=[part, part],
            scratch_shapes=[pltpu.VMEM((pair, D), LOW)],
        ),
        out_shape=[half, half],
        compiler_params=params(),
        cost_estimate=cost(number),
        name="down_grad",
    )(owners, me, act, low)


def up_grad_kernel(
    slots, me_ref, low_ref, wd_ref, slope_ref, hlt_ref, wu_ref, grad_ref,
    keep_ref, send_ref, bias_ref, hidden_ref, before_scr, grad_scr,
):
    step = pl.program_id(0)
    before_scr[...] = (dot(low_ref[...], wd_ref[...], 1, 1) * slope_ref[...].astype(WIDE)).astype(
        LOW
    )
    before = before_scr[...]
    grad_scr[...] = dot(hlt_ref[...], before, 1, 0).astype(LOW)
    unplace(
        (keep_ref, send_ref), lambda part: grad_scr[part], slots, me_ref[0], 0, keep_ref.shape[1]
    )
    bias_ref[...] = jnp.broadcast_to(token_sum(before.astype(WIDE)), (8, TILE))
    back = dot(before, wu_ref[0], 1, 1)

    @pl.when(step == 0)
    def _():
        hidden_ref[...] = back + grad_ref[...]

    @pl.when(step != 0)
    def _():
        hidden_ref[...] += back


def up_grad_call(me, slots, tiles, low, down, slope, hlt, up, grad):
    count = slope.shape[0]
    first, steps = tiles[0], len(tiles)
    kept, rows = len(slots[0]), D // (len(slots[0]) + len(slots[1]))
    part = pl.BlockSpec((kept, rows, TILE), lambda j, *_: (0, j, 0))
    half = jax.ShapeDtypeStruct((kept, steps * rows, TILE), LOW)
    return pl.pallas_call(
        functools.partial(up_grad_kernel, slots),
        grid_spec=pltpu.PrefetchScalarGridSpec(
            num_scalar_prefetch=1,
            grid=(steps,),
            in_specs=[
                whole((count, D)),
                pl.BlockSpec((TILE, D), lambda j, *_: (j + first, 0)),
                pl.BlockSpec((count, TILE), lambda j, *_: (0, j + first)),
                whole((D, count)),
                pl.BlockSpec((1, D, TILE), lambda j, *_: (j + first, 0, 0)),
                whole((count, D)),
            ],
            out_specs=[
                part,
                part,
                pl.BlockSpec((8, TILE), lambda j, *_: (j, 0)),
                whole((count, D)),
            ],
            scratch_shapes=[pltpu.VMEM((count, TILE), LOW), pltpu.VMEM((D, TILE), LOW)],
        ),
        out_shape=[
            half,
            half,
            jax.ShapeDtypeStruct((8 * steps, TILE), WIDE),
            jax.ShapeDtypeStruct((count, D), WIDE),
        ],
        compiler_params=params(),
        cost_estimate=cost(6 * steps),
        name="up_grad",
    )(me, low, down, slope, hlt, up, grad)


def norm_back_kernel(
    slots, groups, me_ref, hidden_ref, norm_ref, inv_ref, vec_ref, wo_ref, ffn_ref, up_ref, *refs
):
    contexts, refs = refs[:groups], refs[groups:]
    grad_ref, keep_ref, send_ref, ctx_ref, low_scr, out_scr = refs
    count = hidden_ref.shape[0]
    step = 256
    gain = vec_ref[ATTN_GAIN : ATTN_GAIN + 1]
    wo = wo_ref[...]
    sums = 0
    for at in range(0, count, step):
        rows = pl.ds(at, step)
        hidden = hidden_ref[rows]
        norm = norm_ref[rows]
        scaled = hidden * gain
        grad = inv_ref[rows][:, 0:1] * (
            scaled - row_mean(scaled) - norm * row_mean(scaled * norm)
        )
        grad_ref[rows] = grad
        low = grad.astype(LOW)
        low_scr[rows] = low
        sums = sums + jnp.concatenate(
            [
                token_sum(hidden * norm),
                token_sum(hidden),
                token_sum(low.astype(WIDE)),
                jnp.zeros((5, D), WIDE),
            ],
            axis=0,
        )
        ctx_ref[rows] = dot(low, wo, 1, 1).astype(LOW)
    at = 0
    for ref in contexts:
        out_scr[at : at + ref.shape[0], :] = dot(ref[...], low_scr[...], 1, 0).astype(LOW)
        at += ref.shape[0]
    quads = D // QUAD
    rows = keep_ref.shape[1] // quads - EXTRA
    steps = up_ref.shape[0] // 8
    extra = [sums[2:3], sums[:2], ffn_ref[2:3], ffn_ref[:2]]
    extra += [up_ref[8 * at : 8 * at + 1] for at in range(steps)]
    extra.append(jnp.zeros((EXTRA - 6 - steps, D), WIDE))
    extra = jnp.concatenate(extra, axis=0)
    for quad in range(quads):
        cols = slice(quad * QUAD, quad * QUAD + QUAD)
        top = quad * (rows + EXTRA)
        targets = keep_ref, send_ref
        unplace(targets, lambda part: out_scr[part, cols], slots, me_ref[0], top, rows)
        to_all(targets, slots, top + rows, extra[:, cols])


def norm_back_call(me, slots, hidden, norm, inv, vec, contexts, wo, ffn_sums, up_sums):
    count = hidden.shape[0]
    kept, rows = len(slots[0]), D // (len(slots[0]) + len(slots[1]))
    half = (kept, (rows + EXTRA) * (D // QUAD), QUAD)
    return pl.pallas_call(
        functools.partial(norm_back_kernel, slots, len(contexts)),
        grid_spec=pltpu.PrefetchScalarGridSpec(
            num_scalar_prefetch=1,
            grid=(1,),
            in_specs=[
                whole((count, D)),
                whole((count, D)),
                whole((count, 128)),
                whole((8, D)),
                whole((D, D)),
                whole((8, D)),
                whole(up_sums.shape),
            ]
            + [whole(context.shape) for context in contexts],
            out_specs=[whole((count, D)), whole(half), whole(half), whole((count, D))],
            scratch_shapes=[pltpu.VMEM((count, D), LOW), pltpu.VMEM((D, D), LOW)],
        ),
        out_shape=[
            jax.ShapeDtypeStruct((count, D), WIDE),
            jax.ShapeDtypeStruct(half, LOW),
            jax.ShapeDtypeStruct(half, LOW),
            jax.ShapeDtypeStruct((count, D), LOW),
        ],
        compiler_params=params(),
        cost_estimate=cost(12),
        name="norm_back",
    )(me, hidden, norm, inv, vec, wo, ffn_sums, up_sums, *contexts)


def input_grad_kernel(places, groups, grad_ref, *refs):
    weights, refs = refs[:groups], refs[groups:]
    total = grad_ref[...]
    for quad, (group, at) in enumerate(places):
        for matrix in range(3):
            total = total + dot(
                refs[3 * quad + matrix][...],
                weights[group][matrix, :, at * QUAD : at * QUAD + QUAD],
                1,
                1,
            )
    refs[-1][...] = total


def input_grad_call(pieces, places, weights, grad):
    count = grad.shape[0]
    tile = 512
    tokens = lambda width: pl.BlockSpec((tile, width), lambda i: (i, 0))
    values = [value for piece in pieces for value in piece]
    return pl.pallas_call(
        functools.partial(input_grad_kernel, places, len(weights)),
        grid=(count // tile,),
        in_specs=[tokens(D)]
        + [whole(weight.shape) for weight in weights]
        + [tokens(QUAD) for _ in values],
        out_specs=tokens(D),
        out_shape=jax.ShapeDtypeStruct((count, D), WIDE),
        compiler_params=params(),
        cost_estimate=cost(0.1),
        name="input_grad",
    )(grad, *weights, *values)


def pack_kernel(places, *refs):
    for ref, (row, col) in zip(refs, places):
        refs[-1][row : row + ref.shape[0], col : col + ref.shape[1]] = ref[...]


def pack(parts, width):
    if any(array.shape[0] % 16 for line in parts for array, _ in line):
        return jnp.concatenate(
            [
                jnp.concatenate([a[:, width * at : width * (at + 1)] for a, at in line], axis=1)
                for line in parts
            ]
        )
    places, specs, row = [], [], 0
    for line in parts:
        for at, (array, block) in enumerate(line):
            places.append((row, at * width))
            specs.append(pl.BlockSpec((array.shape[0], width), lambda i, block=block: (0, block)))
        row += line[0][0].shape[0]
    shape = (row, width * len(parts[0]))
    return pl.pallas_call(
        functools.partial(pack_kernel, places),
        grid=(1,),
        in_specs=specs,
        out_specs=pl.BlockSpec(shape, lambda i: (0, 0)),
        out_shape=jax.ShapeDtypeStruct(shape, LOW),
        compiler_params=params(),
        cost_estimate=cost(1),
        name="pack",
    )(*(array for line in parts for array, _ in line))


def swap(value, mask, count):
    return lax.ppermute(value, "fsdp", [(i, i ^ mask) for i in range(count)])


def after(value, *others):
    return lax.optimization_barrier((value,) + others)[0] if others else value


class Gather:
    def __init__(self, piece, count, half=False):
        self.unit = 1
        if half:
            rows = piece.shape[0] // 2
            piece = lax.dynamic_slice_in_dim(piece, lax.axis_index("rep") * rows, rows, 0)
            self.unit = 2
        self.parts, self.count = [(piece[None], [0])], count
        self.hops = [count >> at for at in range(1, count.bit_length() - 2)]

    def far(self, *others):
        held, _ = self.parts[0]
        self.other = swap(after(held, *others), self.hops[0], self.count)

    def land(self, *others):
        held, order = self.parts[0]
        held = jnp.concatenate([held, after(self.other, *others)], axis=0)
        mask = self.hops.pop(0) * self.unit
        self.parts = [(held, order + [at ^ mask for at in order])]
        return held

    def far_but(self, last):
        while len(self.hops) > last:
            self.far()
            self.land()
        return self.parts[0][0]

    def send(self, part, hop):
        held, order = self.parts[part]
        if hop == "rep":
            other, mask = lax.ppermute(held, "rep", [(0, 1), (1, 0)]), 1
        else:
            other, mask = swap(held, hop, self.count), hop * self.unit
        self.parts.append((other, [at ^ mask for at in order]))

    def tie(self, part, *others):
        held, order = self.parts[part]
        self.parts[part] = (after(held, *others), order)
        return self.parts[part][0]


def matrices(gather, number, rows, me):
    pieces, slots = zip(*gather.parts)
    if rows % 16 == 0:
        return pieces, slots, rows
    parts = in_order(jnp.concatenate(pieces)[:, : number * rows], slots, me)
    count, _, width = parts.shape
    parts = jnp.moveaxis(parts.reshape(count, number, rows, width), 1, 0)
    return (parts.reshape(1, number * count * rows, width),), ([0],), count * rows


def matrix_halves(gather, number, rows, side):
    if rows % 16 == 0:
        split = [([], []), ([], [])]
        for piece, order in gather.parts:
            pieces, slots = split[order[0] & 1]
            pieces.append(piece)
            slots.append([at >> 1 for at in order])
        return *split, rows
    pieces, slots = zip(*gather.parts)
    parts = in_order(jnp.concatenate(pieces), slots, side)
    count, width = parts.shape[0] // 2, parts.shape[-1]
    parts = jnp.moveaxis(parts.reshape(count, number, rows, width), 1, 0)
    parts = parts.reshape(1, number * count * rows, width)
    middle = parts.shape[1] // 2
    return ([parts[:, :middle]], [[0]]), ([parts[:, middle:]], [[0]]), count * rows


def in_order(held, slots, me):
    count = held.shape[0]
    distance = jnp.array([at for order in slots for at in order], jnp.int32)
    chosen = (jnp.arange(count, dtype=jnp.int32) ^ me)[:, None] == distance[None]
    return jnp.einsum(
        "ij,jrc->irc", chosen.astype(LOW), held, preferred_element_type=WIDE
    ).astype(LOW)


def to_slots(parts, slots, me):
    count = parts.shape[0]
    bit = 1
    while bit < count:
        pairs = parts.reshape((count // (2 * bit), 2, bit) + parts.shape[1:])
        parts = jnp.where((me & bit) != 0, pairs[:, ::-1], pairs).reshape(parts.shape)
        bit *= 2
    return tuple(
        jnp.concatenate([parts[at : at + 1] for at in distances]) for distances in slots
    )


def sum_order(count):
    bits = count.bit_length() - 2
    order = [
        sum(2 << place for place in range(bits) if at >> (bits - 1 - place) & 1)
        for at in range(count // 2)
    ]
    return order, [at ^ 1 for at in order]


class Sum:
    def __init__(self, keep, send, count, half=False):
        self.terms, self.send, self.count = [(keep, ())], send, count
        self.slots, self.kernel = keep.shape[0], False
        self.half, self.bit, self.total = half, 1, None

    def start(self, *others):
        send = after(self.send, *others) if others else self.send
        if self.half == "now" or self.bit == self.count:
            self.other = lax.ppermute(send, "rep", [(0, 1), (1, 0)])
        else:
            self.other = swap(send, self.bit, self.count)

    def added(self, *cuts):
        total = 0
        for array, before in self.terms:
            for each in (*before, *cuts):
                array = each(array)
            total = total + array.astype(WIDE)
        return total

    def cut(self, each):
        self.terms = [(array, (*before, each)) for array, before in self.terms]

    def land(self, *others):
        other = after(self.other, *others) if others else self.other
        if self.bit == self.count:
            if self.half:
                low = lax.axis_index("rep") == 0
                both = jnp.where(low, self.send, other), jnp.where(low, other, self.send)
                self.total = jnp.concatenate(both, axis=1)[0].astype(WIDE)
            else:
                self.total = (self.send.astype(WIDE) + other.astype(WIDE))[0]
            return self.total
        self.terms.append((other, ()))
        if self.half == "now":
            self.half = "done"
        else:
            self.bit *= 2
            if self.half is True:
                return self.halve()
        if self.bit == self.count:
            self.send = self.added().astype(LOW)
            return self.send
        middle = self.slots // 2
        if self.kernel and self.slots > 1:
            self.send = add_upper([array for array, _ in self.terms])
            self.kernel = False
        else:
            self.send = self.added(lambda term: term[middle:]).astype(LOW)
        self.cut(lambda term: term[:middle])
        self.slots = middle
        return self.send

    def halve(self):
        mine = lax.axis_index("rep")
        _, rows, width = self.send.shape

        def pick(at):
            return lambda term: lax.dynamic_slice_in_dim(term, at * (rows // 2), rows // 2, 1)

        self.send = self.added(pick(1 - mine)).astype(LOW)
        self.cut(pick(mine))
        self.half = "now"
        return self.send

    def finish(self):
        while self.total is None:
            self.start()
            self.land()


def add_kernel(*refs):
    total = 0
    for ref in refs[:-1]:
        total = total + ref[...].astype(WIDE)
    refs[-1][...] = total.astype(LOW)


def add_upper(terms):
    slots, rows, width = terms[0].shape
    upper = pl.BlockSpec((1, rows, width), lambda at: (at + slots // 2, 0, 0))
    return pl.pallas_call(
        add_kernel,
        grid=(slots // 2,),
        in_specs=[upper] * len(terms),
        out_specs=pl.BlockSpec((1, rows, width), lambda at: (at, 0, 0)),
        out_shape=jax.ShapeDtypeStruct((slots // 2, rows, width), LOW),
        compiler_params=params(),
        cost_estimate=cost(12),
        name="add",
    )(*terms)


def joined(sums):
    first = sums[0]
    whole = Sum(first.send, jnp.concatenate([item.send for item in sums], axis=1), first.count)
    whole.bit, whole.slots = first.bit, first.slots
    whole.terms = [(jnp.concatenate([item.added() for item in sums], axis=1), ())]
    return whole


def shards(
    inputs,
    block_kind,
    query_weight,
    query_bias,
    key_weight,
    value_weight,
    value_bias,
    out_weight,
    out_bias,
    attn_gain,
    attn_shift,
    up_weight,
    up_bias,
    down_weight,
    down_bias,
    ffn_gain,
    ffn_shift,
    cotangent,
):
    rows = query_weight.shape[0]
    count = D // rows
    hidden = up_weight.shape[1]
    steps = hidden // TILE
    vectors = (
        query_bias,
        value_bias,
        out_bias,
        attn_gain,
        attn_shift,
        down_bias,
        ffn_gain,
        ffn_shift,
    )
    down_rows = down_weight.shape[0]
    used = 8 * rows + up_bias.shape[0]
    spare = 16 * QUAD
    packed, at = 0, 0
    for value in vectors + (up_bias,):
        packed = packed + jnp.pad(value, (at, spare - at - value.shape[0]))
        at += value.shape[0]
    me = lax.axis_index("fsdp").astype(jnp.int32)
    own_rows = rows % 16 == 0
    mine = me.reshape(1)
    none = jnp.zeros((1,), jnp.int32)
    me_or_none = mine if own_rows else none
    attn_weights = (query_weight, key_weight, value_weight, out_weight)

    first = Gather(
        pack([[(w, 0)] for w in attn_weights] + [[(packed.reshape(16, QUAD), 0)]], QUAD), count
    )
    inputs_t = inputs.T
    first.far()
    at = first.land()
    rest = Gather(pack([[(w, 1), (w, 2)] for w in attn_weights], QUAD), count)
    second = Gather(pack([[(up_weight, at)] for at in range(steps)], TILE), count, half=True)
    rest.far(at)
    at = rest.land(first.far_but(0), second.parts[0][0])
    third = Gather(down_weight, count)
    first.send(0, 2)
    first.send(0, 1)
    rest.far_but(1)
    rest.far()
    second.far(at)
    at = second.land(inputs_t)
    at = rest.land(at)
    at = first.tie(1, at)
    first.send(1, 1)
    rest.send(0, 2)
    rest.send(0, 1)
    second.far_but(1)
    second.far()
    third.far(at)

    pieces, slots = zip(*first.parts)
    columns = -(-used // QUAD)
    whole_packed = in_order(
        jnp.concatenate([piece[:, 4 * rows : 4 * rows + columns] for piece in pieces]), slots, me
    ).reshape(count, columns * QUAD)
    vec = (
        jnp.moveaxis(whole_packed[:, : 8 * rows].reshape(count, 8, rows), 1, 0)
        .reshape(8, D)
        .astype(WIDE)
    )
    all_up_bias = whole_packed[:, 8 * rows : used].reshape(1, hidden).astype(WIDE)

    places = [(0, 0), (1, 0), (1, 1)]
    heads = [
        attend(
            block_kind, me_or_none, [0], inputs, matrices(first, 4, rows, me), after(vec, all_up_bias)
        )
    ]
    at = second.land(heads[0][3])
    second.send(0, 2)
    second.send(0, "rep")
    second.send(0, 1)
    at = third.land(at)
    third.far_but(1)
    third.far()
    at = rest.tie(1, at)
    rest.send(1, 1)
    heads.append(
        attend(
            block_kind, me_or_none, [1, 2], after(inputs, at), matrices(rest, 4, rows, me), vec
        )
    )
    contexts = [group[3] for group in heads]
    contexts_t = [group[4] for group in heads]
    at = second.tie(1, heads[1][3])
    at = second.tie(2, at)
    second.send(1, "rep")
    second.send(1, 1)
    second.send(2, 1)
    at = third.land(at)
    third.send(0, 2)
    third.send(0, 1)
    norm, first_inv, hl, hlt, wo = out_call(
        me_or_none,
        contexts,
        after(inputs, at),
        [matrices(first, 4, rows, me), matrices(rest, 4, rows, me)],
        vec,
    )
    second.tie(4, hl)
    second.send(4, 1)
    rank = lax.axis_index("rep").astype(jnp.int32)
    own, other, block = matrix_halves(second, steps, rows, 2 * me + rank)
    flip = jnp.stack([me, rank * (steps // 2)]) if own_rows else jnp.zeros((2,), jnp.int32)
    act, slope, up = up_call(flip, hl, own, other, block, all_up_bias)
    third.tie(1, act)
    third.send(1, 1)
    pieces = matrices(third, 1, down_rows, me)
    layer_out, grad, low, ffn_sums, down = down_call(
        mine if down_rows % 16 == 0 else none, act, pieces, norm, vec, cotangent
    )

    order = sum_order(count)
    quads = D // QUAD

    def halves_of(keep, send, k, groups=1):
        if own_rows:
            return keep, send
        width = keep.shape[-1]
        tall = keep.shape[1] // groups
        everything = []
        for group in jnp.split(keep[0], groups):
            parts = jnp.moveaxis(group[: k * D].reshape(k, count, rows, width), 0, 1)
            everything.append(parts.reshape(count, k * rows, width))
            everything.append(jnp.broadcast_to(group[None, k * D :], (count, tall - k * D, width)))
        return to_slots(jnp.concatenate(everything, axis=1), order, me)

    kernel_order = order if own_rows else ([0], [])
    if 2 * down_rows % 128 == 0:
        middle = count // 4
        near, far = ([part[at] for part in order] for at in (slice(middle), slice(middle, None)))
        far_keep, far_send = down_grad_call(mine, far, down_rows, act, low)
        far_other = swap(far_send, 1, count)
        near_keep, near_send = down_grad_call(mine, near, down_rows, act, after(low, far_keep))
        sum_down = Sum(near_keep, None, count)
        sum_down.bit, sum_down.slots, sum_down.kernel = 2, middle, True
        far_other = after(far_other, near_keep)
        sum_down.send = (far_keep.astype(WIDE) + far_other.astype(WIDE)).astype(LOW)
        at = sum_down.send
        sum_down.start()
        sum_down.terms.append((swap(near_send, 1, count), ()))
    else:
        parts = down_grad_plain_call(act, low).reshape(count, down_rows, D)
        sum_down = Sum(*to_slots(parts, order, me), count)
        sum_down.start()
        at = sum_down.land()
        sum_down.start()

    keep, send, up_sums, grad_hidden = up_grad_call(
        me_or_none, kernel_order, list(range(steps)), low, down, slope, hlt, up, after(grad, at)
    )
    sum_up = Sum(*halves_of(keep, send, steps), count, half=True)
    sum_up.start()
    at = sum_down.land(grad_hidden)
    sum_down.start()
    at = sum_up.land(at)
    sum_up.start()
    grad_attn, keep, send, grad_ctx = norm_back_call(
        me_or_none, kernel_order, after(grad_hidden, at), norm, first_inv, vec, contexts_t, wo,
        ffn_sums, up_sums,
    )
    sum_out = Sum(*halves_of(keep, send, 1, quads), count)
    sum_out.start()
    at = grad_attn

    def back(quad, slots, *others):
        group, at = places[quad]
        q, k, v, ctx, _, raised, inv, _ = heads[group]
        dq, dk, dv, *rest = attend_back(
            me_or_none, slots, quad, at, inputs_t, after(grad_ctx, *others), ctx, inv, q, k, v, raised
        )
        return (dq, dk, dv), rest

    def back_sum(quad, *others):
        part, (keep, send) = back(quad, kernel_order, *others)
        return part, Sum(*halves_of(keep, send, 3), count)

    part_0, sum_0 = back_sum(0, at)
    sum_0.start()
    at = sum_down.land(part_0[0])
    sum_down.start()
    at = sum_out.land(at)
    at = sum_up.land(at)
    sum_up.start()
    part_1, sum_1 = back_sum(1, at)
    sum_1.start()
    at = sum_0.land(part_1[0])
    sum_0 = joined([sum_out, sum_0])
    sum_0.start()
    at = sum_down.land(at, sum_0.send)
    at = sum_up.land(at)
    sum_up.start()
    if own_rows:
        middle = count // 4
        send_slots = (order[0], order[1][:middle], order[1][middle:])
        part_2, (keep, near_send, far_send) = back(2, send_slots, at)
        near, far = swap(near_send, 1, count), swap(far_send, 1, count)
        at = sum_1.land(part_2[0])
        sum_1.start()
        far = after(far, at)
        sum_2 = Sum(keep, None, count)
        sum_2.bit, sum_2.slots = 2, middle
        sum_2.send = (keep[middle:].astype(WIDE) + far.astype(WIDE)).astype(LOW)
        sum_2.cut(lambda term: term[:middle])
        sum_2.terms.append((near, ()))
        at = sum_2.send
        sum_2.start()
    else:
        part_2, sum_2 = back_sum(2, at)
        sum_2.start()
        at = sum_1.land(part_2[0])
        sum_1.start()
        at = sum_2.land(at)
        sum_2.start()
    at = sum_0.land(at)
    sum_0.start()
    at = sum_1.land(at)
    at = sum_2.land(at)
    sum_1 = joined([sum_1, sum_2])
    sum_1.start()
    at = sum_up.land(sum_1.send)
    sum_up.start()
    at = sum_0.land(at)
    sum_0.start()
    sum_down.start(at)
    weights = [group[7] for group in heads]
    at = input_grad = input_grad_call(
        [part_0, part_1, part_2], places, weights, after(grad_attn, at)
    )
    while sum_1.total is None:
        for item in (sum_1, sum_up, sum_0, sum_down):
            if item.total is None:
                at = item.land(at)
            if item.total is None:
                item.start()
    for item in (sum_0, sum_up, sum_down):
        while item.total is None:
            item.land()
            if item.total is None:
                item.start()
    tall = 3 * rows + EXTRA
    grad_qkv = jnp.concatenate([sum_0.total[-tall:], sum_1.total[:tall], sum_1.total[tall:]], axis=1)
    grad_out = jnp.concatenate(jnp.split(sum_0.total[:-tall], quads), axis=1)
    of_mine = lambda value, size: lax.dynamic_slice_in_dim(value, me * size, size, value.ndim - 1)
    own = of_mine(
        jnp.concatenate([grad_qkv[3 * rows : 3 * rows + 2], grad_out[rows : rows + 6]]), rows
    )
    grad_up_bias = of_mine(grad_out[rows + 6 : rows + 6 + steps].reshape(-1), up_bias.shape[0])
    grad_up = sum_up.total
    return (
        layer_out,
        input_grad,
        grad_qkv[:rows],
        own[QUERY_BIAS],
        grad_qkv[rows : 2 * rows],
        grad_qkv[2 * rows : 3 * rows],
        own[VALUE_BIAS],
        grad_out[:rows],
        own[OUT_BIAS],
        own[ATTN_GAIN],
        own[ATTN_SHIFT],
        jnp.concatenate([grad_up[rows * i : rows * (i + 1)] for i in range(steps)], axis=1),
        grad_up_bias,
        sum_down.total,
        own[DOWN_BIAS],
        own[FFN_GAIN],
        own[FFN_SHIFT],
    )


def solution(mesh):
    tokens = P(("rep", "fsdp"), None)
    matrix = P("fsdp", None)
    vector = P("fsdp")
    params_placed = (
        matrix,
        vector,
        matrix,
        matrix,
        vector,
        matrix,
        vector,
        vector,
        vector,
        matrix,
        vector,
        matrix,
        vector,
        vector,
        vector,
    )
    return jax.shard_map(
        shards,
        mesh=mesh,
        in_specs=(tokens, P(("rep", "fsdp")), *params_placed, tokens),
        out_specs=(tokens, tokens, *params_placed),
        check_vma=False,
    )
```

```python
import functools

import jax
import jax.numpy as jnp
from jax import lax
from jax.experimental import pallas as pl
from jax.experimental.pallas import tpu as pltpu
from jax.sharding import PartitionSpec as P

D = 768
H = 12
HD = 64
LONG = 512
SHORT = 128
QUAD = 256
PAIR = 128
TILE = 768

EPSILON = 1e-05
BLOCKED = -1e30
LOW = jnp.bfloat16
WIDE = jnp.float32
ROOM = 38 << 20
EXTRA = 16

QUERY_BIAS, VALUE_BIAS, OUT_BIAS, ATTN_GAIN, ATTN_SHIFT, DOWN_BIAS, FFN_GAIN, FFN_SHIFT = range(8)


def dot(left, right, left_dim, right_dim):
    return lax.dot_general(
        left, right, (((left_dim,), (right_dim,)), ((), ())), preferred_element_type=WIDE
    )


def row_mean(value):
    return jnp.mean(value, axis=-1, keepdims=True)


def token_sum(value):
    return jnp.sum(value, axis=0, keepdims=True)


def whole(shape):
    zeros = (0,) * len(shape)
    return pl.BlockSpec(shape, lambda *_: zeros, pipeline_mode=pl.Buffered(1))


def place(target, sources, slots, me):
    rows = sources[0].shape[1]
    for source, distances in zip(sources, slots):
        for at, distance in enumerate(distances):
            start = pl.multiple_of((me ^ distance) * rows, rows)
            target[pl.ds(start, rows), :] = source[at]


def far(value):
    return pltpu.with_memory_space_constraint(value, pltpu.HBM)


def params():
    return pltpu.CompilerParams(vmem_limit_bytes=ROOM)


def cost(microseconds):
    return pl.CostEstimate(
        flops=int(microseconds * 1.1e9), bytes_accessed=1 << 20, transcendentals=0
    )


def unplace(targets, source, slots, me, top, rows):
    for target, distances in zip(targets, slots):
        for at, distance in enumerate(distances):
            start = pl.multiple_of((me ^ distance) * rows, rows)
            target[at, top : top + rows, :] = source(pl.ds(start, rows)).astype(LOW)


def to_all(targets, slots, top, rows):
    low = rows.astype(LOW)
    for target, distances in zip(targets, slots):
        for at in range(len(distances)):
            target[at, top : top + EXTRA, :] = low


def half_masks():
    lane = lax.broadcasted_iota(jnp.int32, (1, PAIR), 1)
    return [jnp.where(lane // HD == half, 1.0, 0.0) for half in range(2)]


def attend_kernel(slots, kind_ref, me_ref, x_ref, vec_ref, *refs):
    pieces = len(slots)
    sources, refs = refs[: 3 * pieces], refs[3 * pieces :]
    q_ref, k_ref, v_ref, ctx_ref, ctxt_ref, raised_ref, inv_ref, weight_ref = refs

    @pl.when(pl.program_id(1) == 0)
    def _():
        for at in range(3):
            place(weight_ref.at[at], sources[at * pieces : (at + 1) * pieces], slots, me_ref[0])

    x = x_ref[...]
    q_ref[...] = (dot(x, weight_ref[0], 1, 0) + vec_ref[QUERY_BIAS : QUERY_BIAS + 1]).astype(LOW)
    k_ref[...] = dot(x, weight_ref[1], 1, 0).astype(LOW)
    v_ref[...] = (dot(x, weight_ref[2], 1, 0) + vec_ref[VALUE_BIAS : VALUE_BIAS + 1]).astype(LOW)
    part = lax.broadcasted_iota(jnp.int32, (LONG, PAIR), 0) // SHORT
    lane = lax.broadcasted_iota(jnp.int32, (LONG, PAIR), 1)
    blocked = jnp.where(kind_ref[pl.program_id(1)] == 1, 0.0, BLOCKED)
    query_part = jnp.where((lane < LONG // SHORT) & (part != lane), blocked, 0.0).astype(LOW)
    key_part = jnp.where(part == lane, 1.0, 0.0).astype(LOW)
    halves = half_masks()
    for pair in range(QUAD // PAIR):
        cols = pl.ds(pair * PAIR, PAIR)
        q2 = q_ref[:, cols].astype(WIDE) * HD ** (-0.5)
        keys = jnp.concatenate([k_ref[:, cols], key_part], axis=1)
        v2t = v_ref[:, cols].T
        contexts, inverses = [], []
        for half in range(2):
            queries = jnp.concatenate([(q2 * halves[half]).astype(LOW), query_part], axis=1)
            scores = dot(keys, queries, 1, 1)
            peak = jnp.max(scores, axis=0, keepdims=True)
            raised = jnp.exp(scores - peak).astype(LOW)
            raised_ref[0, pair * 2 + half] = raised
            left = jnp.concatenate(
                [v2t[HD * half : HD * half + HD], jnp.ones((16, LONG), LOW)], axis=0
            )
            mixed = dot(left, raised, 1, 0)
            inverse = 1.0 / mixed[HD : HD + 1]
            contexts.append(mixed[:HD] * inverse)
            inverses.append(jnp.broadcast_to(inverse, (HD, LONG)))
        context = jnp.concatenate(contexts, axis=0)
        ctxt_ref[pair * PAIR : pair * PAIR + PAIR, :] = context.astype(LOW)
        ctx_ref[:, cols] = context.T.astype(LOW)
        inv_ref[:, cols] = jnp.concatenate(inverses, axis=0).T


def attend(kind, me, quads, x, weights, vec):
    pieces, slots, rows = weights
    count = x.shape[0]
    blocks, number, low = count // LONG, len(quads), quads[0]
    tokens = pl.BlockSpec((LONG, QUAD), lambda j, b, *_: (b, j))
    act = pltpu.HBM((count, number * QUAD), LOW)
    return pl.pallas_call(
        functools.partial(attend_kernel, slots),
        grid_spec=pltpu.PrefetchScalarGridSpec(
            num_scalar_prefetch=2,
            grid=(number, blocks),
            in_specs=[
                pl.BlockSpec((LONG, D), lambda j, b, *_: (b, 0)),
                pl.BlockSpec((8, QUAD), lambda j, b, *_: (0, j + low)),
            ]
            + [
                pl.BlockSpec((piece.shape[0], rows, QUAD), lambda j, b, *_, at=at: (0, at, j))
                for at in range(3)
                for piece in pieces
            ],
            out_specs=[
                tokens,
                tokens,
                tokens,
                tokens,
                pl.BlockSpec((QUAD, LONG), lambda j, b, *_: (j, b)),
                pl.BlockSpec((1, QUAD // HD, LONG, LONG), lambda j, b, *_: (b, j, 0, 0)),
                tokens,
                pl.BlockSpec((3, D, QUAD), lambda j, b, *_: (0, 0, j)),
            ],
        ),
        out_shape=[
            act,
            act,
            act,
            act,
            pltpu.HBM((number * QUAD, count), LOW),
            pltpu.HBM((blocks, number * QUAD // HD, LONG, LONG), LOW),
            pltpu.HBM((count, number * QUAD), WIDE),
            pltpu.HBM((3, D, number * QUAD), LOW),
        ],
        compiler_params=params(),
        cost_estimate=cost(0.1),
        name="attend",
    )(kind, me, far(x), far(vec), *(far(piece) for piece in list(pieces) * 3))


def attend_back_kernel(
    slots,
    me_ref,
    xt_ref,
    d_ref,
    ctx_ref,
    inv_ref,
    q_ref,
    k_ref,
    v_ref,
    raised_ref,
    dq_ref,
    dk_ref,
    dv_ref,
    *refs,
):
    targets, (totals, biases) = refs[:-2], refs[-2:]
    block = pl.program_id(0)
    halves = half_masks()
    minus = jnp.full((LONG, PAIR), -1.0, LOW)
    work = []
    for pair in range(QUAD // PAIR):
        cols = pl.ds(pair * PAIR, PAIR)
        d2 = d_ref[:, cols].astype(WIDE) * inv_ref[:, cols] * HD ** (-0.5)
        along = d2 * ctx_ref[:, cols].astype(WIDE)
        q2 = q_ref[:, cols].astype(WIDE)
        values = jnp.concatenate([v_ref[:, cols], minus], axis=1)
        for half in range(2):
            dm = (d2 * halves[half]).astype(LOW)
            am = (along * halves[half]).astype(LOW)
            qm = (q2 * halves[half]).astype(LOW)
            dp = dot(values, jnp.concatenate([dm, am], axis=1), 1, 1)
            work.append((pair, half, dm, qm, dp))
    k2ts = [k_ref[:, pl.ds(pair * PAIR, PAIR)].T for pair in range(QUAD // PAIR)]
    done = []
    for pair, half, dm, qm, dp in work:
        raised = raised_ref[0, pair * 2 + half]
        ds = (raised.astype(WIDE) * dp).astype(LOW)
        done.append((pair, half, raised, ds, dm, qm))
    for pair in range(QUAD // PAIR):
        cols = pl.ds(pair * PAIR, PAIR)
        dqt, dk, dv = [], 0, 0
        for p, half, raised, ds, dm, qm in done:
            if p == pair:
                dqt.append(dot(k2ts[pair][HD * half : HD * half + HD], ds, 1, 0))
        both = [item for item in done if item[0] == pair]
        wide = lambda at, axis: jnp.concatenate([item[at] for item in both], axis=axis)
        dv = dot(wide(2, 1), wide(4, 0), 1, 0)
        dk = dot(wide(3, 1), wide(5, 0), 1, 0)
        dv_ref[:, cols] = (dv * HD**0.5).astype(LOW)
        dk_ref[:, cols] = dk.astype(LOW)
        dq_ref[:, cols] = jnp.concatenate(dqt, axis=0).T.astype(LOW)
    xt = xt_ref[...]
    for at, ref in enumerate((dq_ref, dk_ref, dv_ref)):
        grad = dot(xt, ref[...], 1, 0)

        @pl.when(block == 0)
        def _(grad=grad, at=at):
            totals[at] = grad

        @pl.when(block != 0)
        def _(grad=grad, at=at):
            totals[at] += grad

    sums = jnp.concatenate(
        [
            token_sum(dq_ref[...].astype(WIDE)),
            token_sum(dv_ref[...].astype(WIDE)),
            jnp.zeros((EXTRA - 2, QUAD), WIDE),
        ],
        axis=0,
    )

    @pl.when(block == 0)
    def _():
        biases[...] = sums

    @pl.when(block != 0)
    def _():
        biases[...] += sums

    @pl.when(block == pl.num_programs(0) - 1)
    def _():
        rows = (targets[0].shape[1] - EXTRA) // 3
        for at in range(3):
            unplace(
                targets, lambda part, at=at: totals[at, part], slots, me_ref[0], at * rows, rows
            )
        to_all(targets, slots, 3 * rows, biases[...])


def attend_back(me, slots, quad, at, xt, d, ctx, inv, q, k, v, raised):
    count = q.shape[0]
    tokens = pl.BlockSpec((LONG, QUAD), lambda b, *_: (b, at))
    grads = pl.BlockSpec((LONG, QUAD), lambda b, *_: (b, 0))
    act = pltpu.HBM((count, QUAD), LOW)
    rows = D // sum(map(len, slots))
    halves = [(max(len(part), 1), 3 * rows + EXTRA, QUAD) for part in slots]
    return pl.pallas_call(
        functools.partial(attend_back_kernel, slots),
        grid_spec=pltpu.PrefetchScalarGridSpec(
            num_scalar_prefetch=1,
            grid=(count // LONG,),
            in_specs=[
                pl.BlockSpec((D, LONG), lambda b, *_: (0, b)),
                pl.BlockSpec((LONG, QUAD), lambda b, *_: (b, quad)),
            ]
            + [tokens] * 5
            + [pl.BlockSpec((1, QUAD // HD, LONG, LONG), lambda b, *_: (b, at, 0, 0))],
            out_specs=[grads, grads, grads] + [whole(half) for half in halves],
            scratch_shapes=[pltpu.VMEM((3, D, QUAD), WIDE), pltpu.VMEM((EXTRA, QUAD), WIDE)],
        ),
        out_shape=[act, act, act] + [pltpu.HBM(half, LOW) for half in halves],
        compiler_params=params(),
        cost_estimate=cost(2),
        name="attend_back",
    )(
        me, far(xt), d, *(value if quad else far(value) for value in (ctx, inv, q, k, v)), far(raised)
    )


def out_kernel(places, groups, me_ref, x_ref, vec_ref, *refs):
    contexts, refs = refs[:groups], refs[groups:]
    norm_ref, inv_ref, hl_ref, hlt_ref, wo_ref = refs[-5:]
    at, col = 0, 0
    for slots in places:
        sources = refs[at : at + len(slots)]
        at += len(slots)
        width = sources[0].shape[2]
        place(wo_ref.at[:, col : col + width], sources, slots, me_ref[0])
        col += width
    bias = vec_ref[OUT_BIAS : OUT_BIAS + 1]
    gain = vec_ref[ATTN_GAIN : ATTN_GAIN + 1]
    shift = vec_ref[ATTN_SHIFT : ATTN_SHIFT + 1]
    wo = wo_ref[...]
    step = 256
    for at in range(0, x_ref.shape[0], step):
        rows = pl.ds(at, step)
        context = jnp.concatenate([ref[rows] for ref in contexts], axis=1)
        total = x_ref[rows].astype(WIDE) + dot(context, wo, 1, 0) + bias
        centered = total - row_mean(total)
        inverse = lax.rsqrt(row_mean(centered * centered) + EPSILON)
        norm = centered * inverse
        norm_ref[rows] = norm
        inv_ref[rows] = jnp.broadcast_to(inverse, (step, 128))
        hidden = (norm * gain + shift).astype(LOW)
        hl_ref[rows] = hidden
        hlt_ref[:, rows] = hidden.T


def out_call(me, contexts, x, weights, vec):
    count = x.shape[0]
    specs, values = [], []
    for pieces, _, rows in weights:
        for piece in pieces:
            specs.append(pl.BlockSpec((piece.shape[0], rows, piece.shape[2]), lambda *_: (0, 3, 0)))
            values.append(piece)
    shapes = [((count, D), WIDE), ((count, 128), WIDE), ((count, D), LOW), ((D, count), LOW), ((D, D), LOW)]
    outs = [pltpu.HBM(shape, dtype) for shape, dtype in shapes]
    outs[2] = jax.ShapeDtypeStruct(*shapes[2])
    return pl.pallas_call(
        functools.partial(out_kernel, [slots for _, slots, _ in weights], len(contexts)),
        grid_spec=pltpu.PrefetchScalarGridSpec(
            num_scalar_prefetch=1,
            grid=(1,),
            in_specs=[whole((count, D)), whole((8, D))]
            + [whole(context.shape) for context in contexts]
            + specs,
            out_specs=[whole(shape) for shape, _ in shapes],
        ),
        out_shape=outs,
        compiler_params=params(),
        cost_estimate=cost(0.1),
        name="out",
    )(me, *(far(value) for value in (x, vec, *contexts, *values)))


def up_kernel(slots, me_ref, hl_ref, bu_ref, *refs):
    own, other = slots
    ups, (act_ref, slope_ref, wu_ref) = refs[:-3], refs[-3:]
    step = 256
    first_half = pl.program_id(0) < pl.num_programs(0) // 2

    @pl.when(first_half)
    def _():
        place(wu_ref.at[0], ups[: len(own)], own, me_ref[0])

    @pl.when(jnp.logical_not(first_half))
    def _():
        place(wu_ref.at[0], ups[len(own) :], other, me_ref[0])

    bias = bu_ref[...]
    weight = wu_ref[0]
    for at in range(0, hl_ref.shape[0], step):
        rows = pl.ds(at, step)
        before = dot(hl_ref[rows], weight, 1, 0) + bias
        half = 0.5 * (1.0 + lax.erf(before * 0.7071067811865476))
        act_ref[rows] = (before * half).astype(LOW)
        slope_ref[rows] = (
            half + before * jnp.exp(-0.5 * before * before) * 0.3989422804014327
        ).astype(LOW)


def up_call(me, hl, own, other, rows, up_bias):
    count = hl.shape[0]
    hidden = up_bias.shape[1]
    steps = hidden // TILE
    half = steps // 2
    cols = lambda r: pl.BlockSpec((r, TILE), lambda j, me: (0, j ^ me[1]))
    early = lambda j, *_: (0, jnp.minimum(j, half - 1), 0)
    late = lambda j, *_: (0, jnp.maximum(j - half, 0), 0)
    return pl.pallas_call(
        functools.partial(up_kernel, (own[1], other[1])),
        grid_spec=pltpu.PrefetchScalarGridSpec(
            num_scalar_prefetch=1,
            grid=(steps,),
            in_specs=[whole((count, D)), cols(1)]
            + [pl.BlockSpec((piece.shape[0], rows, D), early) for piece in own[0]]
            + [pl.BlockSpec((piece.shape[0], rows, D), late) for piece in other[0]],
            out_specs=[
                cols(count),
                cols(count),
                pl.BlockSpec((1, D, TILE), lambda j, me: (j ^ me[1], 0, 0)),
            ],
        ),
        out_shape=[
            jax.ShapeDtypeStruct((count, hidden), LOW),
            pltpu.HBM((count, hidden), LOW),
            pltpu.HBM((steps, D, TILE), LOW),
        ],
        compiler_params=params(),
        cost_estimate=cost(0.1),
        name="up",
    )(me, hl, *(far(value) for value in (up_bias, *own[0], *other[0])))


def down_kernel(slots, me_ref, act_ref, norm_ref, vec_ref, cot_ref, *refs):
    sources = refs[: len(slots)]
    out_ref, grad_ref, low_ref, sums_ref, wd_ref = refs[len(slots) :]

    @pl.when(pl.program_id(0) == 0)
    def _():
        place(wd_ref, sources, slots, me_ref[0])

    row = lambda at: vec_ref[at : at + 1]
    total = (
        norm_ref[...] * row(ATTN_GAIN)
        + row(ATTN_SHIFT)
        + (dot(act_ref[...], wd_ref[...], 1, 0) + row(DOWN_BIAS))
    )
    centered = total - row_mean(total)
    inverse = lax.rsqrt(row_mean(centered * centered) + EPSILON)
    norm = centered * inverse
    out_ref[...] = (norm * row(FFN_GAIN) + row(FFN_SHIFT)).astype(LOW)
    grad_out = cot_ref[...].astype(WIDE)
    scaled = grad_out * row(FFN_GAIN)
    grad = inverse * (scaled - row_mean(scaled) - norm * row_mean(scaled * norm))
    grad_ref[...] = grad
    low = grad.astype(LOW)
    low_ref[...] = low
    sums = jnp.concatenate(
        [
            token_sum(grad_out * norm),
            token_sum(grad_out),
            token_sum(low.astype(WIDE)),
            jnp.zeros((5, D), WIDE),
        ],
        axis=0,
    )

    @pl.when(pl.program_id(0) == 0)
    def _():
        sums_ref[...] = sums

    @pl.when(pl.program_id(0) != 0)
    def _():
        sums_ref[...] += sums


def down_call(me, act, third, norm, vec, cotangent):
    pieces, slots, _ = third
    count, hidden = act.shape
    tile = 256
    rows = lambda c: pl.BlockSpec((tile, c), lambda i, *_: (i, 0))
    return pl.pallas_call(
        functools.partial(down_kernel, slots),
        grid_spec=pltpu.PrefetchScalarGridSpec(
            num_scalar_prefetch=1,
            grid=(count // tile,),
            in_specs=[rows(hidden), rows(D), whole((8, D)), rows(D)]
            + [whole(piece.shape) for piece in pieces],
            out_specs=[rows(D), rows(D), rows(D), whole((8, D)), whole((hidden, D))],
        ),
        out_shape=[
            pltpu.HBM((count, D), LOW),
            jax.ShapeDtypeStruct((count, D), WIDE),
            jax.ShapeDtypeStruct((count, D), LOW),
            pltpu.HBM((8, D), WIDE),
            pltpu.HBM((hidden, D), LOW),
        ],
        compiler_params=params(),
        cost_estimate=cost(13),
        name="down",
    )(me, act, *(far(value) for value in (norm, vec, cotangent, *pieces)))


def down_grad_kernel(owner_ref, me_ref, act_ref, low_ref, keep_ref, send_ref, scratch):
    rows = keep_ref.shape[1]
    scratch[...] = dot(act_ref[...], low_ref[...], 0, 0).astype(LOW)
    mine = lax.rem(me_ref[0], 2) * rows
    keep_ref[0] = scratch[pl.ds(pl.multiple_of(mine, rows), rows)]
    send_ref[0] = scratch[pl.ds(pl.multiple_of(rows - mine, rows), rows)]


def down_grad_plain_kernel(act_ref, low_ref, grad_ref):
    grad_ref[...] = dot(act_ref[...], low_ref[...], 0, 0).astype(LOW)


def down_grad_plain_call(act, low):
    count, hidden = act.shape
    return pl.pallas_call(
        down_grad_plain_kernel,
        grid=(hidden // TILE,),
        in_specs=[pl.BlockSpec((count, TILE), lambda j: (0, j)), whole((count, D))],
        out_specs=pl.BlockSpec((TILE, D), lambda j: (j, 0)),
        out_shape=pltpu.HBM((hidden, D), LOW),
        compiler_params=params(),
        cost_estimate=cost(9),
        name="down_grad",
    )(act, low)


def down_grad_call(me, slots, rows, act, low):
    count, hidden = act.shape
    number = len(slots[0])
    pair = 2 * rows
    owners = (me // 2) ^ (jnp.array(slots[0], jnp.int32) // 2)
    part = pl.BlockSpec((1, rows, D), lambda j, *_: (j, 0, 0))
    half = pltpu.HBM((number, rows, D), LOW)
    return pl.pallas_call(
        down_grad_kernel,
        grid_spec=pltpu.PrefetchScalarGridSpec(
            num_scalar_prefetch=2,
            grid=(number,),
            in_specs=[
                pl.BlockSpec((count, pair), lambda j, owner, _: (0, owner[j])),
                whole((count, D)),
            ],
            out_specs=[part, part],
            scratch_shapes=[pltpu.VMEM((pair, D), LOW)],
        ),
        out_shape=[half, half],
        compiler_params=params(),
        cost_estimate=cost(number),
        name="down_grad",
    )(owners, me, act, low)


def up_grad_kernel(
    slots, me_ref, low_ref, wd_ref, slope_ref, hlt_ref, wu_ref, grad_ref,
    keep_ref, send_ref, bias_ref, hidden_ref, before_scr, grad_scr,
):
    step = pl.program_id(0)
    before_scr[...] = (dot(low_ref[...], wd_ref[...], 1, 1) * slope_ref[...].astype(WIDE)).astype(
        LOW
    )
    before = before_scr[...]
    grad_scr[...] = dot(hlt_ref[...], before, 1, 0).astype(LOW)
    unplace(
        (keep_ref, send_ref), lambda part: grad_scr[part], slots, me_ref[0], 0, keep_ref.shape[1]
    )
    bias_ref[...] = jnp.broadcast_to(token_sum(before.astype(WIDE)), (8, TILE))
    back = dot(before, wu_ref[0], 1, 1)

    @pl.when(step == 0)
    def _():
        hidden_ref[...] = back + grad_ref[...]

    @pl.when(step != 0)
    def _():
        hidden_ref[...] += back


def up_grad_call(me, slots, tiles, low, down, slope, hlt, up, grad):
    count = slope.shape[0]
    first, steps = tiles[0], len(tiles)
    kept, rows = len(slots[0]), D // (len(slots[0]) + len(slots[1]))
    part = pl.BlockSpec((kept, rows, TILE), lambda j, *_: (0, j, 0))
    half = pltpu.HBM((kept, steps * rows, TILE), LOW)
    return pl.pallas_call(
        functools.partial(up_grad_kernel, slots),
        grid_spec=pltpu.PrefetchScalarGridSpec(
            num_scalar_prefetch=1,
            grid=(steps,),
            in_specs=[
                whole((count, D)),
                pl.BlockSpec((TILE, D), lambda j, *_: (j + first, 0)),
                pl.BlockSpec((count, TILE), lambda j, *_: (0, j + first)),
                whole((D, count)),
                pl.BlockSpec((1, D, TILE), lambda j, *_: (j + first, 0, 0)),
                whole((count, D)),
            ],
            out_specs=[
                part,
                part,
                pl.BlockSpec((8, TILE), lambda j, *_: (j, 0)),
                whole((count, D)),
            ],
            scratch_shapes=[pltpu.VMEM((count, TILE), LOW), pltpu.VMEM((D, TILE), LOW)],
        ),
        out_shape=[
            half,
            half,
            pltpu.HBM((8 * steps, TILE), WIDE),
            jax.ShapeDtypeStruct((count, D), WIDE),
        ],
        compiler_params=params(),
        cost_estimate=cost(6 * steps),
        name="up_grad",
    )(me, low, far(down), far(slope), hlt, far(up), grad)


def norm_back_kernel(
    slots, groups, me_ref, hidden_ref, norm_ref, inv_ref, vec_ref, wo_ref, ffn_ref, up_ref, *refs
):
    contexts, refs = refs[:groups], refs[groups:]
    grad_ref, keep_ref, send_ref, ctx_ref, low_scr, out_scr = refs
    count = hidden_ref.shape[0]
    step = 256
    gain = vec_ref[ATTN_GAIN : ATTN_GAIN + 1]
    wo = wo_ref[...]
    sums = 0
    for at in range(0, count, step):
        rows = pl.ds(at, step)
        hidden = hidden_ref[rows]
        norm = norm_ref[rows]
        scaled = hidden * gain
        grad = inv_ref[rows][:, 0:1] * (
            scaled - row_mean(scaled) - norm * row_mean(scaled * norm)
        )
        grad_ref[rows] = grad
        low = grad.astype(LOW)
        low_scr[rows] = low
        sums = sums + jnp.concatenate(
            [
                token_sum(hidden * norm),
                token_sum(hidden),
                token_sum(low.astype(WIDE)),
                jnp.zeros((5, D), WIDE),
            ],
            axis=0,
        )
        ctx_ref[rows] = dot(low, wo, 1, 1).astype(LOW)
    at = 0
    for ref in contexts:
        out_scr[at : at + ref.shape[0], :] = dot(ref[...], low_scr[...], 1, 0).astype(LOW)
        at += ref.shape[0]
    quads = D // QUAD
    rows = keep_ref.shape[1] // quads - EXTRA
    steps = up_ref.shape[0] // 8
    extra = [sums[2:3], sums[:2], ffn_ref[2:3], ffn_ref[:2]]
    extra += [up_ref[8 * at : 8 * at + 1] for at in range(steps)]
    extra.append(jnp.zeros((EXTRA - 6 - steps, D), WIDE))
    extra = jnp.concatenate(extra, axis=0)
    for quad in range(quads):
        cols = slice(quad * QUAD, quad * QUAD + QUAD)
        top = quad * (rows + EXTRA)
        targets = keep_ref, send_ref
        unplace(targets, lambda part: out_scr[part, cols], slots, me_ref[0], top, rows)
        to_all(targets, slots, top + rows, extra[:, cols])


def norm_back_call(me, slots, hidden, norm, inv, vec, contexts, wo, ffn_sums, up_sums):
    count = hidden.shape[0]
    kept, rows = len(slots[0]), D // (len(slots[0]) + len(slots[1]))
    half = (kept, (rows + EXTRA) * (D // QUAD), QUAD)
    return pl.pallas_call(
        functools.partial(norm_back_kernel, slots, len(contexts)),
        grid_spec=pltpu.PrefetchScalarGridSpec(
            num_scalar_prefetch=1,
            grid=(1,),
            in_specs=[
                whole((count, D)),
                whole((count, D)),
                whole((count, 128)),
                whole((8, D)),
                whole((D, D)),
                whole((8, D)),
                whole(up_sums.shape),
            ]
            + [whole(context.shape) for context in contexts],
            out_specs=[whole((count, D)), whole(half), whole(half), whole((count, D))],
            scratch_shapes=[pltpu.VMEM((count, D), LOW), pltpu.VMEM((D, D), LOW)],
        ),
        out_shape=[
            pltpu.HBM((count, D), WIDE),
            pltpu.HBM(half, LOW),
            pltpu.HBM(half, LOW),
            jax.ShapeDtypeStruct((count, D), LOW),
        ],
        compiler_params=params(),
        cost_estimate=cost(12),
        name="norm_back",
    )(me, hidden, norm, inv, far(vec), wo, far(ffn_sums), far(up_sums), *contexts)


def input_grad_kernel(places, groups, grad_ref, *refs):
    weights, refs = refs[:groups], refs[groups:]
    total = grad_ref[...]
    for quad, (group, at) in enumerate(places):
        for matrix in range(3):
            total = total + dot(
                refs[3 * quad + matrix][...],
                weights[group][matrix, :, at * QUAD : at * QUAD + QUAD],
                1,
                1,
            )
    refs[-1][...] = total


def input_grad_call(pieces, places, weights, grad):
    count = grad.shape[0]
    tile = 512
    tokens = lambda width: pl.BlockSpec((tile, width), lambda i: (i, 0))
    values = [value for piece in pieces for value in piece]
    return pl.pallas_call(
        functools.partial(input_grad_kernel, places, len(weights)),
        grid=(count // tile,),
        in_specs=[tokens(D)]
        + [whole(weight.shape) for weight in weights]
        + [tokens(QUAD) for _ in values],
        out_specs=tokens(D),
        out_shape=pltpu.HBM((count, D), WIDE),
        compiler_params=params(),
        cost_estimate=cost(0.1),
        name="input_grad",
    )(*(far(value) for value in (grad, *weights, *values)))


def pack_kernel(places, *refs):
    for ref, (row, col) in zip(refs, places):
        refs[-1][row : row + ref.shape[0], col : col + ref.shape[1]] = ref[...]


def pack(parts, width):
    if any(array.shape[0] % 16 for line in parts for array, _ in line):
        return jnp.concatenate(
            [
                jnp.concatenate([a[:, width * at : width * (at + 1)] for a, at in line], axis=1)
                for line in parts
            ]
        )
    places, specs, row = [], [], 0
    for line in parts:
        for at, (array, block) in enumerate(line):
            places.append((row, at * width))
            specs.append(pl.BlockSpec((array.shape[0], width), lambda i, block=block: (0, block)))
        row += line[0][0].shape[0]
    shape = (row, width * len(parts[0]))
    return pl.pallas_call(
        functools.partial(pack_kernel, places),
        grid=(1,),
        in_specs=specs,
        out_specs=pl.BlockSpec(shape, lambda i: (0, 0)),
        out_shape=pltpu.HBM(shape, LOW),
        compiler_params=params(),
        cost_estimate=cost(1),
        name="pack",
    )(*(far(array) for line in parts for array, _ in line))


def swap(value, mask, count):
    return lax.ppermute(value, "fsdp", [(i, i ^ mask) for i in range(count)])


def after(value, *others):
    return lax.optimization_barrier((value,) + others)[0] if others else value


class Gather:
    def __init__(self, piece, count, half=False):
        self.unit = 1
        if half:
            rows = piece.shape[0] // 2
            piece = lax.dynamic_slice_in_dim(piece, lax.axis_index("rep") * rows, rows, 0)
            self.unit = 2
        self.parts, self.count = [(piece[None], [0])], count
        self.hops = [count >> at for at in range(1, count.bit_length() - 2)]

    def far(self, *others):
        held, _ = self.parts[0]
        self.other = swap(after(held, *others), self.hops[0], self.count)

    def land(self, *others):
        held, order = self.parts[0]
        held = jnp.concatenate([held, after(self.other, *others)], axis=0)
        mask = self.hops.pop(0) * self.unit
        self.parts = [(held, order + [at ^ mask for at in order])]
        return held

    def far_but(self, last):
        while len(self.hops) > last:
            self.far()
            self.land()
        return self.parts[0][0]

    def send(self, part, hop):
        held, order = self.parts[part]
        if hop == "rep":
            other, mask = lax.ppermute(held, "rep", [(0, 1), (1, 0)]), 1
        else:
            other, mask = swap(held, hop, self.count), hop * self.unit
        self.parts.append((other, [at ^ mask for at in order]))

    def tie(self, part, *others):
        held, order = self.parts[part]
        self.parts[part] = (after(held, *others), order)
        return self.parts[part][0]


def matrices(gather, number, rows, me):
    pieces, slots = zip(*gather.parts)
    if rows % 16 == 0:
        return pieces, slots, rows
    parts = in_order(jnp.concatenate(pieces)[:, : number * rows], slots, me)
    count, _, width = parts.shape
    parts = jnp.moveaxis(parts.reshape(count, number, rows, width), 1, 0)
    return (parts.reshape(1, number * count * rows, width),), ([0],), count * rows


def matrix_halves(gather, number, rows, side):
    if rows % 16 == 0:
        split = [([], []), ([], [])]
        for piece, order in gather.parts:
            pieces, slots = split[order[0] & 1]
            pieces.append(piece)
            slots.append([at >> 1 for at in order])
        return *split, rows
    pieces, slots = zip(*gather.parts)
    parts = in_order(jnp.concatenate(pieces), slots, side)
    count, width = parts.shape[0] // 2, parts.shape[-1]
    parts = jnp.moveaxis(parts.reshape(count, number, rows, width), 1, 0)
    parts = parts.reshape(1, number * count * rows, width)
    middle = parts.shape[1] // 2
    return ([parts[:, :middle]], [[0]]), ([parts[:, middle:]], [[0]]), count * rows


def in_order(held, slots, me):
    count = held.shape[0]
    distance = jnp.array([at for order in slots for at in order], jnp.int32)
    chosen = (jnp.arange(count, dtype=jnp.int32) ^ me)[:, None] == distance[None]
    return jnp.einsum(
        "ij,jrc->irc", chosen.astype(LOW), held, preferred_element_type=WIDE
    ).astype(LOW)


def to_slots(parts, slots, me):
    count = parts.shape[0]
    bit = 1
    while bit < count:
        pairs = parts.reshape((count // (2 * bit), 2, bit) + parts.shape[1:])
        parts = jnp.where((me & bit) != 0, pairs[:, ::-1], pairs).reshape(parts.shape)
        bit *= 2
    return tuple(
        jnp.concatenate([parts[at : at + 1] for at in distances]) for distances in slots
    )


def sum_order(count):
    bits = count.bit_length() - 2
    order = [
        sum(2 << place for place in range(bits) if at >> (bits - 1 - place) & 1)
        for at in range(count // 2)
    ]
    return order, [at ^ 1 for at in order]


class Sum:
    def __init__(self, keep, send, count, half=False):
        self.terms, self.send, self.count = [(keep, ())], send, count
        self.slots, self.kernel = keep.shape[0], False
        self.half, self.bit, self.total = half, 1, None

    def start(self, *others):
        send = after(self.send, *others) if others else self.send
        if self.half == "now" or self.bit == self.count:
            self.other = lax.ppermute(send, "rep", [(0, 1), (1, 0)])
        else:
            self.other = swap(send, self.bit, self.count)

    def added(self, *cuts):
        total = 0
        for array, before in self.terms:
            for each in (*before, *cuts):
                array = each(array)
            total = total + array.astype(WIDE)
        return total

    def cut(self, each):
        self.terms = [(array, (*before, each)) for array, before in self.terms]

    def land(self, *others):
        other = after(self.other, *others) if others else self.other
        if self.bit == self.count:
            if self.half:
                low = lax.axis_index("rep") == 0
                both = jnp.where(low, self.send, other), jnp.where(low, other, self.send)
                self.total = jnp.concatenate(both, axis=1)[0].astype(WIDE)
            else:
                self.total = (self.send.astype(WIDE) + other.astype(WIDE))[0]
            return self.total
        self.terms.append((other, ()))
        if self.half == "now":
            self.half = "done"
        else:
            self.bit *= 2
            if self.half is True:
                return self.halve()
        if self.bit == self.count:
            self.send = self.added().astype(LOW)
            return self.send
        middle = self.slots // 2
        if self.kernel and self.slots > 1:
            self.send = add_upper([array for array, _ in self.terms])
            self.kernel = False
        else:
            self.send = self.added(lambda term: term[middle:]).astype(LOW)
        self.cut(lambda term: term[:middle])
        self.slots = middle
        return self.send

    def halve(self):
        mine = lax.axis_index("rep")
        _, rows, width = self.send.shape

        def pick(at):
            return lambda term: lax.dynamic_slice_in_dim(term, at * (rows // 2), rows // 2, 1)

        self.send = self.added(pick(1 - mine)).astype(LOW)
        self.cut(pick(mine))
        self.half = "now"
        return self.send

    def finish(self):
        while self.total is None:
            self.start()
            self.land()


def add_kernel(*refs):
    total = 0
    for ref in refs[:-1]:
        total = total + ref[...].astype(WIDE)
    refs[-1][...] = total.astype(LOW)


def add_upper(terms):
    slots, rows, width = terms[0].shape
    upper = pl.BlockSpec((1, rows, width), lambda at: (at + slots // 2, 0, 0))
    return pl.pallas_call(
        add_kernel,
        grid=(slots // 2,),
        in_specs=[upper] * len(terms),
        out_specs=pl.BlockSpec((1, rows, width), lambda at: (at, 0, 0)),
        out_shape=pltpu.HBM((slots // 2, rows, width), LOW),
        compiler_params=params(),
        cost_estimate=cost(12),
        name="add",
    )(*(far(term) for term in terms))


def joined(sums):
    first = sums[0]
    whole = Sum(first.send, jnp.concatenate([item.send for item in sums], axis=1), first.count)
    whole.bit, whole.slots = first.bit, first.slots
    whole.terms = [(jnp.concatenate([item.added() for item in sums], axis=1), ())]
    return whole


def shards(
    inputs,
    block_kind,
    query_weight,
    query_bias,
    key_weight,
    value_weight,
    value_bias,
    out_weight,
    out_bias,
    attn_gain,
    attn_shift,
    up_weight,
    up_bias,
    down_weight,
    down_bias,
    ffn_gain,
    ffn_shift,
    cotangent,
):
    rows = query_weight.shape[0]
    count = D // rows
    hidden = up_weight.shape[1]
    steps = hidden // TILE
    vectors = (
        query_bias,
        value_bias,
        out_bias,
        attn_gain,
        attn_shift,
        down_bias,
        ffn_gain,
        ffn_shift,
    )
    down_rows = down_weight.shape[0]
    used = 8 * rows + up_bias.shape[0]
    spare = 16 * QUAD
    packed, at = 0, 0
    for value in vectors + (up_bias,):
        packed = packed + jnp.pad(value, (at, spare - at - value.shape[0]))
        at += value.shape[0]
    me = lax.axis_index("fsdp").astype(jnp.int32)
    own_rows = rows % 16 == 0
    mine = me.reshape(1)
    none = jnp.zeros((1,), jnp.int32)
    me_or_none = mine if own_rows else none
    attn_weights = (query_weight, key_weight, value_weight, out_weight)

    first = Gather(
        pack([[(w, 0)] for w in attn_weights] + [[(packed.reshape(16, QUAD), 0)]], QUAD), count
    )
    inputs_t = inputs.T
    first.far()
    at = first.land()
    rest = Gather(pack([[(w, 1), (w, 2)] for w in attn_weights], QUAD), count)
    second = Gather(pack([[(up_weight, at)] for at in range(steps)], TILE), count, half=True)
    rest.far(at)
    at = rest.land(first.far_but(0), second.parts[0][0])
    third = Gather(down_weight, count)
    first.send(0, 2)
    first.send(0, 1)
    rest.far_but(1)
    rest.far()
    second.far(at)
    at = second.land(inputs_t)
    at = rest.land(at)
    at = first.tie(1, at)
    first.send(1, 1)
    rest.send(0, 2)
    rest.send(0, 1)
    second.far_but(1)
    second.far()
    third.far(at)

    pieces, slots = zip(*first.parts)
    columns = -(-used // QUAD)
    whole_packed = in_order(
        jnp.concatenate([piece[:, 4 * rows : 4 * rows + columns] for piece in pieces]), slots, me
    ).reshape(count, columns * QUAD)
    vec = (
        jnp.moveaxis(whole_packed[:, : 8 * rows].reshape(count, 8, rows), 1, 0)
        .reshape(8, D)
        .astype(WIDE)
    )
    all_up_bias = whole_packed[:, 8 * rows : used].reshape(1, hidden).astype(WIDE)

    places = [(0, 0), (1, 0), (1, 1)]
    heads = [
        attend(
            block_kind, me_or_none, [0], inputs, matrices(first, 4, rows, me), after(vec, all_up_bias)
        )
    ]
    at = second.land(heads[0][3])
    second.send(0, 2)
    second.send(0, "rep")
    second.send(0, 1)
    at = third.land(at)
    third.far_but(1)
    third.far()
    at = rest.tie(1, at)
    rest.send(1, 1)
    heads.append(
        attend(
            block_kind, me_or_none, [1, 2], after(inputs, at), matrices(rest, 4, rows, me), vec
        )
    )
    contexts = [group[3] for group in heads]
    contexts_t = [group[4] for group in heads]
    at = second.tie(1, heads[1][3])
    at = second.tie(2, at)
    second.send(1, "rep")
    second.send(1, 1)
    second.send(2, 1)
    at = third.land(at)
    third.send(0, 2)
    third.send(0, 1)
    norm, first_inv, hl, hlt, wo = out_call(
        me_or_none,
        contexts,
        after(inputs, at),
        [matrices(first, 4, rows, me), matrices(rest, 4, rows, me)],
        vec,
    )
    second.tie(4, hl)
    second.send(4, 1)
    rank = lax.axis_index("rep").astype(jnp.int32)
    own, other, block = matrix_halves(second, steps, rows, 2 * me + rank)
    flip = jnp.stack([me, rank * (steps // 2)]) if own_rows else jnp.zeros((2,), jnp.int32)
    act, slope, up = up_call(flip, hl, own, other, block, all_up_bias)
    third.tie(1, act)
    third.send(1, 1)
    pieces = matrices(third, 1, down_rows, me)
    layer_out, grad, low, ffn_sums, down = down_call(
        mine if down_rows % 16 == 0 else none, act, pieces, norm, vec, cotangent
    )

    order = sum_order(count)
    quads = D // QUAD

    def halves_of(keep, send, k, groups=1):
        if own_rows:
            return keep, send
        width = keep.shape[-1]
        tall = keep.shape[1] // groups
        everything = []
        for group in jnp.split(keep[0], groups):
            parts = jnp.moveaxis(group[: k * D].reshape(k, count, rows, width), 0, 1)
            everything.append(parts.reshape(count, k * rows, width))
            everything.append(jnp.broadcast_to(group[None, k * D :], (count, tall - k * D, width)))
        return to_slots(jnp.concatenate(everything, axis=1), order, me)

    kernel_order = order if own_rows else ([0], [])
    if 2 * down_rows % 128 == 0:
        middle = count // 4
        near, far = ([part[at] for part in order] for at in (slice(middle), slice(middle, None)))
        far_keep, far_send = down_grad_call(mine, far, down_rows, act, low)
        far_other = swap(far_send, 1, count)
        near_keep, near_send = down_grad_call(mine, near, down_rows, act, after(low, far_keep))
        sum_down = Sum(near_keep, None, count)
        sum_down.bit, sum_down.slots, sum_down.kernel = 2, middle, True
        far_other = after(far_other, near_keep)
        sum_down.send = (far_keep.astype(WIDE) + far_other.astype(WIDE)).astype(LOW)
        at = sum_down.send
        sum_down.start()
        sum_down.terms.append((swap(near_send, 1, count), ()))
    else:
        parts = down_grad_plain_call(act, low).reshape(count, down_rows, D)
        sum_down = Sum(*to_slots(parts, order, me), count)
        sum_down.start()
        at = sum_down.land()
        sum_down.start()

    keep, send, up_sums, grad_hidden = up_grad_call(
        me_or_none, kernel_order, list(range(steps)), low, down, slope, hlt, up, after(grad, at)
    )
    sum_up = Sum(*halves_of(keep, send, steps), count, half=True)
    sum_up.start()
    at = sum_down.land(grad_hidden)
    sum_down.start()
    at = sum_up.land(at)
    sum_up.start()
    grad_attn, keep, send, grad_ctx = norm_back_call(
        me_or_none, kernel_order, after(grad_hidden, at), norm, first_inv, vec, contexts_t, wo,
        ffn_sums, up_sums,
    )
    sum_out = Sum(*halves_of(keep, send, 1, quads), count)
    sum_out.start()
    at = grad_attn

    def back(quad, slots, *others):
        group, at = places[quad]
        q, k, v, ctx, _, raised, inv, _ = heads[group]
        dq, dk, dv, *rest = attend_back(
            me_or_none, slots, quad, at, inputs_t, after(grad_ctx, *others), ctx, inv, q, k, v, raised
        )
        return (dq, dk, dv), rest

    def back_sum(quad, *others):
        part, (keep, send) = back(quad, kernel_order, *others)
        return part, Sum(*halves_of(keep, send, 3), count)

    part_0, sum_0 = back_sum(0, at)
    sum_0.start()
    at = sum_down.land(part_0[0])
    sum_down.start()
    at = sum_out.land(at)
    at = sum_up.land(at)
    sum_up.start()
    part_1, sum_1 = back_sum(1, at)
    sum_1.start()
    at = sum_0.land(part_1[0])
    sum_0 = joined([sum_out, sum_0])
    sum_0.start()
    at = sum_down.land(at, sum_0.send)
    at = sum_up.land(at)
    sum_up.start()
    if own_rows:
        middle = count // 4
        send_slots = (order[0], order[1][:middle], order[1][middle:])
        part_2, (keep, near_send, far_send) = back(2, send_slots, at)
        near, far = swap(near_send, 1, count), swap(far_send, 1, count)
        at = sum_1.land(part_2[0])
        sum_1.start()
        far = after(far, at)
        sum_2 = Sum(keep, None, count)
        sum_2.bit, sum_2.slots = 2, middle
        sum_2.send = (keep[middle:].astype(WIDE) + far.astype(WIDE)).astype(LOW)
        sum_2.cut(lambda term: term[:middle])
        sum_2.terms.append((near, ()))
        at = sum_2.send
        sum_2.start()
    else:
        part_2, sum_2 = back_sum(2, at)
        sum_2.start()
        at = sum_1.land(part_2[0])
        sum_1.start()
        at = sum_2.land(at)
        sum_2.start()
    at = sum_0.land(at)
    sum_0.start()
    at = sum_1.land(at)
    at = sum_2.land(at)
    sum_1 = joined([sum_1, sum_2])
    sum_1.start()
    at = sum_up.land(sum_1.send)
    sum_up.start()
    at = sum_0.land(at)
    sum_0.start()
    sum_down.start(at)
    weights = [group[7] for group in heads]
    at = input_grad = input_grad_call(
        [part_0, part_1, part_2], places, weights, after(grad_attn, at)
    )
    while sum_1.total is None:
        for item in (sum_1, sum_up, sum_0, sum_down):
            if item.total is None:
                at = item.land(at)
            if item.total is None:
                item.start()
    for item in (sum_0, sum_up, sum_down):
        while item.total is None:
            item.land()
            if item.total is None:
                item.start()
    tall = 3 * rows + EXTRA
    grad_qkv = jnp.concatenate([sum_0.total[-tall:], sum_1.total[:tall], sum_1.total[tall:]], axis=1)
    grad_out = jnp.concatenate(jnp.split(sum_0.total[:-tall], quads), axis=1)
    of_mine = lambda value, size: lax.dynamic_slice_in_dim(value, me * size, size, value.ndim - 1)
    own = of_mine(
        jnp.concatenate([grad_qkv[3 * rows : 3 * rows + 2], grad_out[rows : rows + 6]]), rows
    )
    grad_up_bias = of_mine(grad_out[rows + 6 : rows + 6 + steps].reshape(-1), up_bias.shape[0])
    grad_up = sum_up.total
    return (
        layer_out,
        input_grad,
        grad_qkv[:rows],
        own[QUERY_BIAS],
        grad_qkv[rows : 2 * rows],
        grad_qkv[2 * rows : 3 * rows],
        own[VALUE_BIAS],
        grad_out[:rows],
        own[OUT_BIAS],
        own[ATTN_GAIN],
        own[ATTN_SHIFT],
        jnp.concatenate([grad_up[rows * i : rows * (i + 1)] for i in range(steps)], axis=1),
        grad_up_bias,
        sum_down.total,
        own[DOWN_BIAS],
        own[FFN_GAIN],
        own[FFN_SHIFT],
    )


def solution(mesh):
    tokens = P(("rep", "fsdp"), None)
    matrix = P("fsdp", None)
    vector = P("fsdp")
    params_placed = (
        matrix,
        vector,
        matrix,
        matrix,
        vector,
        matrix,
        vector,
        vector,
        vector,
        matrix,
        vector,
        matrix,
        vector,
        vector,
        vector,
    )
    return jax.shard_map(
        shards,
        mesh=mesh,
        in_specs=(tokens, P(("rep", "fsdp")), *params_placed, tokens),
        out_specs=(tokens, tokens, *params_placed),
        check_vma=False,
    )
```

```python
import functools

import jax
import jax.numpy as jnp
from jax import lax
from jax.experimental import pallas as pl
from jax.experimental.pallas import tpu as pltpu
from jax.sharding import PartitionSpec as P

D = 768
H = 12
HD = 64
LONG = 512
SHORT = 128
QUAD = 256
PAIR = 128
TILE = 768

EPSILON = 1e-05
BLOCKED = -1e30
LOW = jnp.bfloat16
WIDE = jnp.float32
ROOM = 38 << 20
EXTRA = 16

QUERY_BIAS, VALUE_BIAS, OUT_BIAS, ATTN_GAIN, ATTN_SHIFT, DOWN_BIAS, FFN_GAIN, FFN_SHIFT = range(8)


def dot(left, right, left_dim, right_dim):
    return lax.dot_general(
        left, right, (((left_dim,), (right_dim,)), ((), ())), preferred_element_type=WIDE
    )


def row_mean(value):
    return jnp.mean(value, axis=-1, keepdims=True)


def token_sum(value):
    return jnp.sum(value, axis=0, keepdims=True)


def whole(shape):
    zeros = (0,) * len(shape)
    return pl.BlockSpec(shape, lambda *_: zeros, pipeline_mode=pl.Buffered(1))


def place(target, sources, slots, me):
    rows = sources[0].shape[1]
    for source, distances in zip(sources, slots):
        for at, distance in enumerate(distances):
            start = pl.multiple_of((me ^ distance) * rows, rows)
            target[pl.ds(start, rows), :] = source[at]


def far(value):
    return pltpu.with_memory_space_constraint(value, pltpu.HBM)


def params():
    return pltpu.CompilerParams(vmem_limit_bytes=ROOM)


def cost(microseconds):
    return pl.CostEstimate(
        flops=int(microseconds * 1.1e9), bytes_accessed=1 << 20, transcendentals=0
    )


def unplace(targets, source, slots, me, top, rows):
    for target, distances in zip(targets, slots):
        for at, distance in enumerate(distances):
            start = pl.multiple_of((me ^ distance) * rows, rows)
            target[at, top : top + rows, :] = source(pl.ds(start, rows)).astype(LOW)


def to_all(targets, slots, top, rows):
    low = rows.astype(LOW)
    for target, distances in zip(targets, slots):
        for at in range(len(distances)):
            target[at, top : top + EXTRA, :] = low


def half_masks():
    lane = lax.broadcasted_iota(jnp.int32, (1, PAIR), 1)
    return [jnp.where(lane // HD == half, 1.0, 0.0) for half in range(2)]


def attend_kernel(slots, kind_ref, me_ref, x_ref, vec_ref, *refs):
    pieces = len(slots)
    sources, refs = refs[: 3 * pieces], refs[3 * pieces :]
    q_ref, k_ref, v_ref, ctx_ref, ctxt_ref, raised_ref, inv_ref, weight_ref = refs

    @pl.when(pl.program_id(1) == 0)
    def _():
        for at in range(3):
            place(weight_ref.at[at], sources[at * pieces : (at + 1) * pieces], slots, me_ref[0])

    x = x_ref[...]
    q_ref[...] = (dot(x, weight_ref[0], 1, 0) + vec_ref[QUERY_BIAS : QUERY_BIAS + 1]).astype(LOW)
    k_ref[...] = dot(x, weight_ref[1], 1, 0).astype(LOW)
    v_ref[...] = (dot(x, weight_ref[2], 1, 0) + vec_ref[VALUE_BIAS : VALUE_BIAS + 1]).astype(LOW)
    part = lax.broadcasted_iota(jnp.int32, (LONG, PAIR), 0) // SHORT
    lane = lax.broadcasted_iota(jnp.int32, (LONG, PAIR), 1)
    blocked = jnp.where(kind_ref[pl.program_id(1)] == 1, 0.0, BLOCKED)
    query_part = jnp.where((lane < LONG // SHORT) & (part != lane), blocked, 0.0).astype(LOW)
    key_part = jnp.where(part == lane, 1.0, 0.0).astype(LOW)
    halves = half_masks()
    everything = []
    for pair in range(QUAD // PAIR):
        cols = pl.ds(pair * PAIR, PAIR)
        q2 = q_ref[:, cols].astype(WIDE) * HD ** (-0.5)
        keys = jnp.concatenate([k_ref[:, cols], key_part], axis=1)
        for half in range(2):
            queries = jnp.concatenate([(q2 * halves[half]).astype(LOW), query_part], axis=1)
            everything.append(dot(keys, queries, 1, 1))
    low = []
    for head, scores in enumerate(everything):
        peak = jnp.max(scores, axis=0, keepdims=True)
        raised = jnp.exp(scores - peak).astype(LOW)
        raised_ref[0, head] = raised
        low.append(raised)
    for pair in range(QUAD // PAIR):
        cols = pl.ds(pair * PAIR, PAIR)
        v2t = v_ref[:, cols].T
        contexts, inverses = [], []
        for half in range(2):
            left = jnp.concatenate(
                [v2t[HD * half : HD * half + HD], jnp.ones((16, LONG), LOW)], axis=0
            )
            mixed = dot(left, low[pair * 2 + half], 1, 0)
            inverse = 1.0 / mixed[HD : HD + 1]
            contexts.append(mixed[:HD] * inverse)
            inverses.append(jnp.broadcast_to(inverse, (HD, LONG)))
        context = jnp.concatenate(contexts, axis=0)
        ctxt_ref[pair * PAIR : pair * PAIR + PAIR, :] = context.astype(LOW)
        ctx_ref[:, cols] = context.T.astype(LOW)
        inv_ref[:, cols] = jnp.concatenate(inverses, axis=0).T


def attend(kind, me, quads, x, weights, vec):
    pieces, slots, rows = weights
    count = x.shape[0]
    blocks, number, low = count // LONG, len(quads), quads[0]
    tokens = pl.BlockSpec((LONG, QUAD), lambda j, b, *_: (b, j))
    act = pltpu.HBM((count, number * QUAD), LOW)
    return pl.pallas_call(
        functools.partial(attend_kernel, slots),
        grid_spec=pltpu.PrefetchScalarGridSpec(
            num_scalar_prefetch=2,
            grid=(number, blocks),
            in_specs=[
                pl.BlockSpec((LONG, D), lambda j, b, *_: (b, 0)),
                pl.BlockSpec((8, QUAD), lambda j, b, *_: (0, j + low)),
            ]
            + [
                pl.BlockSpec((piece.shape[0], rows, QUAD), lambda j, b, *_, at=at: (0, at, j))
                for at in range(3)
                for piece in pieces
            ],
            out_specs=[
                tokens,
                tokens,
                tokens,
                tokens,
                pl.BlockSpec((QUAD, LONG), lambda j, b, *_: (j, b)),
                pl.BlockSpec((1, QUAD // HD, LONG, LONG), lambda j, b, *_: (b, j, 0, 0)),
                tokens,
                pl.BlockSpec((3, D, QUAD), lambda j, b, *_: (0, 0, j)),
            ],
        ),
        out_shape=[
            act,
            act,
            act,
            act,
            pltpu.HBM((number * QUAD, count), LOW),
            pltpu.HBM((blocks, number * QUAD // HD, LONG, LONG), LOW),
            pltpu.HBM((count, number * QUAD), WIDE),
            pltpu.HBM((3, D, number * QUAD), LOW),
        ],
        compiler_params=params(),
        cost_estimate=cost(0.1),
        name="attend",
    )(kind, me, far(x), far(vec), *(far(piece) for piece in list(pieces) * 3))


def attend_back_kernel(
    slots,
    me_ref,
    xt_ref,
    d_ref,
    ctx_ref,
    inv_ref,
    q_ref,
    k_ref,
    v_ref,
    raised_ref,
    dq_ref,
    dk_ref,
    dv_ref,
    *refs,
):
    targets, (totals, biases) = refs[:-2], refs[-2:]
    block = pl.program_id(0)
    halves = half_masks()
    minus = jnp.full((LONG, PAIR), -1.0, LOW)
    work = []
    for pair in range(QUAD // PAIR):
        cols = pl.ds(pair * PAIR, PAIR)
        d2 = d_ref[:, cols].astype(WIDE) * inv_ref[:, cols] * HD ** (-0.5)
        along = d2 * ctx_ref[:, cols].astype(WIDE)
        q2 = q_ref[:, cols].astype(WIDE)
        values = jnp.concatenate([v_ref[:, cols], minus], axis=1)
        for half in range(2):
            dm = (d2 * halves[half]).astype(LOW)
            am = (along * halves[half]).astype(LOW)
            qm = (q2 * halves[half]).astype(LOW)
            dp = dot(values, jnp.concatenate([dm, am], axis=1), 1, 1)
            work.append((pair, half, dm, qm, dp))
    k2ts = [k_ref[:, pl.ds(pair * PAIR, PAIR)].T for pair in range(QUAD // PAIR)]
    done = []
    for pair, half, dm, qm, dp in work:
        raised = raised_ref[0, pair * 2 + half]
        ds = (raised.astype(WIDE) * dp).astype(LOW)
        done.append((pair, half, raised, ds, dm, qm))
    for pair in range(QUAD // PAIR):
        cols = pl.ds(pair * PAIR, PAIR)
        dqt, dk, dv = [], 0, 0
        for p, half, raised, ds, dm, qm in done:
            if p == pair:
                dqt.append(dot(k2ts[pair][HD * half : HD * half + HD], ds, 1, 0))
        both = [item for item in done if item[0] == pair]
        wide = lambda at, axis: jnp.concatenate([item[at] for item in both], axis=axis)
        dv = dot(wide(2, 1), wide(4, 0), 1, 0)
        dk = dot(wide(3, 1), wide(5, 0), 1, 0)
        dv_ref[:, cols] = (dv * HD**0.5).astype(LOW)
        dk_ref[:, cols] = dk.astype(LOW)
        dq_ref[:, cols] = jnp.concatenate(dqt, axis=0).T.astype(LOW)
    xt = xt_ref[...]
    for at, ref in enumerate((dq_ref, dk_ref, dv_ref)):
        grad = dot(xt, ref[...], 1, 0)

        @pl.when(block == 0)
        def _(grad=grad, at=at):
            totals[at] = grad

        @pl.when(block != 0)
        def _(grad=grad, at=at):
            totals[at] += grad

    sums = jnp.concatenate(
        [
            token_sum(dq_ref[...].astype(WIDE)),
            token_sum(dv_ref[...].astype(WIDE)),
            jnp.zeros((EXTRA - 2, QUAD), WIDE),
        ],
        axis=0,
    )

    @pl.when(block == 0)
    def _():
        biases[...] = sums

    @pl.when(block != 0)
    def _():
        biases[...] += sums

    @pl.when(block == pl.num_programs(0) - 1)
    def _():
        rows = (targets[0].shape[1] - EXTRA) // 3
        for at in range(3):
            unplace(
                targets, lambda part, at=at: totals[at, part], slots, me_ref[0], at * rows, rows
            )
        to_all(targets, slots, 3 * rows, biases[...])


def attend_back(me, slots, quad, at, xt, d, ctx, inv, q, k, v, raised):
    count = q.shape[0]
    tokens = pl.BlockSpec((LONG, QUAD), lambda b, *_: (b, at))
    grads = pl.BlockSpec((LONG, QUAD), lambda b, *_: (b, 0))
    act = pltpu.HBM((count, QUAD), LOW)
    rows = D // sum(map(len, slots))
    halves = [(max(len(part), 1), 3 * rows + EXTRA, QUAD) for part in slots]
    return pl.pallas_call(
        functools.partial(attend_back_kernel, slots),
        grid_spec=pltpu.PrefetchScalarGridSpec(
            num_scalar_prefetch=1,
            grid=(count // LONG,),
            in_specs=[
                pl.BlockSpec((D, LONG), lambda b, *_: (0, b)),
                pl.BlockSpec((LONG, QUAD), lambda b, *_: (b, quad)),
            ]
            + [tokens] * 5
            + [pl.BlockSpec((1, QUAD // HD, LONG, LONG), lambda b, *_: (b, at, 0, 0))],
            out_specs=[grads, grads, grads] + [whole(half) for half in halves],
            scratch_shapes=[pltpu.VMEM((3, D, QUAD), WIDE), pltpu.VMEM((EXTRA, QUAD), WIDE)],
        ),
        out_shape=[act, act, act] + [pltpu.HBM(half, LOW) for half in halves],
        compiler_params=params(),
        cost_estimate=cost(2),
        name="attend_back",
    )(
        me, far(xt), d, *(value if quad else far(value) for value in (ctx, inv, q, k, v)), far(raised)
    )


def out_kernel(places, groups, me_ref, x_ref, vec_ref, *refs):
    contexts, refs = refs[:groups], refs[groups:]
    norm_ref, inv_ref, hl_ref, hlt_ref, wo_ref = refs[-5:]
    at, col = 0, 0
    for slots in places:
        sources = refs[at : at + len(slots)]
        at += len(slots)
        width = sources[0].shape[2]
        place(wo_ref.at[:, col : col + width], sources, slots, me_ref[0])
        col += width
    bias = vec_ref[OUT_BIAS : OUT_BIAS + 1]
    gain = vec_ref[ATTN_GAIN : ATTN_GAIN + 1]
    shift = vec_ref[ATTN_SHIFT : ATTN_SHIFT + 1]
    wo = wo_ref[...]
    step = 256
    for at in range(0, x_ref.shape[0], step):
        rows = pl.ds(at, step)
        context = jnp.concatenate([ref[rows] for ref in contexts], axis=1)
        total = x_ref[rows].astype(WIDE) + dot(context, wo, 1, 0) + bias
        centered = total - row_mean(total)
        inverse = lax.rsqrt(row_mean(centered * centered) + EPSILON)
        norm = centered * inverse
        norm_ref[rows] = norm
        inv_ref[rows] = jnp.broadcast_to(inverse, (step, 128))
        hidden = (norm * gain + shift).astype(LOW)
        hl_ref[rows] = hidden
        hlt_ref[:, rows] = hidden.T


def out_call(me, contexts, x, weights, vec):
    count = x.shape[0]
    specs, values = [], []
    for pieces, _, rows in weights:
        for piece in pieces:
            specs.append(pl.BlockSpec((piece.shape[0], rows, piece.shape[2]), lambda *_: (0, 3, 0)))
            values.append(piece)
    shapes = [((count, D), WIDE), ((count, 128), WIDE), ((count, D), LOW), ((D, count), LOW), ((D, D), LOW)]
    outs = [pltpu.HBM(shape, dtype) for shape, dtype in shapes]
    outs[2] = jax.ShapeDtypeStruct(*shapes[2])
    return pl.pallas_call(
        functools.partial(out_kernel, [slots for _, slots, _ in weights], len(contexts)),
        grid_spec=pltpu.PrefetchScalarGridSpec(
            num_scalar_prefetch=1,
            grid=(1,),
            in_specs=[whole((count, D)), whole((8, D))]
            + [whole(context.shape) for context in contexts]
            + specs,
            out_specs=[whole(shape) for shape, _ in shapes],
        ),
        out_shape=outs,
        compiler_params=params(),
        cost_estimate=cost(0.1),
        name="out",
    )(me, *(far(value) for value in (x, vec, *contexts, *values)))


def up_kernel(slots, me_ref, hl_ref, bu_ref, *refs):
    own, other = slots
    ups, (act_ref, slope_ref, wu_ref) = refs[:-3], refs[-3:]
    step = 256
    first_half = pl.program_id(0) < pl.num_programs(0) // 2

    @pl.when(first_half)
    def _():
        place(wu_ref.at[0], ups[: len(own)], own, me_ref[0])

    @pl.when(jnp.logical_not(first_half))
    def _():
        place(wu_ref.at[0], ups[len(own) :], other, me_ref[0])

    bias = bu_ref[...]
    weight = wu_ref[0]
    for at in range(0, hl_ref.shape[0], step):
        rows = pl.ds(at, step)
        before = dot(hl_ref[rows], weight, 1, 0) + bias
        half = 0.5 * (1.0 + lax.erf(before * 0.7071067811865476))
        act_ref[rows] = (before * half).astype(LOW)
        slope_ref[rows] = (
            half + before * jnp.exp(-0.5 * before * before) * 0.3989422804014327
        ).astype(LOW)


def up_call(me, hl, own, other, rows, up_bias):
    count = hl.shape[0]
    hidden = up_bias.shape[1]
    steps = hidden // TILE
    half = steps // 2
    cols = lambda r: pl.BlockSpec((r, TILE), lambda j, me: (0, j ^ me[1]))
    early = lambda j, *_: (0, jnp.minimum(j, half - 1), 0)
    late = lambda j, *_: (0, jnp.maximum(j - half, 0), 0)
    return pl.pallas_call(
        functools.partial(up_kernel, (own[1], other[1])),
        grid_spec=pltpu.PrefetchScalarGridSpec(
            num_scalar_prefetch=1,
            grid=(steps,),
            in_specs=[whole((count, D)), cols(1)]
            + [pl.BlockSpec((piece.shape[0], rows, D), early) for piece in own[0]]
            + [pl.BlockSpec((piece.shape[0], rows, D), late) for piece in other[0]],
            out_specs=[
                cols(count),
                cols(count),
                pl.BlockSpec((1, D, TILE), lambda j, me: (j ^ me[1], 0, 0)),
            ],
        ),
        out_shape=[
            jax.ShapeDtypeStruct((count, hidden), LOW),
            pltpu.HBM((count, hidden), LOW),
            pltpu.HBM((steps, D, TILE), LOW),
        ],
        compiler_params=params(),
        cost_estimate=cost(0.1),
        name="up",
    )(me, hl, *(far(value) for value in (up_bias, *own[0], *other[0])))


def down_kernel(slots, me_ref, act_ref, norm_ref, vec_ref, cot_ref, *refs):
    sources = refs[: len(slots)]
    out_ref, grad_ref, low_ref, sums_ref, wd_ref = refs[len(slots) :]

    @pl.when(pl.program_id(0) == 0)
    def _():
        place(wd_ref, sources, slots, me_ref[0])

    row = lambda at: vec_ref[at : at + 1]
    total = (
        norm_ref[...] * row(ATTN_GAIN)
        + row(ATTN_SHIFT)
        + (dot(act_ref[...], wd_ref[...], 1, 0) + row(DOWN_BIAS))
    )
    centered = total - row_mean(total)
    inverse = lax.rsqrt(row_mean(centered * centered) + EPSILON)
    norm = centered * inverse
    out_ref[...] = (norm * row(FFN_GAIN) + row(FFN_SHIFT)).astype(LOW)
    grad_out = cot_ref[...].astype(WIDE)
    scaled = grad_out * row(FFN_GAIN)
    grad = inverse * (scaled - row_mean(scaled) - norm * row_mean(scaled * norm))
    grad_ref[...] = grad
    low = grad.astype(LOW)
    low_ref[...] = low
    sums = jnp.concatenate(
        [
            token_sum(grad_out * norm),
            token_sum(grad_out),
            token_sum(low.astype(WIDE)),
            jnp.zeros((5, D), WIDE),
        ],
        axis=0,
    )

    @pl.when(pl.program_id(0) == 0)
    def _():
        sums_ref[...] = sums

    @pl.when(pl.program_id(0) != 0)
    def _():
        sums_ref[...] += sums


def down_call(me, act, third, norm, vec, cotangent):
    pieces, slots, _ = third
    count, hidden = act.shape
    tile = 256
    rows = lambda c: pl.BlockSpec((tile, c), lambda i, *_: (i, 0))
    return pl.pallas_call(
        functools.partial(down_kernel, slots),
        grid_spec=pltpu.PrefetchScalarGridSpec(
            num_scalar_prefetch=1,
            grid=(count // tile,),
            in_specs=[rows(hidden), rows(D), whole((8, D)), rows(D)]
            + [whole(piece.shape) for piece in pieces],
            out_specs=[rows(D), rows(D), rows(D), whole((8, D)), whole((hidden, D))],
        ),
        out_shape=[
            pltpu.HBM((count, D), LOW),
            jax.ShapeDtypeStruct((count, D), WIDE),
            jax.ShapeDtypeStruct((count, D), LOW),
            pltpu.HBM((8, D), WIDE),
            pltpu.HBM((hidden, D), LOW),
        ],
        compiler_params=params(),
        cost_estimate=cost(13),
        name="down",
    )(me, act, *(far(value) for value in (norm, vec, cotangent, *pieces)))


def down_grad_kernel(owner_ref, me_ref, act_ref, low_ref, keep_ref, send_ref, scratch):
    rows = keep_ref.shape[1]
    scratch[...] = dot(act_ref[...], low_ref[...], 0, 0).astype(LOW)
    mine = lax.rem(me_ref[0], 2) * rows
    keep_ref[0] = scratch[pl.ds(pl.multiple_of(mine, rows), rows)]
    send_ref[0] = scratch[pl.ds(pl.multiple_of(rows - mine, rows), rows)]


def down_grad_plain_kernel(act_ref, low_ref, grad_ref):
    grad_ref[...] = dot(act_ref[...], low_ref[...], 0, 0).astype(LOW)


def down_grad_plain_call(act, low):
    count, hidden = act.shape
    return pl.pallas_call(
        down_grad_plain_kernel,
        grid=(hidden // TILE,),
        in_specs=[pl.BlockSpec((count, TILE), lambda j: (0, j)), whole((count, D))],
        out_specs=pl.BlockSpec((TILE, D), lambda j: (j, 0)),
        out_shape=pltpu.HBM((hidden, D), LOW),
        compiler_params=params(),
        cost_estimate=cost(9),
        name="down_grad",
    )(act, low)


def down_grad_call(me, slots, rows, act, low):
    count, hidden = act.shape
    number = len(slots[0])
    pair = 2 * rows
    owners = (me // 2) ^ (jnp.array(slots[0], jnp.int32) // 2)
    part = pl.BlockSpec((1, rows, D), lambda j, *_: (j, 0, 0))
    half = pltpu.HBM((number, rows, D), LOW)
    return pl.pallas_call(
        down_grad_kernel,
        grid_spec=pltpu.PrefetchScalarGridSpec(
            num_scalar_prefetch=2,
            grid=(number,),
            in_specs=[
                pl.BlockSpec((count, pair), lambda j, owner, _: (0, owner[j])),
                whole((count, D)),
            ],
            out_specs=[part, part],
            scratch_shapes=[pltpu.VMEM((pair, D), LOW)],
        ),
        out_shape=[half, half],
        compiler_params=params(),
        cost_estimate=cost(number),
        name="down_grad",
    )(owners, me, act, low)


def up_grad_kernel(
    slots, me_ref, low_ref, wd_ref, slope_ref, hlt_ref, wu_ref, grad_ref,
    keep_ref, send_ref, bias_ref, hidden_ref, before_scr, grad_scr,
):
    step = pl.program_id(0)
    before_scr[...] = (dot(low_ref[...], wd_ref[...], 1, 1) * slope_ref[...].astype(WIDE)).astype(
        LOW
    )
    before = before_scr[...]
    grad_scr[...] = dot(hlt_ref[...], before, 1, 0).astype(LOW)
    unplace(
        (keep_ref, send_ref), lambda part: grad_scr[part], slots, me_ref[0], 0, keep_ref.shape[1]
    )
    bias_ref[...] = jnp.broadcast_to(token_sum(before.astype(WIDE)), (8, TILE))
    back = dot(before, wu_ref[0], 1, 1)

    @pl.when(step == 0)
    def _():
        hidden_ref[...] = back + grad_ref[...]

    @pl.when(step != 0)
    def _():
        hidden_ref[...] += back


def up_grad_call(me, slots, tiles, low, down, slope, hlt, up, grad):
    count = slope.shape[0]
    first, steps = tiles[0], len(tiles)
    kept, rows = len(slots[0]), D // (len(slots[0]) + len(slots[1]))
    part = pl.BlockSpec((kept, rows, TILE), lambda j, *_: (0, j, 0))
    half = pltpu.HBM((kept, steps * rows, TILE), LOW)
    return pl.pallas_call(
        functools.partial(up_grad_kernel, slots),
        grid_spec=pltpu.PrefetchScalarGridSpec(
            num_scalar_prefetch=1,
            grid=(steps,),
            in_specs=[
                whole((count, D)),
                pl.BlockSpec((TILE, D), lambda j, *_: (j + first, 0)),
                pl.BlockSpec((count, TILE), lambda j, *_: (0, j + first)),
                whole((D, count)),
                pl.BlockSpec((1, D, TILE), lambda j, *_: (j + first, 0, 0)),
                whole((count, D)),
            ],
            out_specs=[
                part,
                part,
                pl.BlockSpec((8, TILE), lambda j, *_: (j, 0)),
                whole((count, D)),
            ],
            scratch_shapes=[pltpu.VMEM((count, TILE), LOW), pltpu.VMEM((D, TILE), LOW)],
        ),
        out_shape=[
            half,
            half,
            pltpu.HBM((8 * steps, TILE), WIDE),
            jax.ShapeDtypeStruct((count, D), WIDE),
        ],
        compiler_params=params(),
        cost_estimate=cost(6 * steps),
        name="up_grad",
    )(me, low, far(down), far(slope), hlt, far(up), grad)


def norm_back_kernel(
    slots, groups, me_ref, hidden_ref, norm_ref, inv_ref, vec_ref, wo_ref, ffn_ref, up_ref, *refs
):
    contexts, refs = refs[:groups], refs[groups:]
    grad_ref, keep_ref, send_ref, ctx_ref, low_scr, out_scr = refs
    count = hidden_ref.shape[0]
    step = 256
    gain = vec_ref[ATTN_GAIN : ATTN_GAIN + 1]
    wo = wo_ref[...]
    sums = 0
    for at in range(0, count, step):
        rows = pl.ds(at, step)
        hidden = hidden_ref[rows]
        norm = norm_ref[rows]
        scaled = hidden * gain
        grad = inv_ref[rows][:, 0:1] * (
            scaled - row_mean(scaled) - norm * row_mean(scaled * norm)
        )
        grad_ref[rows] = grad
        low = grad.astype(LOW)
        low_scr[rows] = low
        sums = sums + jnp.concatenate(
            [
                token_sum(hidden * norm),
                token_sum(hidden),
                token_sum(low.astype(WIDE)),
                jnp.zeros((5, D), WIDE),
            ],
            axis=0,
        )
        ctx_ref[rows] = dot(low, wo, 1, 1).astype(LOW)
    at = 0
    for ref in contexts:
        out_scr[at : at + ref.shape[0], :] = dot(ref[...], low_scr[...], 1, 0).astype(LOW)
        at += ref.shape[0]
    quads = D // QUAD
    rows = keep_ref.shape[1] // quads - EXTRA
    steps = up_ref.shape[0] // 8
    extra = [sums[2:3], sums[:2], ffn_ref[2:3], ffn_ref[:2]]
    extra += [up_ref[8 * at : 8 * at + 1] for at in range(steps)]
    extra.append(jnp.zeros((EXTRA - 6 - steps, D), WIDE))
    extra = jnp.concatenate(extra, axis=0)
    for quad in range(quads):
        cols = slice(quad * QUAD, quad * QUAD + QUAD)
        top = quad * (rows + EXTRA)
        targets = keep_ref, send_ref
        unplace(targets, lambda part: out_scr[part, cols], slots, me_ref[0], top, rows)
        to_all(targets, slots, top + rows, extra[:, cols])


def norm_back_call(me, slots, hidden, norm, inv, vec, contexts, wo, ffn_sums, up_sums):
    count = hidden.shape[0]
    kept, rows = len(slots[0]), D // (len(slots[0]) + len(slots[1]))
    half = (kept, (rows + EXTRA) * (D // QUAD), QUAD)
    return pl.pallas_call(
        functools.partial(norm_back_kernel, slots, len(contexts)),
        grid_spec=pltpu.PrefetchScalarGridSpec(
            num_scalar_prefetch=1,
            grid=(1,),
            in_specs=[
                whole((count, D)),
                whole((count, D)),
                whole((count, 128)),
                whole((8, D)),
                whole((D, D)),
                whole((8, D)),
                whole(up_sums.shape),
            ]
            + [whole(context.shape) for context in contexts],
            out_specs=[whole((count, D)), whole(half), whole(half), whole((count, D))],
            scratch_shapes=[pltpu.VMEM((count, D), LOW), pltpu.VMEM((D, D), LOW)],
        ),
        out_shape=[
            pltpu.HBM((count, D), WIDE),
            pltpu.HBM(half, LOW),
            pltpu.HBM(half, LOW),
            jax.ShapeDtypeStruct((count, D), LOW),
        ],
        compiler_params=params(),
        cost_estimate=cost(12),
        name="norm_back",
    )(me, hidden, norm, inv, far(vec), wo, far(ffn_sums), far(up_sums), *contexts)


def input_grad_kernel(places, groups, grad_ref, *refs):
    weights, refs = refs[:groups], refs[groups:]
    total = grad_ref[...]
    for quad, (group, at) in enumerate(places):
        for matrix in range(3):
            total = total + dot(
                refs[3 * quad + matrix][...],
                weights[group][matrix, :, at * QUAD : at * QUAD + QUAD],
                1,
                1,
            )
    refs[-1][...] = total


def input_grad_call(pieces, places, weights, grad):
    count = grad.shape[0]
    tile = 512
    tokens = lambda width: pl.BlockSpec((tile, width), lambda i: (i, 0))
    values = [value for piece in pieces for value in piece]
    return pl.pallas_call(
        functools.partial(input_grad_kernel, places, len(weights)),
        grid=(count // tile,),
        in_specs=[tokens(D)]
        + [whole(weight.shape) for weight in weights]
        + [tokens(QUAD) for _ in values],
        out_specs=tokens(D),
        out_shape=pltpu.HBM((count, D), WIDE),
        compiler_params=params(),
        cost_estimate=cost(0.1),
        name="input_grad",
    )(*(far(value) for value in (grad, *weights, *values)))


def pack_kernel(places, *refs):
    for ref, (row, col) in zip(refs, places):
        refs[-1][row : row + ref.shape[0], col : col + ref.shape[1]] = ref[...]


def pack(parts, width):
    if any(array.shape[0] % 16 for line in parts for array, _ in line):
        return jnp.concatenate(
            [
                jnp.concatenate([a[:, width * at : width * (at + 1)] for a, at in line], axis=1)
                for line in parts
            ]
        )
    places, specs, row = [], [], 0
    for line in parts:
        for at, (array, block) in enumerate(line):
            places.append((row, at * width))
            specs.append(pl.BlockSpec((array.shape[0], width), lambda i, block=block: (0, block)))
        row += line[0][0].shape[0]
    shape = (row, width * len(parts[0]))
    return pl.pallas_call(
        functools.partial(pack_kernel, places),
        grid=(1,),
        in_specs=specs,
        out_specs=pl.BlockSpec(shape, lambda i: (0, 0)),
        out_shape=pltpu.HBM(shape, LOW),
        compiler_params=params(),
        cost_estimate=cost(1),
        name="pack",
    )(*(far(array) for line in parts for array, _ in line))


def swap(value, mask, count):
    return lax.ppermute(value, "fsdp", [(i, i ^ mask) for i in range(count)])


def after(value, *others):
    return lax.optimization_barrier((value,) + others)[0] if others else value


class Gather:
    def __init__(self, piece, count, half=False):
        self.unit = 1
        if half:
            rows = piece.shape[0] // 2
            piece = lax.dynamic_slice_in_dim(piece, lax.axis_index("rep") * rows, rows, 0)
            self.unit = 2
        self.parts, self.count = [(piece[None], [0])], count
        self.hops = [count >> at for at in range(1, count.bit_length() - 2)]

    def far(self, *others):
        held, _ = self.parts[0]
        self.other = swap(after(held, *others), self.hops[0], self.count)

    def land(self, *others):
        held, order = self.parts[0]
        held = jnp.concatenate([held, after(self.other, *others)], axis=0)
        mask = self.hops.pop(0) * self.unit
        self.parts = [(held, order + [at ^ mask for at in order])]
        return held

    def far_but(self, last):
        while len(self.hops) > last:
            self.far()
            self.land()
        return self.parts[0][0]

    def send(self, part, hop):
        held, order = self.parts[part]
        if hop == "rep":
            other, mask = lax.ppermute(held, "rep", [(0, 1), (1, 0)]), 1
        else:
            other, mask = swap(held, hop, self.count), hop * self.unit
        self.parts.append((other, [at ^ mask for at in order]))

    def tie(self, part, *others):
        held, order = self.parts[part]
        self.parts[part] = (after(held, *others), order)
        return self.parts[part][0]


def matrices(gather, number, rows, me):
    pieces, slots = zip(*gather.parts)
    if rows % 16 == 0:
        return pieces, slots, rows
    parts = in_order(jnp.concatenate(pieces)[:, : number * rows], slots, me)
    count, _, width = parts.shape
    parts = jnp.moveaxis(parts.reshape(count, number, rows, width), 1, 0)
    return (parts.reshape(1, number * count * rows, width),), ([0],), count * rows


def matrix_halves(gather, number, rows, side):
    if rows % 16 == 0:
        split = [([], []), ([], [])]
        for piece, order in gather.parts:
            pieces, slots = split[order[0] & 1]
            pieces.append(piece)
            slots.append([at >> 1 for at in order])
        return *split, rows
    pieces, slots = zip(*gather.parts)
    parts = in_order(jnp.concatenate(pieces), slots, side)
    count, width = parts.shape[0] // 2, parts.shape[-1]
    parts = jnp.moveaxis(parts.reshape(count, number, rows, width), 1, 0)
    parts = parts.reshape(1, number * count * rows, width)
    middle = parts.shape[1] // 2
    return ([parts[:, :middle]], [[0]]), ([parts[:, middle:]], [[0]]), count * rows


def in_order(held, slots, me):
    count = held.shape[0]
    distance = jnp.array([at for order in slots for at in order], jnp.int32)
    chosen = (jnp.arange(count, dtype=jnp.int32) ^ me)[:, None] == distance[None]
    return jnp.einsum(
        "ij,jrc->irc", chosen.astype(LOW), held, preferred_element_type=WIDE
    ).astype(LOW)


def to_slots(parts, slots, me):
    count = parts.shape[0]
    bit = 1
    while bit < count:
        pairs = parts.reshape((count // (2 * bit), 2, bit) + parts.shape[1:])
        parts = jnp.where((me & bit) != 0, pairs[:, ::-1], pairs).reshape(parts.shape)
        bit *= 2
    return tuple(
        jnp.concatenate([parts[at : at + 1] for at in distances]) for distances in slots
    )


def sum_order(count):
    bits = count.bit_length() - 2
    order = [
        sum(2 << place for place in range(bits) if at >> (bits - 1 - place) & 1)
        for at in range(count // 2)
    ]
    return order, [at ^ 1 for at in order]


class Sum:
    def __init__(self, keep, send, count, half=False):
        self.terms, self.send, self.count = [(keep, ())], send, count
        self.slots, self.kernel = keep.shape[0], False
        self.half, self.bit, self.total = half, 1, None

    def start(self, *others):
        send = after(self.send, *others) if others else self.send
        if self.half == "now" or self.bit == self.count:
            self.other = lax.ppermute(send, "rep", [(0, 1), (1, 0)])
        else:
            self.other = swap(send, self.bit, self.count)

    def added(self, *cuts):
        total = 0
        for array, before in self.terms:
            for each in (*before, *cuts):
                array = each(array)
            total = total + array.astype(WIDE)
        return total

    def cut(self, each):
        self.terms = [(array, (*before, each)) for array, before in self.terms]

    def land(self, *others):
        other = after(self.other, *others) if others else self.other
        if self.bit == self.count:
            if self.half:
                low = lax.axis_index("rep") == 0
                both = jnp.where(low, self.send, other), jnp.where(low, other, self.send)
                self.total = jnp.concatenate(both, axis=1)[0].astype(WIDE)
            else:
                self.total = (self.send.astype(WIDE) + other.astype(WIDE))[0]
            return self.total
        self.terms.append((other, ()))
        if self.half == "now":
            self.half = "done"
        else:
            self.bit *= 2
            if self.half is True:
                return self.halve()
        if self.bit == self.count:
            self.send = self.added().astype(LOW)
            return self.send
        middle = self.slots // 2
        if self.kernel and self.slots > 1:
            self.send = add_upper([array for array, _ in self.terms])
            self.kernel = False
        else:
            self.send = self.added(lambda term: term[middle:]).astype(LOW)
        self.cut(lambda term: term[:middle])
        self.slots = middle
        return self.send

    def halve(self):
        mine = lax.axis_index("rep")
        _, rows, width = self.send.shape

        def pick(at):
            return lambda term: lax.dynamic_slice_in_dim(term, at * (rows // 2), rows // 2, 1)

        self.send = self.added(pick(1 - mine)).astype(LOW)
        self.cut(pick(mine))
        self.half = "now"
        return self.send

    def finish(self):
        while self.total is None:
            self.start()
            self.land()


def add_kernel(*refs):
    total = 0
    for ref in refs[:-1]:
        total = total + ref[...].astype(WIDE)
    refs[-1][...] = total.astype(LOW)


def add_upper(terms):
    slots, rows, width = terms[0].shape
    upper = pl.BlockSpec((1, rows, width), lambda at: (at + slots // 2, 0, 0))
    return pl.pallas_call(
        add_kernel,
        grid=(slots // 2,),
        in_specs=[upper] * len(terms),
        out_specs=pl.BlockSpec((1, rows, width), lambda at: (at, 0, 0)),
        out_shape=pltpu.HBM((slots // 2, rows, width), LOW),
        compiler_params=params(),
        cost_estimate=cost(12),
        name="add",
    )(*(far(term) for term in terms))


def joined(sums):
    first = sums[0]
    whole = Sum(first.send, jnp.concatenate([item.send for item in sums], axis=1), first.count)
    whole.bit, whole.slots = first.bit, first.slots
    whole.terms = [(jnp.concatenate([item.added() for item in sums], axis=1), ())]
    return whole


def shards(
    inputs,
    block_kind,
    query_weight,
    query_bias,
    key_weight,
    value_weight,
    value_bias,
    out_weight,
    out_bias,
    attn_gain,
    attn_shift,
    up_weight,
    up_bias,
    down_weight,
    down_bias,
    ffn_gain,
    ffn_shift,
    cotangent,
):
    rows = query_weight.shape[0]
    count = D // rows
    hidden = up_weight.shape[1]
    steps = hidden // TILE
    vectors = (
        query_bias,
        value_bias,
        out_bias,
        attn_gain,
        attn_shift,
        down_bias,
        ffn_gain,
        ffn_shift,
    )
    down_rows = down_weight.shape[0]
    used = 8 * rows + up_bias.shape[0]
    spare = 16 * QUAD
    packed, at = 0, 0
    for value in vectors + (up_bias,):
        packed = packed + jnp.pad(value, (at, spare - at - value.shape[0]))
        at += value.shape[0]
    me = lax.axis_index("fsdp").astype(jnp.int32)
    own_rows = rows % 16 == 0
    mine = me.reshape(1)
    none = jnp.zeros((1,), jnp.int32)
    me_or_none = mine if own_rows else none
    attn_weights = (query_weight, key_weight, value_weight, out_weight)

    first = Gather(
        pack([[(w, 0)] for w in attn_weights] + [[(packed.reshape(16, QUAD), 0)]], QUAD), count
    )
    inputs_t = inputs.T
    first.far()
    at = first.land()
    rest = Gather(pack([[(w, 1), (w, 2)] for w in attn_weights], QUAD), count)
    second = Gather(pack([[(up_weight, at)] for at in range(steps)], TILE), count, half=True)
    rest.far(at)
    at = rest.land(first.far_but(0), second.parts[0][0])
    third = Gather(down_weight, count)
    first.send(0, 2)
    first.send(0, 1)
    rest.far_but(1)
    rest.far()
    second.far(at)
    at = second.land(inputs_t)
    at = rest.land(at)
    at = first.tie(1, at)
    first.send(1, 1)
    rest.send(0, 2)
    rest.send(0, 1)
    second.far_but(1)
    second.far()
    third.far(at)

    pieces, slots = zip(*first.parts)
    columns = -(-used // QUAD)
    whole_packed = in_order(
        jnp.concatenate([piece[:, 4 * rows : 4 * rows + columns] for piece in pieces]), slots, me
    ).reshape(count, columns * QUAD)
    vec = (
        jnp.moveaxis(whole_packed[:, : 8 * rows].reshape(count, 8, rows), 1, 0)
        .reshape(8, D)
        .astype(WIDE)
    )
    all_up_bias = whole_packed[:, 8 * rows : used].reshape(1, hidden).astype(WIDE)

    places = [(0, 0), (1, 0), (1, 1)]
    heads = [
        attend(
            block_kind, me_or_none, [0], inputs, matrices(first, 4, rows, me), after(vec, all_up_bias)
        )
    ]
    at = second.land(heads[0][3])
    second.send(0, 2)
    second.send(0, "rep")
    second.send(0, 1)
    at = third.land(at)
    third.far_but(1)
    third.far()
    at = rest.tie(1, at)
    rest.send(1, 1)
    heads.append(
        attend(
            block_kind, me_or_none, [1, 2], after(inputs, at), matrices(rest, 4, rows, me), vec
        )
    )
    contexts = [group[3] for group in heads]
    contexts_t = [group[4] for group in heads]
    at = second.tie(1, heads[1][3])
    at = second.tie(2, at)
    second.send(1, "rep")
    second.send(1, 1)
    second.send(2, 1)
    at = third.land(at)
    third.send(0, 2)
    third.send(0, 1)
    norm, first_inv, hl, hlt, wo = out_call(
        me_or_none,
        contexts,
        after(inputs, at),
        [matrices(first, 4, rows, me), matrices(rest, 4, rows, me)],
        vec,
    )
    second.tie(4, hl)
    second.send(4, 1)
    rank = lax.axis_index("rep").astype(jnp.int32)
    own, other, block = matrix_halves(second, steps, rows, 2 * me + rank)
    flip = jnp.stack([me, rank * (steps // 2)]) if own_rows else jnp.zeros((2,), jnp.int32)
    act, slope, up = up_call(flip, hl, own, other, block, all_up_bias)
    third.tie(1, act)
    third.send(1, 1)
    pieces = matrices(third, 1, down_rows, me)
    layer_out, grad, low, ffn_sums, down = down_call(
        mine if down_rows % 16 == 0 else none, act, pieces, norm, vec, cotangent
    )

    order = sum_order(count)
    quads = D // QUAD

    def halves_of(keep, send, k, groups=1):
        if own_rows:
            return keep, send
        width = keep.shape[-1]
        tall = keep.shape[1] // groups
        everything = []
        for group in jnp.split(keep[0], groups):
            parts = jnp.moveaxis(group[: k * D].reshape(k, count, rows, width), 0, 1)
            everything.append(parts.reshape(count, k * rows, width))
            everything.append(jnp.broadcast_to(group[None, k * D :], (count, tall - k * D, width)))
        return to_slots(jnp.concatenate(everything, axis=1), order, me)

    kernel_order = order if own_rows else ([0], [])
    if 2 * down_rows % 128 == 0:
        middle = count // 4
        near, far = ([part[at] for part in order] for at in (slice(middle), slice(middle, None)))
        far_keep, far_send = down_grad_call(mine, far, down_rows, act, low)
        far_other = swap(far_send, 1, count)
        near_keep, near_send = down_grad_call(mine, near, down_rows, act, after(low, far_keep))
        sum_down = Sum(near_keep, None, count)
        sum_down.bit, sum_down.slots, sum_down.kernel = 2, middle, True
        far_other = after(far_other, near_keep)
        sum_down.send = (far_keep.astype(WIDE) + far_other.astype(WIDE)).astype(LOW)
        at = sum_down.send
        sum_down.start()
        sum_down.terms.append((swap(near_send, 1, count), ()))
    else:
        parts = down_grad_plain_call(act, low).reshape(count, down_rows, D)
        sum_down = Sum(*to_slots(parts, order, me), count)
        sum_down.start()
        at = sum_down.land()
        sum_down.start()

    keep, send, up_sums, grad_hidden = up_grad_call(
        me_or_none, kernel_order, list(range(steps)), low, down, slope, hlt, up, after(grad, at)
    )
    sum_up = Sum(*halves_of(keep, send, steps), count, half=True)
    sum_up.start()
    at = sum_down.land(grad_hidden)
    sum_down.start()
    at = sum_up.land(at)
    sum_up.start()
    grad_attn, keep, send, grad_ctx = norm_back_call(
        me_or_none, kernel_order, after(grad_hidden, at), norm, first_inv, vec, contexts_t, wo,
        ffn_sums, up_sums,
    )
    sum_out = Sum(*halves_of(keep, send, 1, quads), count)
    sum_out.start()
    at = grad_attn

    def back(quad, slots, *others):
        group, at = places[quad]
        q, k, v, ctx, _, raised, inv, _ = heads[group]
        dq, dk, dv, *rest = attend_back(
            me_or_none, slots, quad, at, inputs_t, after(grad_ctx, *others), ctx, inv, q, k, v, raised
        )
        return (dq, dk, dv), rest

    def back_sum(quad, *others):
        part, (keep, send) = back(quad, kernel_order, *others)
        return part, Sum(*halves_of(keep, send, 3), count)

    part_0, sum_0 = back_sum(0, at)
    sum_0.start()
    at = sum_down.land(part_0[0])
    sum_down.start()
    at = sum_out.land(at)
    at = sum_up.land(at)
    sum_up.start()
    part_1, sum_1 = back_sum(1, at)
    sum_1.start()
    at = sum_0.land(part_1[0])
    sum_0 = joined([sum_out, sum_0])
    sum_0.start()
    at = sum_down.land(at, sum_0.send)
    at = sum_up.land(at)
    sum_up.start()
    if own_rows:
        middle = count // 4
        quarter = middle // 2
        send_slots = (order[0],) + tuple(
            order[1][part : part + quarter] for part in range(0, count // 2, quarter)
        )
        part_2, (keep, *sends) = back(2, send_slots, at)
        parts = [swap(send, 1, count) for send in sends]
        at = sum_1.land(part_2[0])
        sum_1.start()
        near = jnp.concatenate(parts[:2])
        far_part = jnp.concatenate([after(part, at) for part in parts[2:]])
        sum_2 = Sum(keep, None, count)
        sum_2.bit, sum_2.slots = 2, middle
        sum_2.send = (keep[middle:].astype(WIDE) + far_part.astype(WIDE)).astype(LOW)
        sum_2.cut(lambda term: term[:middle])
        sum_2.terms.append((near, ()))
        at = sum_2.send
        sum_2.start()
    else:
        part_2, sum_2 = back_sum(2, at)
        sum_2.start()
        at = sum_1.land(part_2[0])
        sum_1.start()
        at = sum_2.land(at)
        sum_2.start()
    at = sum_up.land(at)
    sum_up.start()
    at = sum_0.land(at)
    sum_0.start()
    weights = [group[7] for group in heads]
    input_grad = input_grad_call(
        [part_0, part_1, part_2], places, weights, after(grad_attn, at)
    )
    at = sum_1.land(input_grad)
    at = sum_2.land(at)
    sum_1 = joined([sum_1, sum_2])
    sum_1.start()
    at = sum_up.land(sum_1.send)
    sum_up.start()
    at = sum_0.land(at)
    sum_0.start()
    sum_down.start(at)
    while sum_1.total is None:
        at = sum_1.land(at)
        if sum_1.total is None:
            sum_1.start()
        for item in (sum_up, sum_down) if sum_1.bit < count else (sum_0, sum_up):
            if item.total is None:
                at = item.land(at)
            if item.total is None:
                item.start()
    for item in (sum_0, sum_up, sum_down):
        while item.total is None:
            item.land()
            if item.total is None:
                item.start()
    tall = 3 * rows + EXTRA
    grad_qkv = jnp.concatenate([sum_0.total[-tall:], sum_1.total[:tall], sum_1.total[tall:]], axis=1)
    grad_out = jnp.concatenate(jnp.split(sum_0.total[:-tall], quads), axis=1)
    of_mine = lambda value, size: lax.dynamic_slice_in_dim(value, me * size, size, value.ndim - 1)
    own = of_mine(
        jnp.concatenate([grad_qkv[3 * rows : 3 * rows + 2], grad_out[rows : rows + 6]]), rows
    )
    grad_up_bias = of_mine(grad_out[rows + 6 : rows + 6 + steps].reshape(-1), up_bias.shape[0])
    grad_up = sum_up.total
    return (
        layer_out,
        input_grad,
        grad_qkv[:rows],
        own[QUERY_BIAS],
        grad_qkv[rows : 2 * rows],
        grad_qkv[2 * rows : 3 * rows],
        own[VALUE_BIAS],
        grad_out[:rows],
        own[OUT_BIAS],
        own[ATTN_GAIN],
        own[ATTN_SHIFT],
        jnp.concatenate([grad_up[rows * i : rows * (i + 1)] for i in range(steps)], axis=1),
        grad_up_bias,
        sum_down.total,
        own[DOWN_BIAS],
        own[FFN_GAIN],
        own[FFN_SHIFT],
    )


def solution(mesh):
    tokens = P(("rep", "fsdp"), None)
    matrix = P("fsdp", None)
    vector = P("fsdp")
    params_placed = (
        matrix,
        vector,
        matrix,
        matrix,
        vector,
        matrix,
        vector,
        vector,
        vector,
        matrix,
        vector,
        matrix,
        vector,
        vector,
        vector,
    )
    return jax.shard_map(
        shards,
        mesh=mesh,
        in_specs=(tokens, P(("rep", "fsdp")), *params_placed, tokens),
        out_specs=(tokens, tokens, *params_placed),
        check_vma=False,
    )
```

```python
import functools

import jax
import jax.numpy as jnp
from jax import lax
from jax.experimental import pallas as pl
from jax.experimental.pallas import tpu as pltpu
from jax.sharding import PartitionSpec as P

D = 768
H = 12
HD = 64
LONG = 512
SHORT = 128
QUAD = 256
PAIR = 128
TILE = 768

EPSILON = 1e-05
BLOCKED = -1e30
LOW = jnp.bfloat16
WIDE = jnp.float32
ROOM = 38 << 20
EXTRA = 16

QUERY_BIAS, VALUE_BIAS, OUT_BIAS, ATTN_GAIN, ATTN_SHIFT, DOWN_BIAS, FFN_GAIN, FFN_SHIFT = range(8)


def dot(left, right, left_dim, right_dim):
    return lax.dot_general(
        left, right, (((left_dim,), (right_dim,)), ((), ())), preferred_element_type=WIDE
    )


def row_mean(value):
    return jnp.mean(value, axis=-1, keepdims=True)


def token_sum(value):
    return jnp.sum(value, axis=0, keepdims=True)


def whole(shape):
    zeros = (0,) * len(shape)
    return pl.BlockSpec(shape, lambda *_: zeros, pipeline_mode=pl.Buffered(1))


def place(target, sources, slots, me):
    rows = sources[0].shape[1]
    for source, distances in zip(sources, slots):
        for at, distance in enumerate(distances):
            start = pl.multiple_of((me ^ distance) * rows, rows)
            target[pl.ds(start, rows), :] = source[at]


def far(value):
    return pltpu.with_memory_space_constraint(value, pltpu.HBM)


def params():
    return pltpu.CompilerParams(vmem_limit_bytes=ROOM)


def cost(microseconds):
    return pl.CostEstimate(
        flops=int(microseconds * 1.1e9), bytes_accessed=1 << 20, transcendentals=0
    )


def unplace(targets, source, slots, me, top, rows):
    for target, distances in zip(targets, slots):
        for at, distance in enumerate(distances):
            start = pl.multiple_of((me ^ distance) * rows, rows)
            target[at, top : top + rows, :] = source(pl.ds(start, rows)).astype(LOW)


def to_all(targets, slots, top, rows):
    low = rows.astype(LOW)
    for target, distances in zip(targets, slots):
        for at in range(len(distances)):
            target[at, top : top + EXTRA, :] = low


def half_masks():
    lane = lax.broadcasted_iota(jnp.int32, (1, PAIR), 1)
    return [jnp.where(lane // HD == half, 1.0, 0.0) for half in range(2)]


def attend_kernel(slots, kind_ref, me_ref, x_ref, vec_ref, *refs):
    pieces = len(slots)
    sources, refs = refs[: 3 * pieces], refs[3 * pieces :]
    q_ref, k_ref, v_ref, ctx_ref, ctxt_ref, raised_ref, inv_ref, weight_ref = refs

    @pl.when(pl.program_id(1) == 0)
    def _():
        for at in range(3):
            place(weight_ref.at[at], sources[at * pieces : (at + 1) * pieces], slots, me_ref[0])

    x = x_ref[...]
    q_ref[...] = (dot(x, weight_ref[0], 1, 0) + vec_ref[QUERY_BIAS : QUERY_BIAS + 1]).astype(LOW)
    k_ref[...] = dot(x, weight_ref[1], 1, 0).astype(LOW)
    v_ref[...] = (dot(x, weight_ref[2], 1, 0) + vec_ref[VALUE_BIAS : VALUE_BIAS + 1]).astype(LOW)
    part = lax.broadcasted_iota(jnp.int32, (LONG, PAIR), 0) // SHORT
    lane = lax.broadcasted_iota(jnp.int32, (LONG, PAIR), 1)
    blocked = jnp.where(kind_ref[pl.program_id(1)] == 1, 0.0, BLOCKED)
    query_part = jnp.where((lane < LONG // SHORT) & (part != lane), blocked, 0.0).astype(LOW)
    key_part = jnp.where(part == lane, 1.0, 0.0).astype(LOW)
    halves = half_masks()
    everything = []
    for pair in range(QUAD // PAIR):
        cols = pl.ds(pair * PAIR, PAIR)
        q2 = q_ref[:, cols].astype(WIDE) * HD ** (-0.5)
        keys = jnp.concatenate([k_ref[:, cols], key_part], axis=1)
        for half in range(2):
            queries = jnp.concatenate([(q2 * halves[half]).astype(LOW), query_part], axis=1)
            everything.append(dot(keys, queries, 1, 1))
    low = []
    for head, scores in enumerate(everything):
        peak = jnp.max(scores, axis=0, keepdims=True)
        raised = jnp.exp(scores - peak).astype(LOW)
        raised_ref[0, head] = raised
        low.append(raised)
    for pair in range(QUAD // PAIR):
        cols = pl.ds(pair * PAIR, PAIR)
        v2t = v_ref[:, cols].T
        contexts, inverses = [], []
        for half in range(2):
            left = jnp.concatenate(
                [v2t[HD * half : HD * half + HD], jnp.ones((16, LONG), LOW)], axis=0
            )
            mixed = dot(left, low[pair * 2 + half], 1, 0)
            inverse = 1.0 / mixed[HD : HD + 1]
            contexts.append(mixed[:HD] * inverse)
            inverses.append(jnp.broadcast_to(inverse, (HD, LONG)))
        context = jnp.concatenate(contexts, axis=0)
        ctxt_ref[pair * PAIR : pair * PAIR + PAIR, :] = context.astype(LOW)
        ctx_ref[:, cols] = context.T.astype(LOW)
        inv_ref[:, cols] = jnp.concatenate(inverses, axis=0).T


def attend(kind, me, quads, x, weights, vec):
    pieces, slots, rows = weights
    count = x.shape[0]
    blocks, number, low = count // LONG, len(quads), quads[0]
    tokens = pl.BlockSpec((LONG, QUAD), lambda j, b, *_: (b, j))
    act = pltpu.HBM((count, number * QUAD), LOW)
    return pl.pallas_call(
        functools.partial(attend_kernel, slots),
        grid_spec=pltpu.PrefetchScalarGridSpec(
            num_scalar_prefetch=2,
            grid=(number, blocks),
            in_specs=[
                pl.BlockSpec((LONG, D), lambda j, b, *_: (b, 0)),
                pl.BlockSpec((8, QUAD), lambda j, b, *_: (0, j + low)),
            ]
            + [
                pl.BlockSpec((piece.shape[0], rows, QUAD), lambda j, b, *_, at=at: (0, at, j))
                for at in range(3)
                for piece in pieces
            ],
            out_specs=[
                tokens,
                tokens,
                tokens,
                tokens,
                pl.BlockSpec((QUAD, LONG), lambda j, b, *_: (j, b)),
                pl.BlockSpec((1, QUAD // HD, LONG, LONG), lambda j, b, *_: (b, j, 0, 0)),
                tokens,
                pl.BlockSpec((3, D, QUAD), lambda j, b, *_: (0, 0, j)),
            ],
        ),
        out_shape=[
            act,
            act,
            act,
            act,
            pltpu.HBM((number * QUAD, count), LOW),
            pltpu.HBM((blocks, number * QUAD // HD, LONG, LONG), LOW),
            pltpu.HBM((count, number * QUAD), WIDE),
            pltpu.HBM((3, D, number * QUAD), LOW),
        ],
        compiler_params=params(),
        cost_estimate=cost(0.1),
        name="attend",
    )(kind, me, far(x), far(vec), *(far(piece) for piece in list(pieces) * 3))


def attend_back_kernel(
    slots,
    me_ref,
    xt_ref,
    d_ref,
    ctx_ref,
    inv_ref,
    q_ref,
    k_ref,
    v_ref,
    raised_ref,
    dq_ref,
    dk_ref,
    dv_ref,
    *refs,
):
    targets, (totals, biases) = refs[:-2], refs[-2:]
    block = pl.program_id(0)
    halves = half_masks()
    minus = jnp.full((LONG, PAIR), -1.0, LOW)
    work = []
    for pair in range(QUAD // PAIR):
        cols = pl.ds(pair * PAIR, PAIR)
        d2 = d_ref[:, cols].astype(WIDE) * inv_ref[:, cols] * HD ** (-0.5)
        along = d2 * ctx_ref[:, cols].astype(WIDE)
        q2 = q_ref[:, cols].astype(WIDE)
        values = jnp.concatenate([v_ref[:, cols], minus], axis=1)
        for half in range(2):
            dm = (d2 * halves[half]).astype(LOW)
            am = (along * halves[half]).astype(LOW)
            qm = (q2 * halves[half]).astype(LOW)
            dp = dot(values, jnp.concatenate([dm, am], axis=1), 1, 1)
            work.append((pair, half, dm, qm, dp))
    k2ts = [k_ref[:, pl.ds(pair * PAIR, PAIR)].T for pair in range(QUAD // PAIR)]
    done = []
    for pair, half, dm, qm, dp in work:
        raised = raised_ref[0, pair * 2 + half]
        ds = (raised.astype(WIDE) * dp).astype(LOW)
        done.append((pair, half, raised, ds, dm, qm))
    for pair in range(QUAD // PAIR):
        cols = pl.ds(pair * PAIR, PAIR)
        dqt, dk, dv = [], 0, 0
        for p, half, raised, ds, dm, qm in done:
            if p == pair:
                dqt.append(dot(k2ts[pair][HD * half : HD * half + HD], ds, 1, 0))
        both = [item for item in done if item[0] == pair]
        wide = lambda at, axis: jnp.concatenate([item[at] for item in both], axis=axis)
        dv = dot(wide(2, 1), wide(4, 0), 1, 0)
        dk = dot(wide(3, 1), wide(5, 0), 1, 0)
        dv_ref[:, cols] = (dv * HD**0.5).astype(LOW)
        dk_ref[:, cols] = dk.astype(LOW)
        dq_ref[:, cols] = jnp.concatenate(dqt, axis=0).T.astype(LOW)
    xt = xt_ref[...]
    for at, ref in enumerate((dq_ref, dk_ref, dv_ref)):
        grad = dot(xt, ref[...], 1, 0)

        @pl.when(block == 0)
        def _(grad=grad, at=at):
            totals[at] = grad

        @pl.when(block != 0)
        def _(grad=grad, at=at):
            totals[at] += grad

    sums = jnp.concatenate(
        [
            token_sum(dq_ref[...].astype(WIDE)),
            token_sum(dv_ref[...].astype(WIDE)),
            jnp.zeros((EXTRA - 2, QUAD), WIDE),
        ],
        axis=0,
    )

    @pl.when(block == 0)
    def _():
        biases[...] = sums

    @pl.when(block != 0)
    def _():
        biases[...] += sums

    @pl.when(block == pl.num_programs(0) - 1)
    def _():
        rows = (targets[0].shape[1] - EXTRA) // 3
        for at in range(3):
            unplace(
                targets, lambda part, at=at: totals[at, part], slots, me_ref[0], at * rows, rows
            )
        to_all(targets, slots, 3 * rows, biases[...])


def attend_back(me, slots, quad, at, xt, d, ctx, inv, q, k, v, raised):
    count = q.shape[0]
    tokens = pl.BlockSpec((LONG, QUAD), lambda b, *_: (b, at))
    grads = pl.BlockSpec((LONG, QUAD), lambda b, *_: (b, 0))
    act = pltpu.HBM((count, QUAD), LOW)
    rows = D // sum(map(len, slots))
    halves = [(max(len(part), 1), 3 * rows + EXTRA, QUAD) for part in slots]
    return pl.pallas_call(
        functools.partial(attend_back_kernel, slots),
        grid_spec=pltpu.PrefetchScalarGridSpec(
            num_scalar_prefetch=1,
            grid=(count // LONG,),
            in_specs=[
                pl.BlockSpec((D, LONG), lambda b, *_: (0, b)),
                pl.BlockSpec((LONG, QUAD), lambda b, *_: (b, quad)),
            ]
            + [tokens] * 5
            + [pl.BlockSpec((1, QUAD // HD, LONG, LONG), lambda b, *_: (b, at, 0, 0))],
            out_specs=[grads, grads, grads] + [whole(half) for half in halves],
            scratch_shapes=[pltpu.VMEM((3, D, QUAD), WIDE), pltpu.VMEM((EXTRA, QUAD), WIDE)],
        ),
        out_shape=[act, act, act] + [pltpu.HBM(half, LOW) for half in halves],
        compiler_params=params(),
        cost_estimate=cost(2),
        name="attend_back",
    )(
        me, far(xt), d, *(value if quad else far(value) for value in (ctx, inv, q, k, v)), far(raised)
    )


def out_kernel(places, groups, me_ref, x_ref, vec_ref, *refs):
    contexts, refs = refs[:groups], refs[groups:]
    norm_ref, inv_ref, hl_ref, hlt_ref, wo_ref = refs[-5:]
    at, col = 0, 0
    for slots in places:
        sources = refs[at : at + len(slots)]
        at += len(slots)
        width = sources[0].shape[2]
        place(wo_ref.at[:, col : col + width], sources, slots, me_ref[0])
        col += width
    bias = vec_ref[OUT_BIAS : OUT_BIAS + 1]
    gain = vec_ref[ATTN_GAIN : ATTN_GAIN + 1]
    shift = vec_ref[ATTN_SHIFT : ATTN_SHIFT + 1]
    wo = wo_ref[...]
    step = 256
    for at in range(0, x_ref.shape[0], step):
        rows = pl.ds(at, step)
        context = jnp.concatenate([ref[rows] for ref in contexts], axis=1)
        total = x_ref[rows].astype(WIDE) + dot(context, wo, 1, 0) + bias
        centered = total - row_mean(total)
        inverse = lax.rsqrt(row_mean(centered * centered) + EPSILON)
        norm = centered * inverse
        norm_ref[rows] = norm
        inv_ref[rows] = jnp.broadcast_to(inverse, (step, 128))
        hidden = (norm * gain + shift).astype(LOW)
        hl_ref[rows] = hidden
        hlt_ref[:, rows] = hidden.T


def out_call(me, contexts, x, weights, vec):
    count = x.shape[0]
    specs, values = [], []
    for pieces, _, rows in weights:
        for piece in pieces:
            specs.append(pl.BlockSpec((piece.shape[0], rows, piece.shape[2]), lambda *_: (0, 3, 0)))
            values.append(piece)
    shapes = [((count, D), WIDE), ((count, 128), WIDE), ((count, D), LOW), ((D, count), LOW), ((D, D), LOW)]
    outs = [pltpu.HBM(shape, dtype) for shape, dtype in shapes]
    outs[2] = jax.ShapeDtypeStruct(*shapes[2])
    return pl.pallas_call(
        functools.partial(out_kernel, [slots for _, slots, _ in weights], len(contexts)),
        grid_spec=pltpu.PrefetchScalarGridSpec(
            num_scalar_prefetch=1,
            grid=(1,),
            in_specs=[whole((count, D)), whole((8, D))]
            + [whole(context.shape) for context in contexts]
            + specs,
            out_specs=[whole(shape) for shape, _ in shapes],
        ),
        out_shape=outs,
        compiler_params=params(),
        cost_estimate=cost(0.1),
        name="out",
    )(me, *(far(value) for value in (x, vec, *contexts, *values)))


def up_kernel(slots, me_ref, hl_ref, bu_ref, *refs):
    own, other = slots
    ups, (act_ref, slope_ref, wu_ref) = refs[:-3], refs[-3:]
    step = 256
    first_half = pl.program_id(0) < pl.num_programs(0) // 2

    @pl.when(first_half)
    def _():
        place(wu_ref.at[0], ups[: len(own)], own, me_ref[0])

    @pl.when(jnp.logical_not(first_half))
    def _():
        place(wu_ref.at[0], ups[len(own) :], other, me_ref[0])

    bias = bu_ref[...]
    weight = wu_ref[0]
    for at in range(0, hl_ref.shape[0], step):
        rows = pl.ds(at, step)
        before = dot(hl_ref[rows], weight, 1, 0) + bias
        half = 0.5 * (1.0 + lax.erf(before * 0.7071067811865476))
        act_ref[rows] = (before * half).astype(LOW)
        slope_ref[rows] = (
            half + before * jnp.exp(-0.5 * before * before) * 0.3989422804014327
        ).astype(LOW)


def up_call(me, hl, own, other, rows, up_bias):
    count = hl.shape[0]
    hidden = up_bias.shape[1]
    steps = hidden // TILE
    half = steps // 2
    cols = lambda r: pl.BlockSpec((r, TILE), lambda j, me: (0, j ^ me[1]))
    early = lambda j, *_: (0, jnp.minimum(j, half - 1), 0)
    late = lambda j, *_: (0, jnp.maximum(j - half, 0), 0)
    return pl.pallas_call(
        functools.partial(up_kernel, (own[1], other[1])),
        grid_spec=pltpu.PrefetchScalarGridSpec(
            num_scalar_prefetch=1,
            grid=(steps,),
            in_specs=[whole((count, D)), cols(1)]
            + [pl.BlockSpec((piece.shape[0], rows, D), early) for piece in own[0]]
            + [pl.BlockSpec((piece.shape[0], rows, D), late) for piece in other[0]],
            out_specs=[
                cols(count),
                cols(count),
                pl.BlockSpec((1, D, TILE), lambda j, me: (j ^ me[1], 0, 0)),
            ],
        ),
        out_shape=[
            jax.ShapeDtypeStruct((count, hidden), LOW),
            pltpu.HBM((count, hidden), LOW),
            pltpu.HBM((steps, D, TILE), LOW),
        ],
        compiler_params=params(),
        cost_estimate=cost(0.1),
        name="up",
    )(me, hl, *(far(value) for value in (up_bias, *own[0], *other[0])))


def down_kernel(slots, me_ref, act_ref, norm_ref, vec_ref, cot_ref, *refs):
    sources = refs[: len(slots)]
    out_ref, grad_ref, low_ref, sums_ref, wd_ref = refs[len(slots) :]

    @pl.when(pl.program_id(0) == 0)
    def _():
        place(wd_ref, sources, slots, me_ref[0])

    row = lambda at: vec_ref[at : at + 1]
    total = (
        norm_ref[...] * row(ATTN_GAIN)
        + row(ATTN_SHIFT)
        + (dot(act_ref[...], wd_ref[...], 1, 0) + row(DOWN_BIAS))
    )
    centered = total - row_mean(total)
    inverse = lax.rsqrt(row_mean(centered * centered) + EPSILON)
    norm = centered * inverse
    out_ref[...] = (norm * row(FFN_GAIN) + row(FFN_SHIFT)).astype(LOW)
    grad_out = cot_ref[...].astype(WIDE)
    scaled = grad_out * row(FFN_GAIN)
    grad = inverse * (scaled - row_mean(scaled) - norm * row_mean(scaled * norm))
    grad_ref[...] = grad
    low = grad.astype(LOW)
    low_ref[...] = low
    sums = jnp.concatenate(
        [
            token_sum(grad_out * norm),
            token_sum(grad_out),
            token_sum(low.astype(WIDE)),
            jnp.zeros((5, D), WIDE),
        ],
        axis=0,
    )

    @pl.when(pl.program_id(0) == 0)
    def _():
        sums_ref[...] = sums

    @pl.when(pl.program_id(0) != 0)
    def _():
        sums_ref[...] += sums


def down_call(me, act, third, norm, vec, cotangent):
    pieces, slots, _ = third
    count, hidden = act.shape
    tile = 256
    rows = lambda c: pl.BlockSpec((tile, c), lambda i, *_: (i, 0))
    return pl.pallas_call(
        functools.partial(down_kernel, slots),
        grid_spec=pltpu.PrefetchScalarGridSpec(
            num_scalar_prefetch=1,
            grid=(count // tile,),
            in_specs=[rows(hidden), rows(D), whole((8, D)), rows(D)]
            + [whole(piece.shape) for piece in pieces],
            out_specs=[rows(D), rows(D), rows(D), whole((8, D)), whole((hidden, D))],
        ),
        out_shape=[
            pltpu.HBM((count, D), LOW),
            jax.ShapeDtypeStruct((count, D), WIDE),
            jax.ShapeDtypeStruct((count, D), LOW),
            pltpu.HBM((8, D), WIDE),
            pltpu.HBM((hidden, D), LOW),
        ],
        compiler_params=params(),
        cost_estimate=cost(13),
        name="down",
    )(me, act, *(far(value) for value in (norm, vec, cotangent, *pieces)))


def down_grad_kernel(owner_ref, me_ref, act_ref, low_ref, keep_ref, send_ref, scratch):
    rows = keep_ref.shape[1]
    scratch[...] = dot(act_ref[...], low_ref[...], 0, 0).astype(LOW)
    mine = lax.rem(me_ref[0], 2) * rows
    keep_ref[0] = scratch[pl.ds(pl.multiple_of(mine, rows), rows)]
    send_ref[0] = scratch[pl.ds(pl.multiple_of(rows - mine, rows), rows)]


def down_grad_plain_kernel(act_ref, low_ref, grad_ref):
    grad_ref[...] = dot(act_ref[...], low_ref[...], 0, 0).astype(LOW)


def down_grad_plain_call(act, low):
    count, hidden = act.shape
    return pl.pallas_call(
        down_grad_plain_kernel,
        grid=(hidden // TILE,),
        in_specs=[pl.BlockSpec((count, TILE), lambda j: (0, j)), whole((count, D))],
        out_specs=pl.BlockSpec((TILE, D), lambda j: (j, 0)),
        out_shape=pltpu.HBM((hidden, D), LOW),
        compiler_params=params(),
        cost_estimate=cost(9),
        name="down_grad",
    )(act, low)


def down_grad_call(me, slots, rows, act, low):
    count, hidden = act.shape
    number = len(slots[0])
    pair = 2 * rows
    owners = (me // 2) ^ (jnp.array(slots[0], jnp.int32) // 2)
    part = pl.BlockSpec((1, rows, D), lambda j, *_: (j, 0, 0))
    half = pltpu.HBM((number, rows, D), LOW)
    return pl.pallas_call(
        down_grad_kernel,
        grid_spec=pltpu.PrefetchScalarGridSpec(
            num_scalar_prefetch=2,
            grid=(number,),
            in_specs=[
                pl.BlockSpec((count, pair), lambda j, owner, _: (0, owner[j])),
                whole((count, D)),
            ],
            out_specs=[part, part],
            scratch_shapes=[pltpu.VMEM((pair, D), LOW)],
        ),
        out_shape=[half, half],
        compiler_params=params(),
        cost_estimate=cost(number),
        name="down_grad",
    )(owners, me, act, low)


def up_grad_kernel(
    slots, me_ref, low_ref, wd_ref, slope_ref, hlt_ref, wu_ref, grad_ref,
    keep_ref, send_ref, bias_ref, hidden_ref, before_scr, grad_scr,
):
    step = pl.program_id(0)
    before_scr[...] = (dot(low_ref[...], wd_ref[...], 1, 1) * slope_ref[...].astype(WIDE)).astype(
        LOW
    )
    before = before_scr[...]
    grad_scr[...] = dot(hlt_ref[...], before, 1, 0).astype(LOW)
    unplace(
        (keep_ref, send_ref), lambda part: grad_scr[part], slots, me_ref[0], 0, keep_ref.shape[1]
    )
    bias_ref[...] = jnp.broadcast_to(token_sum(before.astype(WIDE)), (8, TILE))
    back = dot(before, wu_ref[0], 1, 1)

    @pl.when(step == 0)
    def _():
        hidden_ref[...] = back + grad_ref[...]

    @pl.when(step != 0)
    def _():
        hidden_ref[...] += back


def up_grad_call(me, slots, tiles, low, down, slope, hlt, up, grad):
    count = slope.shape[0]
    first, steps = tiles[0], len(tiles)
    kept, rows = len(slots[0]), D // (len(slots[0]) + len(slots[1]))
    part = pl.BlockSpec((kept, rows, TILE), lambda j, *_: (0, j, 0))
    half = pltpu.HBM((kept, steps * rows, TILE), LOW)
    return pl.pallas_call(
        functools.partial(up_grad_kernel, slots),
        grid_spec=pltpu.PrefetchScalarGridSpec(
            num_scalar_prefetch=1,
            grid=(steps,),
            in_specs=[
                whole((count, D)),
                pl.BlockSpec((TILE, D), lambda j, *_: (j + first, 0)),
                pl.BlockSpec((count, TILE), lambda j, *_: (0, j + first)),
                whole((D, count)),
                pl.BlockSpec((1, D, TILE), lambda j, *_: (j + first, 0, 0)),
                whole((count, D)),
            ],
            out_specs=[
                part,
                part,
                pl.BlockSpec((8, TILE), lambda j, *_: (j, 0)),
                whole((count, D)),
            ],
            scratch_shapes=[pltpu.VMEM((count, TILE), LOW), pltpu.VMEM((D, TILE), LOW)],
        ),
        out_shape=[
            half,
            half,
            pltpu.HBM((8 * steps, TILE), WIDE),
            jax.ShapeDtypeStruct((count, D), WIDE),
        ],
        compiler_params=params(),
        cost_estimate=cost(6 * steps),
        name="up_grad",
    )(me, low, far(down), far(slope), hlt, far(up), grad)


def norm_back_kernel(
    slots, groups, me_ref, hidden_ref, norm_ref, inv_ref, vec_ref, wo_ref, ffn_ref, up_ref, *refs
):
    contexts, refs = refs[:groups], refs[groups:]
    grad_ref, keep_ref, send_ref, ctx_ref, low_scr, out_scr = refs
    count = hidden_ref.shape[0]
    step = 256
    gain = vec_ref[ATTN_GAIN : ATTN_GAIN + 1]
    wo = wo_ref[...]
    sums = 0
    for at in range(0, count, step):
        rows = pl.ds(at, step)
        hidden = hidden_ref[rows]
        norm = norm_ref[rows]
        scaled = hidden * gain
        grad = inv_ref[rows][:, 0:1] * (
            scaled - row_mean(scaled) - norm * row_mean(scaled * norm)
        )
        grad_ref[rows] = grad
        low = grad.astype(LOW)
        low_scr[rows] = low
        sums = sums + jnp.concatenate(
            [
                token_sum(hidden * norm),
                token_sum(hidden),
                token_sum(low.astype(WIDE)),
                jnp.zeros((5, D), WIDE),
            ],
            axis=0,
        )
        ctx_ref[rows] = dot(low, wo, 1, 1).astype(LOW)
    at = 0
    for ref in contexts:
        out_scr[at : at + ref.shape[0], :] = dot(ref[...], low_scr[...], 1, 0).astype(LOW)
        at += ref.shape[0]
    quads = D // QUAD
    rows = keep_ref.shape[1] // quads - EXTRA
    steps = up_ref.shape[0] // 8
    extra = [sums[2:3], sums[:2], ffn_ref[2:3], ffn_ref[:2]]
    extra += [up_ref[8 * at : 8 * at + 1] for at in range(steps)]
    extra.append(jnp.zeros((EXTRA - 6 - steps, D), WIDE))
    extra = jnp.concatenate(extra, axis=0)
    for quad in range(quads):
        cols = slice(quad * QUAD, quad * QUAD + QUAD)
        top = quad * (rows + EXTRA)
        targets = keep_ref, send_ref
        unplace(targets, lambda part: out_scr[part, cols], slots, me_ref[0], top, rows)
        to_all(targets, slots, top + rows, extra[:, cols])


def norm_back_call(me, slots, hidden, norm, inv, vec, contexts, wo, ffn_sums, up_sums):
    count = hidden.shape[0]
    kept, rows = len(slots[0]), D // (len(slots[0]) + len(slots[1]))
    half = (kept, (rows + EXTRA) * (D // QUAD), QUAD)
    return pl.pallas_call(
        functools.partial(norm_back_kernel, slots, len(contexts)),
        grid_spec=pltpu.PrefetchScalarGridSpec(
            num_scalar_prefetch=1,
            grid=(1,),
            in_specs=[
                whole((count, D)),
                whole((count, D)),
                whole((count, 128)),
                whole((8, D)),
                whole((D, D)),
                whole((8, D)),
                whole(up_sums.shape),
            ]
            + [whole(context.shape) for context in contexts],
            out_specs=[whole((count, D)), whole(half), whole(half), whole((count, D))],
            scratch_shapes=[pltpu.VMEM((count, D), LOW), pltpu.VMEM((D, D), LOW)],
        ),
        out_shape=[
            pltpu.HBM((count, D), WIDE),
            pltpu.HBM(half, LOW),
            pltpu.HBM(half, LOW),
            jax.ShapeDtypeStruct((count, D), LOW),
        ],
        compiler_params=params(),
        cost_estimate=cost(12),
        name="norm_back",
    )(me, hidden, norm, inv, far(vec), wo, far(ffn_sums), far(up_sums), *contexts)


def input_grad_kernel(places, groups, grad_ref, *refs):
    weights, refs = refs[:groups], refs[groups:]
    total = grad_ref[...]
    for quad, (group, at) in enumerate(places):
        for matrix in range(3):
            total = total + dot(
                refs[3 * quad + matrix][...],
                weights[group][matrix, :, at * QUAD : at * QUAD + QUAD],
                1,
                1,
            )
    refs[-1][...] = total


def input_grad_call(pieces, places, weights, grad):
    count = grad.shape[0]
    tile = 512
    tokens = lambda width: pl.BlockSpec((tile, width), lambda i: (i, 0))
    values = [value for piece in pieces for value in piece]
    return pl.pallas_call(
        functools.partial(input_grad_kernel, places, len(weights)),
        grid=(count // tile,),
        in_specs=[tokens(D)]
        + [whole(weight.shape) for weight in weights]
        + [tokens(QUAD) for _ in values],
        out_specs=tokens(D),
        out_shape=pltpu.HBM((count, D), WIDE),
        compiler_params=params(),
        cost_estimate=cost(0.1),
        name="input_grad",
    )(*(far(value) for value in (grad, *weights, *values)))


def pack_kernel(places, *refs):
    for ref, (row, col) in zip(refs, places):
        refs[-1][row : row + ref.shape[0], col : col + ref.shape[1]] = ref[...]


def pack(parts, width):
    if any(array.shape[0] % 16 for line in parts for array, _ in line):
        return jnp.concatenate(
            [
                jnp.concatenate([a[:, width * at : width * (at + 1)] for a, at in line], axis=1)
                for line in parts
            ]
        )
    places, specs, row = [], [], 0
    for line in parts:
        for at, (array, block) in enumerate(line):
            places.append((row, at * width))
            specs.append(pl.BlockSpec((array.shape[0], width), lambda i, block=block: (0, block)))
        row += line[0][0].shape[0]
    shape = (row, width * len(parts[0]))
    return pl.pallas_call(
        functools.partial(pack_kernel, places),
        grid=(1,),
        in_specs=specs,
        out_specs=pl.BlockSpec(shape, lambda i: (0, 0)),
        out_shape=pltpu.HBM(shape, LOW),
        compiler_params=params(),
        cost_estimate=cost(1),
        name="pack",
    )(*(far(array) for line in parts for array, _ in line))


def swap(value, mask, count):
    return lax.ppermute(value, "fsdp", [(i, i ^ mask) for i in range(count)])


def after(value, *others):
    return lax.optimization_barrier((value,) + others)[0] if others else value


class Gather:
    def __init__(self, piece, count, half=False):
        self.unit = 1
        if half:
            rows = piece.shape[0] // 2
            piece = lax.dynamic_slice_in_dim(piece, lax.axis_index("rep") * rows, rows, 0)
            self.unit = 2
        self.parts, self.count = [(piece[None], [0])], count
        self.hops = [count >> at for at in range(1, count.bit_length() - 2)]

    def far(self, *others):
        held, _ = self.parts[0]
        self.other = swap(after(held, *others), self.hops[0], self.count)

    def land(self, *others):
        held, order = self.parts[0]
        held = jnp.concatenate([held, after(self.other, *others)], axis=0)
        mask = self.hops.pop(0) * self.unit
        self.parts = [(held, order + [at ^ mask for at in order])]
        return held

    def far_but(self, last):
        while len(self.hops) > last:
            self.far()
            self.land()
        return self.parts[0][0]

    def send(self, part, hop):
        held, order = self.parts[part]
        if hop == "rep":
            other, mask = lax.ppermute(held, "rep", [(0, 1), (1, 0)]), 1
        else:
            other, mask = swap(held, hop, self.count), hop * self.unit
        self.parts.append((other, [at ^ mask for at in order]))

    def tie(self, part, *others):
        held, order = self.parts[part]
        self.parts[part] = (after(held, *others), order)
        return self.parts[part][0]


def matrices(gather, number, rows, me):
    pieces, slots = zip(*gather.parts)
    if rows % 16 == 0:
        return pieces, slots, rows
    parts = in_order(jnp.concatenate(pieces)[:, : number * rows], slots, me)
    count, _, width = parts.shape
    parts = jnp.moveaxis(parts.reshape(count, number, rows, width), 1, 0)
    return (parts.reshape(1, number * count * rows, width),), ([0],), count * rows


def matrix_halves(gather, number, rows, side):
    if rows % 16 == 0:
        split = [([], []), ([], [])]
        for piece, order in gather.parts:
            pieces, slots = split[order[0] & 1]
            pieces.append(piece)
            slots.append([at >> 1 for at in order])
        return *split, rows
    pieces, slots = zip(*gather.parts)
    parts = in_order(jnp.concatenate(pieces), slots, side)
    count, width = parts.shape[0] // 2, parts.shape[-1]
    parts = jnp.moveaxis(parts.reshape(count, number, rows, width), 1, 0)
    parts = parts.reshape(1, number * count * rows, width)
    middle = parts.shape[1] // 2
    return ([parts[:, :middle]], [[0]]), ([parts[:, middle:]], [[0]]), count * rows


def in_order(held, slots, me):
    count = held.shape[0]
    distance = jnp.array([at for order in slots for at in order], jnp.int32)
    chosen = (jnp.arange(count, dtype=jnp.int32) ^ me)[:, None] == distance[None]
    return jnp.einsum(
        "ij,jrc->irc", chosen.astype(LOW), held, preferred_element_type=WIDE
    ).astype(LOW)


def to_slots(parts, slots, me):
    count = parts.shape[0]
    bit = 1
    while bit < count:
        pairs = parts.reshape((count // (2 * bit), 2, bit) + parts.shape[1:])
        parts = jnp.where((me & bit) != 0, pairs[:, ::-1], pairs).reshape(parts.shape)
        bit *= 2
    return tuple(
        jnp.concatenate([parts[at : at + 1] for at in distances]) for distances in slots
    )


def sum_order(count):
    bits = count.bit_length() - 2
    order = [
        sum(2 << place for place in range(bits) if at >> (bits - 1 - place) & 1)
        for at in range(count // 2)
    ]
    return order, [at ^ 1 for at in order]


class Sum:
    def __init__(self, keep, send, count, half=False):
        self.terms, self.send, self.count = [(keep, ())], send, count
        self.slots, self.kernel = keep.shape[0], False
        self.half, self.bit, self.total = half, 1, None

    def start(self, *others):
        send = after(self.send, *others) if others else self.send
        if self.half == "now" or self.bit == self.count:
            self.other = lax.ppermute(send, "rep", [(0, 1), (1, 0)])
        else:
            self.other = swap(send, self.bit, self.count)

    def added(self, *cuts):
        total = 0
        for array, before in self.terms:
            for each in (*before, *cuts):
                array = each(array)
            total = total + array.astype(WIDE)
        return total

    def cut(self, each):
        self.terms = [(array, (*before, each)) for array, before in self.terms]

    def land(self, *others):
        other = after(self.other, *others) if others else self.other
        if self.bit == self.count:
            if self.half:
                low = lax.axis_index("rep") == 0
                both = jnp.where(low, self.send, other), jnp.where(low, other, self.send)
                self.total = jnp.concatenate(both, axis=1)[0].astype(WIDE)
            else:
                self.total = (self.send.astype(WIDE) + other.astype(WIDE))[0]
            return self.total
        self.terms.append((other, ()))
        if self.half == "now":
            self.half = "done"
        else:
            self.bit *= 2
            if self.half is True:
                return self.halve()
        if self.bit == self.count:
            self.send = self.added().astype(LOW)
            return self.send
        middle = self.slots // 2
        if self.kernel and self.slots > 1:
            self.send = add_upper([array for array, _ in self.terms])
            self.kernel = False
        else:
            self.send = self.added(lambda term: term[middle:]).astype(LOW)
        self.cut(lambda term: term[:middle])
        self.slots = middle
        return self.send

    def halve(self):
        mine = lax.axis_index("rep")
        _, rows, width = self.send.shape

        def pick(at):
            return lambda term: lax.dynamic_slice_in_dim(term, at * (rows // 2), rows // 2, 1)

        self.send = self.added(pick(1 - mine)).astype(LOW)
        self.cut(pick(mine))
        self.half = "now"
        return self.send

    def finish(self):
        while self.total is None:
            self.start()
            self.land()


def add_kernel(*refs):
    total = 0
    for ref in refs[:-1]:
        total = total + ref[...].astype(WIDE)
    refs[-1][...] = total.astype(LOW)


def add_upper(terms):
    slots, rows, width = terms[0].shape
    upper = pl.BlockSpec((1, rows, width), lambda at: (at + slots // 2, 0, 0))
    return pl.pallas_call(
        add_kernel,
        grid=(slots // 2,),
        in_specs=[upper] * len(terms),
        out_specs=pl.BlockSpec((1, rows, width), lambda at: (at, 0, 0)),
        out_shape=pltpu.HBM((slots // 2, rows, width), LOW),
        compiler_params=params(),
        cost_estimate=cost(12),
        name="add",
    )(*(far(term) for term in terms))


def joined(sums):
    first = sums[0]
    whole = Sum(first.send, jnp.concatenate([item.send for item in sums], axis=1), first.count)
    whole.bit, whole.slots = first.bit, first.slots
    whole.terms = [(jnp.concatenate([item.added() for item in sums], axis=1), ())]
    return whole


def shards(
    inputs,
    block_kind,
    query_weight,
    query_bias,
    key_weight,
    value_weight,
    value_bias,
    out_weight,
    out_bias,
    attn_gain,
    attn_shift,
    up_weight,
    up_bias,
    down_weight,
    down_bias,
    ffn_gain,
    ffn_shift,
    cotangent,
):
    rows = query_weight.shape[0]
    count = D // rows
    hidden = up_weight.shape[1]
    steps = hidden // TILE
    vectors = (
        query_bias,
        value_bias,
        out_bias,
        attn_gain,
        attn_shift,
        down_bias,
        ffn_gain,
        ffn_shift,
    )
    down_rows = down_weight.shape[0]
    used = 8 * rows + up_bias.shape[0]
    spare = 16 * QUAD
    packed, at = 0, 0
    for value in vectors + (up_bias,):
        packed = packed + jnp.pad(value, (at, spare - at - value.shape[0]))
        at += value.shape[0]
    me = lax.axis_index("fsdp").astype(jnp.int32)
    own_rows = rows % 16 == 0
    mine = me.reshape(1)
    none = jnp.zeros((1,), jnp.int32)
    me_or_none = mine if own_rows else none
    attn_weights = (query_weight, key_weight, value_weight, out_weight)

    first = Gather(
        pack([[(w, 0)] for w in attn_weights] + [[(packed.reshape(16, QUAD), 0)]], QUAD), count
    )
    inputs_t = inputs.T
    first.far()
    at = first.land()
    rest = Gather(pack([[(w, 1), (w, 2)] for w in attn_weights], QUAD), count)
    second = Gather(pack([[(up_weight, at)] for at in range(steps)], TILE), count, half=True)
    rest.far(at)
    at = rest.land(first.far_but(0), second.parts[0][0])
    third = Gather(down_weight, count)
    first.send(0, 2)
    first.send(0, 1)
    rest.far_but(1)
    rest.far()
    second.far(at)
    at = second.land(inputs_t)
    at = rest.land(at)
    at = first.tie(1, at)
    first.send(1, 1)
    rest.send(0, 2)
    rest.send(0, 1)
    second.far_but(1)
    second.far()
    third.far(at)

    pieces, slots = zip(*first.parts)
    columns = -(-used // QUAD)
    whole_packed = in_order(
        jnp.concatenate([piece[:, 4 * rows : 4 * rows + columns] for piece in pieces]), slots, me
    ).reshape(count, columns * QUAD)
    vec = (
        jnp.moveaxis(whole_packed[:, : 8 * rows].reshape(count, 8, rows), 1, 0)
        .reshape(8, D)
        .astype(WIDE)
    )
    all_up_bias = whole_packed[:, 8 * rows : used].reshape(1, hidden).astype(WIDE)

    places = [(0, 0), (1, 0), (1, 1)]
    heads = [
        attend(
            block_kind, me_or_none, [0], inputs, matrices(first, 4, rows, me), after(vec, all_up_bias)
        )
    ]
    at = second.land(heads[0][3])
    second.send(0, 2)
    second.send(0, "rep")
    second.send(0, 1)
    at = third.land(at)
    third.far_but(1)
    third.far()
    at = rest.tie(1, at)
    rest.send(1, 1)
    heads.append(
        attend(
            block_kind, me_or_none, [1, 2], after(inputs, at), matrices(rest, 4, rows, me), vec
        )
    )
    contexts = [group[3] for group in heads]
    contexts_t = [group[4] for group in heads]
    at = second.tie(1, heads[1][3])
    at = second.tie(2, at)
    second.send(1, "rep")
    second.send(1, 1)
    second.send(2, 1)
    at = third.land(at)
    third.send(0, 2)
    third.send(0, 1)
    norm, first_inv, hl, hlt, wo = out_call(
        me_or_none,
        contexts,
        after(inputs, at),
        [matrices(first, 4, rows, me), matrices(rest, 4, rows, me)],
        vec,
    )
    second.tie(4, hl)
    second.send(4, 1)
    rank = lax.axis_index("rep").astype(jnp.int32)
    own, other, block = matrix_halves(second, steps, rows, 2 * me + rank)
    flip = jnp.stack([me, rank * (steps // 2)]) if own_rows else jnp.zeros((2,), jnp.int32)
    act, slope, up = up_call(flip, hl, own, other, block, all_up_bias)
    third.tie(1, act)
    third.send(1, 1)
    pieces = matrices(third, 1, down_rows, me)
    layer_out, grad, low, ffn_sums, down = down_call(
        mine if down_rows % 16 == 0 else none, act, pieces, norm, vec, cotangent
    )

    order = sum_order(count)
    quads = D // QUAD

    def halves_of(keep, send, k, groups=1):
        if own_rows:
            return keep, send
        width = keep.shape[-1]
        tall = keep.shape[1] // groups
        everything = []
        for group in jnp.split(keep[0], groups):
            parts = jnp.moveaxis(group[: k * D].reshape(k, count, rows, width), 0, 1)
            everything.append(parts.reshape(count, k * rows, width))
            everything.append(jnp.broadcast_to(group[None, k * D :], (count, tall - k * D, width)))
        return to_slots(jnp.concatenate(everything, axis=1), order, me)

    kernel_order = order if own_rows else ([0], [])
    if 2 * down_rows % 128 == 0:
        middle = count // 4
        near, far = ([part[at] for part in order] for at in (slice(middle), slice(middle, None)))
        far_keep, far_send = down_grad_call(mine, far, down_rows, act, low)
        far_other = swap(far_send, 1, count)
        near_keep, near_send = down_grad_call(mine, near, down_rows, act, after(low, far_keep))
        sum_down = Sum(near_keep, None, count)
        sum_down.bit, sum_down.slots, sum_down.kernel = 2, middle, True
        far_other = after(far_other, near_keep)
        sum_down.send = (far_keep.astype(WIDE) + far_other.astype(WIDE)).astype(LOW)
        at = sum_down.send
        sum_down.start()
        sum_down.terms.append((swap(near_send, 1, count), ()))
    else:
        parts = down_grad_plain_call(act, low).reshape(count, down_rows, D)
        sum_down = Sum(*to_slots(parts, order, me), count)
        sum_down.start()
        at = sum_down.land()
        sum_down.start()

    keep, send, up_sums, grad_hidden = up_grad_call(
        me_or_none, kernel_order, list(range(steps)), low, down, slope, hlt, up, after(grad, at)
    )
    sum_up = Sum(*halves_of(keep, send, steps), count, half=True)
    sum_up.start()
    at = sum_down.land(grad_hidden)
    sum_down.start()
    at = sum_up.land(at)
    sum_up.start()
    grad_attn, keep, send, grad_ctx = norm_back_call(
        me_or_none, kernel_order, after(grad_hidden, at), norm, first_inv, vec, contexts_t, wo,
        ffn_sums, up_sums,
    )
    sum_out = Sum(*halves_of(keep, send, 1, quads), count)
    sum_out.start()
    at = grad_attn

    def back(quad, slots, *others):
        group, at = places[quad]
        q, k, v, ctx, _, raised, inv, _ = heads[group]
        dq, dk, dv, *rest = attend_back(
            me_or_none, slots, quad, at, inputs_t, after(grad_ctx, *others), ctx, inv, q, k, v, raised
        )
        return (dq, dk, dv), rest

    def back_sum(quad, *others):
        part, (keep, send) = back(quad, kernel_order, *others)
        return part, Sum(*halves_of(keep, send, 3), count)

    part_0, sum_0 = back_sum(0, at)
    sum_0.start()
    at = sum_down.land(part_0[0])
    sum_down.start()
    at = sum_out.land(at)
    at = sum_up.land(at)
    sum_up.start()
    part_1, sum_1 = back_sum(1, at)
    sum_1.start()
    at = sum_0.land(part_1[0])
    sum_0 = joined([sum_out, sum_0])
    sum_0.start()
    at = sum_down.land(at, sum_0.send)
    at = sum_up.land(at)
    sum_up.start()
    if own_rows:
        middle = count // 4
        quarter = middle // 2
        send_slots = (order[0],) + tuple(
            order[1][part : part + quarter] for part in range(0, count // 2, quarter)
        )
        part_2, (keep, *sends) = back(2, send_slots, at)
        parts = [swap(send, 1, count) for send in sends]
        at = sum_1.land(part_2[0])
        sum_1.start()
        near = jnp.concatenate(parts[:2])
        far_part = jnp.concatenate([after(part, at) for part in parts[2:]])
        sum_2 = Sum(keep, None, count)
        sum_2.bit, sum_2.slots = 2, middle
        sum_2.send = (keep[middle:].astype(WIDE) + far_part.astype(WIDE)).astype(LOW)
        sum_2.cut(lambda term: term[:middle])
        sum_2.terms.append((near, ()))
        at = sum_2.send
        sum_2.start()
    else:
        part_2, sum_2 = back_sum(2, at)
        sum_2.start()
        at = sum_1.land(part_2[0])
        sum_1.start()
        at = sum_2.land(at)
        sum_2.start()
    at = sum_up.land(at)
    sum_up.start()
    at = sum_0.land(at)
    sum_0.start()
    at = sum_1.land(at)
    at = sum_2.land(at)
    sum_1 = joined([sum_1, sum_2])
    sum_1.start()
    at = after(at, sum_1.send)
    at = sum_0.land(at)
    sum_0.start()
    at = sum_up.land(at)
    sum_up.start()
    sum_down.start(at)
    weights = [group[7] for group in heads]
    at = input_grad = input_grad_call(
        [part_0, part_1, part_2], places, weights, after(grad_attn, at)
    )
    while sum_1.total is None:
        at = sum_1.land(at)
        if sum_1.total is None:
            sum_1.start()
        for item in (sum_up, sum_down) if sum_1.bit < count else (sum_0, sum_up):
            if item.total is None:
                at = item.land(at)
            if item.total is None:
                item.start()
    for item in (sum_0, sum_up, sum_down):
        while item.total is None:
            item.land()
            if item.total is None:
                item.start()
    tall = 3 * rows + EXTRA
    grad_qkv = jnp.concatenate([sum_0.total[-tall:], sum_1.total[:tall], sum_1.total[tall:]], axis=1)
    grad_out = jnp.concatenate(jnp.split(sum_0.total[:-tall], quads), axis=1)
    of_mine = lambda value, size: lax.dynamic_slice_in_dim(value, me * size, size, value.ndim - 1)
    own = of_mine(
        jnp.concatenate([grad_qkv[3 * rows : 3 * rows + 2], grad_out[rows : rows + 6]]), rows
    )
    grad_up_bias = of_mine(grad_out[rows + 6 : rows + 6 + steps].reshape(-1), up_bias.shape[0])
    grad_up = sum_up.total
    return (
        layer_out,
        input_grad,
        grad_qkv[:rows],
        own[QUERY_BIAS],
        grad_qkv[rows : 2 * rows],
        grad_qkv[2 * rows : 3 * rows],
        own[VALUE_BIAS],
        grad_out[:rows],
        own[OUT_BIAS],
        own[ATTN_GAIN],
        own[ATTN_SHIFT],
        jnp.concatenate([grad_up[rows * i : rows * (i + 1)] for i in range(steps)], axis=1),
        grad_up_bias,
        sum_down.total,
        own[DOWN_BIAS],
        own[FFN_GAIN],
        own[FFN_SHIFT],
    )


def solution(mesh):
    tokens = P(("rep", "fsdp"), None)
    matrix = P("fsdp", None)
    vector = P("fsdp")
    params_placed = (
        matrix,
        vector,
        matrix,
        matrix,
        vector,
        matrix,
        vector,
        vector,
        vector,
        matrix,
        vector,
        matrix,
        vector,
        vector,
        vector,
    )
    return jax.shard_map(
        shards,
        mesh=mesh,
        in_specs=(tokens, P(("rep", "fsdp")), *params_placed, tokens),
        out_specs=(tokens, tokens, *params_placed),
        check_vma=False,
    )
```
